32 devices in a mesh: group: 4 (over y, core), space: 8 (over z, x).
Axes of the slice: x: 2, y: 2, z: 4, core: 2. Of those that a mesh axis runs over, the one named last changes fastest.
Arguments:
- initial_state: float32 [32, 3, 32, 1024], P(('group', 'space')), may hold values from -3 to 3
- phases: int32 [32, 32, 1024], P(('group', 'space')), may hold values from 0 to 2
- brick_coords: int32 [32, 3], P(('group', 'space')), may hold values from -1 to 7, as said below
- neighbours: int32 [32, 6], P(('group', 'space')), may hold values from -1 to 31, as said below
- source: float32 [32, 3, 32, 1024], P(('group', 'space'))
- coarse_inverse: float32 [4, 24, 24], P('group', 'space')
Outputs:
- final_state: float32 [32, 3, 32, 1024], P(('group', 'space'))
The draws below stay inside these ranges and needn't reach their ends.
Inputs may be any that keep to these rules, and one draw needn't show every extreme that they name: `brick_coords`: an occupied slot of device (g, s) holds the brick at x place bx, y = s, z = g; each x place occurs at most once on a device; an empty slot is -1 in all three; device (0, 0), every device with s = 7, and device (3, 6) have every slot occupied. Global slot = device index (group index * 8 + space index) + slot. The -x and +x neighbours lie on the same device, -y and +y on the device one step lower or higher along space, -z and +z one step lower or higher along group, always at the same x place; a face has a neighbour exactly where that brick is occupied; the relation is symmetric; empty slots have -1 everywhere.
All inputs are finite; a program needn't handle non-finite values.
Results may differ from the reference program's by a relative error of at most 0.0003.
Values sent between devices are 32-bit elements; how exact they have to be, the bound alone decides.
A program may use at most 64 MiB of HBM per device.

```python
import jax
import jax.numpy as jnp
from jax import lax

E = 32
BRICK_DEV = 1
NEWTON = 2
SMOOTH = 4
GROUPS = 4
COLUMNS = 8
GROUP_SLOTS = 8
SLOTS = 32


def brick_layout(key):
    first_key, second_key, third_key = jax.random.split(key, 3)
    shape = (GROUPS, COLUMNS, BRICK_DEV)
    share = jax.random.randint(first_key, (GROUPS, COLUMNS, 1), 40, 101)
    group_place = lax.broadcasted_iota(jnp.int32, (GROUPS, COLUMNS, 1), 0)
    column_place = lax.broadcasted_iota(jnp.int32, (GROUPS, COLUMNS, 1), 1)
    corner = (group_place + column_place == 0) | (column_place == COLUMNS - 1) | (column_place == COLUMNS - 2) & (group_place == GROUPS - 1)
    rolls = jax.random.randint(second_key, shape, 0, 100)
    filled = (rolls < share) | corner
    scores = jax.random.randint(third_key, shape, 0, 1 << 20) * BRICK_DEV + lax.broadcasted_iota(jnp.int32, shape, 2)
    order = jnp.argsort(scores, axis=2, stable=True).astype(jnp.int32)
    place = jnp.argsort(order, axis=2, stable=True).astype(jnp.int32)
    return (filled, order, place)


def shifted(values, axis, step, fill):
    size = values.shape[axis]
    padding = jnp.full_like(lax.slice_in_dim(values, 0, 1, axis=axis), fill)
    if step > 0:
        return jnp.concatenate([padding, lax.slice_in_dim(values, 0, size - 1, axis=axis)], axis)
    return jnp.concatenate([lax.slice_in_dim(values, 1, size, axis=axis), padding], axis)


def draw_brick_coords(key, part):
    filled, order, place = brick_layout(jax.random.fold_in(key, 11))
    taken = jnp.take_along_axis(filled, order, axis=2)
    shape = (GROUPS, COLUMNS, BRICK_DEV)
    column_index = lax.broadcasted_iota(jnp.int32, shape, 1)
    group_index = lax.broadcasted_iota(jnp.int32, shape, 0)
    placed = jnp.stack([order, column_index, group_index], -1)
    placed = jnp.where(taken[..., None], placed, -1)
    return placed.reshape(SLOTS, 3).astype(jnp.int32)


def draw_neighbours(key, part):
    filled, order, place = brick_layout(jax.random.fold_in(key, 11))
    taken = jnp.take_along_axis(filled, order, axis=2)
    device = lax.broadcasted_iota(jnp.int32, (GROUPS, COLUMNS, 1), 0) * COLUMNS + lax.broadcasted_iota(jnp.int32, (GROUPS, COLUMNS, 1), 1)
    result = []
    for axis, step, offset in ((2, 1, 0), (2, -1, 0), (1, 1, -1), (1, -1, 1), (0, 1, -COLUMNS), (0, -1, COLUMNS)):
        other_filled = jnp.take_along_axis(shifted(filled, axis, step, False), order, axis=2)
        other_slot = jnp.take_along_axis(shifted(place, axis, step, 0), order, axis=2)
        linked = (device + offset) * BRICK_DEV + other_slot
        result.append(jnp.where(taken & other_filled, linked, -1))
    return jnp.stack(result, -1).reshape(SLOTS, 6).astype(jnp.int32)


def draw_source(key, part):
    shape = (SLOTS, 3, E, E * E)
    first_key = jax.random.fold_in(jax.random.fold_in(key, 23), 0)
    position = lax.broadcasted_iota(jnp.float32, (SLOTS, 1, 1, 1), 0) / float(SLOTS - 1)
    scale = 0.3 * jnp.power(10.0, position)
    base = jax.random.normal(first_key, shape, jnp.float32)
    return (base * scale).astype(jnp.float32)


def draw_coarse_inverse(key, part):
    order_size = 3 * GROUP_SLOTS
    noise_key = jax.random.fold_in(key, 37)
    shape = (GROUPS, order_size, order_size)
    noise = jax.random.normal(noise_key, shape, jnp.float32)
    identity = (lax.broadcasted_iota(jnp.int32, shape, 1) == lax.broadcasted_iota(jnp.int32, shape, 2)).astype(jnp.float32)
    return ((identity + 0.5 * noise / jnp.sqrt(float(order_size))) / float(E * E)).astype(jnp.float32)


def place_ends(values, stream_key, smallest, largest):
    spot = [jax.random.randint(jax.random.fold_in(stream_key, axis), (), 0, length) for axis, length in enumerate(values.shape)]
    longest = values.shape.index(max(values.shape))
    beside = spot[:longest] + [(spot[longest] + 1) % values.shape[longest]] + spot[longest + 1:]
    return values.at[tuple(spot)].set(smallest).at[tuple(beside)].set(largest)


def block_scale(rng, dims, cuts, smallest, largest):
    def one(dim, shards_of):
        heights = jax.random.uniform(jax.random.fold_in(jax.random.fold_in(rng, 6), dim), (shards_of,), jnp.float32, smallest / len(cuts), largest / len(cuts))
        return jnp.repeat(jnp.exp(heights), dims[dim] // shards_of).reshape((-1,) + (1,) * (len(dims) - dim - 1))

    factor_of = one(*cuts[0])
    for cut in cuts[1:]:
        factor_of = factor_of * one(*cut)
    return factor_of


def scatter_about(stream_key, dims, deviation, most, cuts=(), held_as=jnp.bfloat16):
    values = deviation * jax.random.normal(stream_key, dims, jnp.float32)
    if cuts:
        values = values * block_scale(stream_key, dims, cuts, -0.22, 0.18)
    return jnp.clip(values, -most, most).astype(held_as)


def setup_inputs(seed: int = 0) -> dict:
    key_of = jax.random.split(jax.random.key(seed), 7)
    initial_state = scatter_about(key_of[0], (SLOTS, 3, E, E * E), 0.5, 3.0, ((0, 32),), jnp.float32)
    phases = place_ends(jax.random.randint(key_of[1], (SLOTS, E, E * E), 0, 3), jax.random.fold_in(key_of[1], 1), 0, 2).astype(jnp.int32)
    brick_coords = draw_brick_coords(jax.random.fold_in(key_of[6], 71), 0)
    neighbours = draw_neighbours(jax.random.fold_in(key_of[6], 71), 0)
    source = draw_source(jax.random.fold_in(key_of[6], 71), 0)
    coarse_inverse = draw_coarse_inverse(jax.random.fold_in(key_of[6], 71), 0)
    return dict(initial_state=initial_state, phases=phases, brick_coords=brick_coords, neighbours=neighbours, source=source, coarse_inverse=coarse_inverse)


SHIFT_TERM = 0.5
BETA_SLOPE = 0.5
ALPHA_SHARE = 0.5
LITHIUM_RATE = 0.5
OMEGA_DAMP = 0.8
CONDUCT_TABLE = ((1.0, 0.2, 0.2), (1.0, 0.1, 0.1), (0.05, 0.5, 1.5))
RATE_TABLE = (0.0, 0.3, 0.02)

def coefficients(phases):
    conductance = jnp.zeros((phases.shape[0], 3) + phases.shape[1:], jnp.float32)
    rates = jnp.zeros((phases.shape[0], 1) + phases.shape[1:], jnp.float32)
    for label in range(3):
        landed = (phases == label).astype(jnp.float32)[:, None]
        column = jnp.array([CONDUCT_TABLE[0][label], CONDUCT_TABLE[1][label], CONDUCT_TABLE[2][label]], jnp.float32)
        conductance = conductance + landed * column[None, :, None, None]
        rates = rates + landed * RATE_TABLE[label]
    return (conductance, rates)

def face_planes(field):
    slots_here, fields, edge_cells, lanes = field.shape
    cube = field.reshape(slots_here, fields, edge_cells, edge_cells, edge_cells)
    return (field[:, :, 0, :], field[:, :, -1, :], field[..., :edge_cells].reshape(slots_here, fields, lanes), field[..., lanes - edge_cells:].reshape(slots_here, fields, lanes), cube[..., 0].reshape(slots_here, fields, lanes), cube[..., -1].reshape(slots_here, fields, lanes))

def neighbour_sum(field, ghosts):
    lower_x, upper_x, lower_y, upper_y, lower_z, upper_z = ghosts
    slots_here, fields, edge_cells, lanes = field.shape
    along_x = jnp.concatenate([field[:, :, 1:], upper_x[:, :, None]], 2) + jnp.concatenate([lower_x[:, :, None], field[:, :, :-1]], 2)
    along_y = jnp.concatenate([field[..., edge_cells:], upper_y.reshape(slots_here, fields, edge_cells, edge_cells)], 3)
    along_y = along_y + jnp.concatenate([lower_y.reshape(slots_here, fields, edge_cells, edge_cells), field[..., :lanes - edge_cells]], 3)
    depth = lax.broadcasted_iota(jnp.int32, (1, 1, 1, lanes), 3) % edge_cells

    def spread(plane):
        return jnp.broadcast_to(plane.reshape(slots_here, fields, edge_cells, edge_cells, 1), (slots_here, fields, edge_cells, edge_cells, edge_cells)).reshape(slots_here, fields, edge_cells, lanes)
    forward = jnp.where(depth == edge_cells - 1, spread(upper_z), jnp.concatenate([field[..., 1:], field[..., :1]], 3))
    backward = jnp.where(depth == 0, spread(lower_z), jnp.concatenate([field[..., -1:], field[..., :-1]], 3))
    return along_x + along_y + forward + backward

def place_ghosts(sources, neighbours, walls):
    result = []
    for direction in range(6):
        linked = neighbours[:, direction]
        usable = linked >= 0
        target = jnp.where(usable, linked, 0) % sources[direction].shape[0]
        picked = jnp.take(sources[direction], target, axis=0)
        result.append(jnp.where(usable[:, None, None], picked, walls[:, :, None]))
    return tuple(result)

def local_terms(state, around, conductance, rates, source, mask):
    lithium = state[:, 0:1]
    electrolyte = state[:, 1:2]
    solid_phase = state[:, 2:3]
    overpotential = solid_phase - electrolyte - BETA_SLOPE * lithium
    forward_rate = jnp.exp(ALPHA_SHARE * overpotential)
    backward_rate = jnp.exp(-ALPHA_SHARE * overpotential)
    current = rates * (forward_rate - backward_rate)
    slope_term = rates * ALPHA_SHARE * (forward_rate + backward_rate)
    reaction = jnp.concatenate([-LITHIUM_RATE * current, -current, current], 1)
    misfit = (SHIFT_TERM * state + conductance * (6.0 * state - around) + reaction - source) * mask
    return (misfit, slope_term)

def linear_image(update, around, conductance, slope_term, mask):
    coupled = slope_term * (update[:, 2:3] - update[:, 1:2] - BETA_SLOPE * update[:, 0:1])
    reaction = jnp.concatenate([-LITHIUM_RATE * coupled, -coupled, coupled], 1)
    return (SHIFT_TERM * update + conductance * (6.0 * update - around) + reaction) * mask

def diagonal_of(conductance, slope_term):
    reaction = jnp.concatenate([LITHIUM_RATE * BETA_SLOPE * slope_term, slope_term, slope_term], 1)
    return SHIFT_TERM + 6.0 * conductance + reaction

def gather_around(field, neighbours, walls):
    faces = face_planes(field)
    sources = (faces[1], faces[0], faces[3], faces[2], faces[5], faces[4])
    return neighbour_sum(field, place_ghosts(sources, neighbours, walls))

def reference(initial_state, phases, brick_coords, neighbours, source, coarse_inverse):
    mask = (brick_coords[:, 0] >= 0).astype(jnp.float32)[:, None, None, None]
    conductance, rates = coefficients(phases)
    placed = brick_coords.astype(jnp.float32)
    wall_phi = placed[:, 0] / BRICK_DEV + placed[:, 1] / COLUMNS + placed[:, 2] / GROUPS - 1.0
    blank = jnp.zeros_like(wall_phi)
    walls = jnp.stack([blank, blank, wall_phi], 1)
    zero_walls = jnp.zeros_like(walls)
    state = initial_state * mask
    total_cells = 3.0 * SLOTS * E * E * E
    for sweep_index in range(NEWTON):
        misfit, slope_term = local_terms(state, gather_around(state, neighbours, walls), conductance, rates, source, mask)
        squares = jnp.sum(misfit * misfit)
        diagonal = diagonal_of(conductance, slope_term)

        def apply_jacobian(update):
            return linear_image(update, gather_around(update, neighbours, zero_walls), conductance, slope_term, mask)
        update = OMEGA_DAMP * -misfit / diagonal
        for pass_index in range(SMOOTH - 1):
            update = update + OMEGA_DAMP * (-misfit - apply_jacobian(update)) / diagonal
        leftover = -misfit - apply_jacobian(update)
        coarse_residual = lax.optimization_barrier(jnp.sum(leftover, axis=(2, 3))).reshape(GROUPS, 3 * GROUP_SLOTS)
        correction = jnp.einsum('gij,gj->gi', coarse_inverse, coarse_residual, precision=lax.Precision.HIGHEST)
        update = update + correction.reshape(SLOTS, 3)[:, :, None, None] * mask
        damping = 1.0 / (1.0 + jnp.sqrt(squares / total_cells + 1e-06))
        state = state + damping * update
    return state
```

```python
import functools

import jax
import jax.numpy as jnp
from jax import lax
from jax.experimental import pallas as pl
from jax.experimental.pallas import tpu as pltpu
from jax.sharding import PartitionSpec as P

NEWTON = 2
SMOOTH = 4
E = 32
RAW = 8
DEEP = 5
WIDE = E + 2 * DEEP
BLOCKS = 3
TILES = WIDE // BLOCKS
PAD = 8
OMEGA = 0.8
FAR = -1000.0
MESH = pl.DeviceIdType.MESH
F32 = jnp.float32


def roll(x, shift):
    shift = shift % 128
    return x if shift == 0 else pltpu.roll(x, shift, 1)


def spot(y):
    block, tile = divmod(y + DEEP, TILES)
    return tile, WIDE * block + DEEP


def kernel(
    n, m,
    coords_in, inverse_in, state_hbm, phase_hbm, source_hbm, out,
    coords, inverse, state_in, phase_in, source_in, fetch,
    state, upd, gain, mix, diag, source, label, last_u,
    near, y_state, y_source, y_misc_out, y_misc, d_out, d_in, z_out, z_in, in_send, in_recv,
    yu_out, yu_in, du_out, du_in, zu_out, zu_in, u_send, u_recv,
    squares, sq_send, sq_recv, coarse, c_send, c_recv,
):
    me_s = lax.axis_index("space")
    me_g = lax.axis_index("group")
    lane = lax.broadcasted_iota(jnp.int32, (E, 128), 1)
    quarter = lane // 32
    block = jnp.where(lane < WIDE, 0, jnp.where(lane < 2 * WIDE, 1, 2))
    column = lane - WIDE * block
    slot = column // DEEP
    own_columns = (column >= DEEP) & (column < DEEP + E)
    low_columns = column < DEEP
    high_columns = (column >= DEEP + E) & (column < WIDE)
    own_rows = (block != 0, block >= 0, block != 2)
    lane8 = lax.broadcasted_iota(jnp.int32, (8, 128), 1)

    def kind(t):
        return 0 if t < DEEP else (1 if t < TILES - DEEP else 2)

    fetches = [
        pltpu.make_async_copy(a, b, fetch.at[i])
        for i, (a, b) in enumerate((
            (coords_in, coords), (state_hbm, state_in), (phase_hbm, phase_in),
            (source_hbm, source_in), (inverse_in, inverse),
        ))
    ]
    for copy in fetches:
        copy.start()

    def there(ds, dg):
        s, g = me_s + ds, me_g + dg
        return (s >= 0) & (s < n) & (g >= 0) & (g < m)

    def at(ds, dg):
        return {"space": jnp.clip(me_s + ds, 0, n - 1), "group": jnp.clip(me_g + dg, 0, m - 1)}

    barrier = pltpu.get_barrier_semaphore()

    def greet(s, g):
        pl.semaphore_signal(barrier, inc=1, device_id={"space": s, "group": g}, device_id_type=MESH)

    for dg in (-1, 0, 1):
        @pl.when(there(0, dg))
        def _():
            for d in range(1 if dg == 0 else 0, n):
                greet(lax.rem(me_s + d, n), jnp.clip(me_g + dg, 0, m - 1))
    for d in range(2, m - 1):
        @pl.when((lax.rem(me_g + d, m) != me_g - 1) & (lax.rem(me_g + d, m) != me_g + 1))
        def _():
            greet(me_s, lax.rem(me_g + d, m))
    for d in sorted({1, m - 1}):
        other = lax.rem(me_g + d, m)

        @pl.when((other != me_g - 1) & (other != me_g + 1))
        def _():
            greet(me_s, other)
    sides = jnp.where(me_g > 0, 1, 0) + jnp.where(me_g < m - 1, 1, 0)
    greeted = n - 1 + n * sides + (m - 1 - sides)

    def message(src, dst, sems, i, ds, dg):
        return pltpu.make_async_remote_copy(
            src_ref=src, dst_ref=dst, send_sem=sems[0].at[i], recv_sem=sems[1].at[i],
            device_id=at(ds, dg), device_id_type=MESH)

    ins = (in_send, in_recv)
    us = (u_send, u_recv)
    steps = (1, -1)
    first_messages, update_messages = {}, {}
    for side in range(2):
        cut = pl.ds(128 * (RAW - 1), 128) if side == 0 else pl.ds(0, 128)
        step = steps[side]
        first_messages["state", side] = (state_hbm.at[:, :, cut], y_state.at[side], ins, side, step, 0)
        first_messages["source", side] = (source_hbm.at[:, :, cut], y_source.at[side], ins, 2 + side, step, 0)
        first_messages["misc", side] = (y_misc_out.at[side], y_misc.at[side], ins, 4 + side, step, 0)
        first_messages["z", side] = (z_out.at[side], z_in.at[side], ins, 6 + side, 0, step)
        update_messages["y", side] = (yu_out.at[side], yu_in.at[side], us, side, step, 0)
        update_messages["z", side] = (zu_out.at[side], zu_in.at[side], us, 2 + side, 0, step)
        for over in range(2):
            c = 2 * side + over
            first_messages["d", c] = (d_out.at[c], d_in.at[c], ins, 8 + c, step, steps[over])
            update_messages["d", c] = (du_out.at[c], du_in.at[c], us, 4 + c, step, steps[over])

    def start(spec):
        @pl.when(there(spec[4], spec[5]))
        def _():
            message(*spec).start()

    def arrive(spec):
        @pl.when(there(-spec[4], -spec[5]))
        def _():
            message(*spec).wait_recv()

    def left(spec):
        @pl.when(there(spec[4], spec[5]))
        def _():
            message(*spec).wait_send()

    pl.semaphore_wait(barrier, greeted)
    for side in range(2):
        start(first_messages["state", side])
        start(first_messages["source", side])

    fetches[0].wait()
    occupied = coords[0, 0] >= 0
    mask = jnp.where(occupied, 1.0, 0.0).astype(F32)
    place_x = coords[0, 0].astype(F32)
    offset = 4.0 * place_x
    compare = jnp.where(occupied, offset, 1000.0)

    fetches[4].wait()
    near[4] = jnp.zeros((8, 128), F32)
    for f in range(3):
        near[4, f:f + 1, 0:3 * n] = inverse[f]
    mine = near[4]

    fetches[1].wait()
    fetches[2].wait()

    def raw_state(f, t):
        return state_in[f, :, t * 128:(t + 1) * 128]

    def raw_source(f, t):
        return source_in[f, :, t * 128:(t + 1) * 128]

    def raw_label(t):
        return phase_in[:, t * 128:(t + 1) * 128].astype(F32) + offset

    for side in range(2):
        edge, inner, q = ((RAW - 1, RAW - 2, 3), (0, 1, 0))[side]
        y_misc_out[side, 0:E] = raw_label(edge)
        fifth = roll(raw_label(inner), 32 * (3 - q))
        for f in range(3):
            fifth = jnp.where(quarter == f, roll(raw_state(f, inner), 32 * (f - q)), fifth)
        y_misc_out[side, E:2 * E] = fifth
        y_misc_out[side, 2 * E:] = mine
        start(first_messages["misc", side])

    small = (lane % 32) // 4

    def corner_pack(tiles, over):
        out_tile = None
        for a, tile in enumerate(tiles):
            part = roll(tile, 4 * a - (28 if over == 0 else 0))
            out_tile = part if out_tile is None else jnp.where(small == a, part, out_tile)
        return out_tile

    fetches[3].wait()
    for side in range(2):
        edge = (RAW - 1, 0)[side]
        tiles = [raw_state(f, edge) for f in range(3)] + [raw_source(f, edge) for f in range(3)] + [raw_label(edge)]
        for over in range(2):
            c = 2 * side + over
            d_out[c, 0:E] = corner_pack(tiles, over)
            d_out[c, E:] = mine
            start(first_messages["d", c])

    class View:
        def __init__(self, read, write):
            self.read, self.write = read, write

    def padded(ref, f):
        def write(t, v):
            ref[f, t, PAD:PAD + E] = v
        return View(lambda t: ref[f, t, PAD:PAD + E], write)

    def plain(ref, *index):
        def write(t, v):
            ref[(*index, t)] = v
        return View(lambda t: ref[(*index, t)], write)

    views = [padded(state, f) for f in range(3)] + [plain(source, f) for f in range(3)] + [plain(label)]
    raws = [functools.partial(raw_state, f) for f in range(3)] + [functools.partial(raw_source, f) for f in range(3)] + [raw_label]

    zero_rows = jnp.zeros((PAD, 128), F32)
    for t in range(TILES):
        for f in range(3):
            state[f, t, 0:PAD] = zero_rows
            state[f, t, PAD + E:] = zero_rows
            for b in range(SMOOTH - 1):
                upd[b, f, t, 0:PAD] = zero_rows
                upd[b, f, t, PAD + E:] = zero_rows
        for a, (view, raw) in enumerate(zip(views, raws)):
            tile = jnp.full((E, 128), FAR if a == 6 else 0.0, F32)
            for b in range(BLOCKS):
                y = TILES * b + t - DEEP
                if 0 <= y < E:
                    moved = roll(raw(y // 4), WIDE * b + DEEP - 32 * (y % 4))
                    tile = jnp.where(own_columns & (block == b), moved, tile)
            view.write(t, tile)

    half_slots = WIDE // DEEP

    def z_pack(parts, side):
        shift = -(E if side == 0 else DEEP)
        packed = []
        for view in parts:
            for low in (0, half_slots):
                acc = None
                for j in range(min(half_slots, TILES - low)):
                    part = roll(view.read(low + j), DEEP * j + shift)
                    acc = part if acc is None else jnp.where(slot == j, part, acc)
                packed.append(acc)
        return packed

    def z_unpack(parts, got):
        for a, view in enumerate(parts):
            for t in range(TILES):
                half, j = divmod(t, half_slots)
                rows = own_rows[kind(t)]
                tile = jnp.where(low_columns & rows, roll(got(0, 2 * a + half), -DEEP * j), view.read(t))
                view.write(t, jnp.where(high_columns & rows, roll(got(1, 2 * a + half), DEEP + E - DEEP * j), tile))

    def halo_tile(side, q):
        if side == 0:
            return (0 if q < 0 else 1 + q), 0
        return (TILES - 1 if q < 0 else TILES - DEEP + q), 2 * WIDE

    def corner_unpack(parts, got):
        for side in range(2):
            for q in range(4):
                t, first = halo_tile(side, q)
                for a, view in enumerate(parts):
                    tile = view.read(t)
                    for over in range(2):
                        begin = first + (1 if over == 0 else DEEP + E)
                        moved = roll(got(2 * side + over), begin - (32 * q + 4 * a))
                        tile = jnp.where((lane >= begin) & (lane < begin + 4), moved, tile)
                    view.write(t, tile)

    def y_unpack(parts, got, fifth, blocks):
        for side in range(2):
            for q in range(-1, 4):
                t, first = halo_tile(side, q)
                here = (lane >= first + DEEP) & (lane < first + DEEP + E)
                for a, view in enumerate(parts):
                    if q < 0 and blocks[a] is None:
                        continue
                    if q < 0:
                        moved = roll(fifth(side), first + DEEP - 32 * blocks[a])
                    else:
                        moved = roll(got(side, a), first + DEEP - 32 * q)
                    view.write(t, jnp.where(here, moved, view.read(t)))

    for side in range(2):
        for i, tile in enumerate(z_pack(views, side)):
            z_out[side, E * i:E * (i + 1)] = tile
        z_out[side, 14 * E:] = mine
        start(first_messages["z", side])

    far = jnp.full((E, 128), FAR, F32)
    none = jnp.zeros((8, 128), F32)
    blank = jnp.zeros((E, 128), F32)
    for side in range(2):
        @pl.when(jnp.logical_not(there(-steps[side], 0)))
        def _():
            for f in range(3):
                y_state[side, f] = blank
                y_source[side, f] = blank
            for i in range(2):
                y_misc[side, E * i:E * (i + 1)] = far
            y_misc[side, 2 * E:] = none
            for i in range(4):
                yu_in[side, E * i:E * (i + 1)] = blank

        @pl.when(jnp.logical_not(there(0, -steps[side])))
        def _():
            for i in range(14):
                z_in[side, E * i:E * (i + 1)] = far
            z_in[side, 14 * E:] = none
            for i in range(6):
                zu_in[side, E * i:E * (i + 1)] = blank
            for k in range(NEWTON):
                for d in range(n):
                    coarse[k, 2 * side, d] = none

        for over in range(2):
            @pl.when(jnp.logical_not(there(-steps[side], -steps[over])))
            def _():
                d_in[2 * side + over, 0:E] = far
                d_in[2 * side + over, E:] = none
                du_in[2 * side + over] = blank

    for side in range(2):
        arrive(first_messages["z", side])
    z_unpack(views, lambda side, i: z_in[side, E * i:E * (i + 1)])
    for c in range(4):
        arrive(first_messages["d", c])
    corner_unpack(views, lambda c: d_in[c, 0:E])
    for side in range(2):
        for name in ("state", "source", "misc"):
            arrive(first_messages[name, side])

    def y_got(side, a):
        if a < 3:
            return y_state[side, a]
        return y_source[side, a - 3] if a < 6 else y_misc[side, 0:E]

    y_unpack(views, y_got, lambda side: y_misc[side, E:2 * E], (0, 1, 2, None, None, None, 3))

    for side in range(2):
        near[1 + 6 * side] = y_misc[side, 2 * E:]
        near[3 + 2 * side] = z_in[side, 14 * E:]
        for over in range(2):
            near[6 * side + 2 * over] = d_in[2 * side + over, E:]

    def by_region(values, t_kind):
        def row(i):
            return jnp.where(low_columns, values[i][0], jnp.where(own_columns, values[i][1], values[i][2]))
        middle = row(1)
        if t_kind == 0:
            return jnp.where(block == 0, row(0), middle)
        return jnp.where(block == 2, row(2), middle) if t_kind == 2 else middle

    walls = [[place_x + (me_s + i).astype(F32) / n + (me_g + j).astype(F32) / m - 1.0 for j in (-1, 0, 1)] for i in (-1, 0, 1)]
    wall_maps = [by_region(walls, i) for i in range(3)]
    row_index = lax.broadcasted_iota(jnp.int32, (E, 128), 0)
    x_open = jnp.where((row_index == 0) | (row_index == E - 1), 1.0, 0.0).astype(F32)

    def is_valid(rel):
        return (rel >= 0.0) & (rel <= 2.0)

    bricks = [jnp.where(is_valid(label[t, 0:8] - compare), 1.0, 0.0).astype(F32) for t in range(TILES)]
    for t in range(TILES):
        rel = label[t] - compare
        label[t] = rel
        good = is_valid(rel)
        for f in range(3):
            state[f, t, PAD:PAD + E] = jnp.where(good, state[f, t, PAD:PAD + E], 0.0)
        below = bricks[t - 1] if t > 0 else roll(bricks[TILES - 1], WIDE)
        above = bricks[t + 1] if t < TILES - 1 else roll(bricks[0], -WIDE)
        shut = 4.0 - (below + above + roll(bricks[t], 1) + roll(bricks[t], -1))
        missing = jnp.concatenate([shut] * 4, axis=0) + x_open
        solid = jnp.where(rel == 0.0, 0.05, jnp.where(rel == 1.0, 0.5, 1.5))
        source[2, t] = source[2, t] + solid * (wall_maps[kind(t)] * missing)

    def around(ref, f, t):
        c = ref[f, t, PAD:PAD + E]
        total = ref[f, t, PAD - 1:PAD - 1 + E] + ref[f, t, PAD + 1:PAD + 1 + E]
        total = total + (roll(c, 1) + roll(c, -1))
        total = total + (ref[f, t - 1, PAD:PAD + E] if t > 0 else roll(ref[f, TILES - 1, PAD:PAD + E], WIDE))
        total = total + (ref[f, t + 1, PAD:PAD + E] if t < TILES - 1 else roll(ref[f, 0, PAD:PAD + E], -WIDE))
        return c, total

    def fold(x):
        return x[0:8] + x[8:16] + x[16:24] + x[24:32]

    def total_of(x):
        return jnp.sum(jnp.sum(x, axis=0, keepdims=True), axis=1, keepdims=True)

    def square_copy(k, d):
        return pltpu.make_async_remote_copy(
            src_ref=squares.at[k, 0], dst_ref=squares.at[k, d],
            send_sem=sq_send.at[k, d], recv_sem=sq_recv.at[k, d],
            device_id={"group": lax.rem(me_g + d, m)}, device_id_type=MESH)

    def coarse_copy(k, dg, d):
        return pltpu.make_async_remote_copy(
            src_ref=coarse.at[k, 1, me_s], dst_ref=coarse.at[k, 1 - dg, me_s],
            send_sem=c_send.at[k, 1 + dg, d], recv_sem=c_recv.at[k, 1 - dg, me_s],
            device_id={"space": lax.rem(me_s + d, n), "group": jnp.clip(me_g + dg, 0, m - 1)}, device_id_type=MESH)

    def coarse_arrival(k, dg, d):
        who = lax.rem(me_s + d, n)
        return pltpu.make_async_remote_copy(
            src_ref=coarse.at[k, 1 + dg, who], dst_ref=coarse.at[k, 1 + dg, who],
            send_sem=c_send.at[k, 1 + dg, d], recv_sem=c_recv.at[k, 1 + dg, who],
            device_id={"space": lax.rem(me_s + (1 if n > 1 else 0), n)}, device_id_type=MESH)

    def sweep(k, carry):
        square = jnp.zeros((E, 128), F32)
        for t in range(TILES):
            rel = label[t]
            pore = rel == 0.0
            active = rel == 1.0
            good = is_valid(rel)
            mine_here = good & own_columns & own_rows[kind(t)]
            conduct = (jnp.where(pore, 1.0, 0.2), jnp.where(pore, 1.0, 0.1),
                       jnp.where(pore, 0.05, jnp.where(active, 0.5, 1.5)))
            rates = jnp.where(pore, 0.0, jnp.where(active, 0.3, 0.02))
            pairs = [around(state, f, t) for f in range(3)]
            c, e, s = (p[0] for p in pairs)
            eta = s - e - 0.5 * c
            forward = jnp.exp(0.5 * eta)
            backward = jnp.exp(-0.5 * eta)
            current = rates * (forward - backward)
            slope = 0.5 * rates * (forward + backward)
            react = (-0.5 * current, -current, current)
            weight = jnp.where(good, OMEGA, 0.0)
            for f in range(3):
                v, total = pairs[f]
                misfit = 0.5 * v + conduct[f] * (6.0 * v - total) + react[f] - source[f, t]
                square = square + jnp.where(mine_here, misfit * misfit, 0.0)
                dg = 0.5 + 6.0 * conduct[f] + (0.25 * slope if f == 0 else slope)
                w = weight / dg
                upd[0, f, t, PAD:PAD + E] = -w * misfit
                gain[f, t] = w * conduct[f]
                mix[f, t] = w * slope * (0.5 if f == 0 else 1.0)
                diag[f, t] = jnp.where(mine_here, dg * (1.0 / OMEGA), 0.0)
        squares[k, 0] = fold(square)
        for d in range(1, m):
            square_copy(k, d).start()

        def terms(u, t):
            pairs = [around(u, f, t) for f in range(3)]
            c, e, s = (p[0] for p in pairs)
            half = 0.5 * c
            cross = (s - e, s - half, e + half)
            return [(pairs[f][0], upd[0, f, t, PAD:PAD + E] + gain[f, t] * pairs[f][1] + mix[f, t] * cross[f]) for f in range(3)]

        def smooth(p, carry):
            u = upd.at[jnp.where(p == 0, 0, 1 + lax.rem(p + 1, 2))]
            later = upd.at[1 + lax.rem(p, 2)]
            for t in range(TILES):
                for f, (v, term) in enumerate(terms(u, t)):
                    later[f, t, PAD:PAD + E] = (1.0 - OMEGA) * v + term
            return carry

        lax.fori_loop(0, SMOOTH - 1, smooth, 0)
        final = 1 + (SMOOTH - 2) % 2
        u = upd.at[final]
        sums = [jnp.zeros((E, 128), F32) for _ in range(3)]
        for t in range(TILES):
            for f, (v, term) in enumerate(terms(u, t)):
                sums[f] = sums[f] + diag[f, t] * (term - OMEGA * v)
        totals = [total_of(x) for x in sums]
        for d in range(1, m):
            square_copy(k, d).wait_recv()
        part = squares[k, 0]
        for d in range(1, m):
            part = part + squares[k, d]
        packed = jnp.where(lane8 == 127, total_of(part), 0.0)
        for f in range(3):
            packed = jnp.where(lane8 == 3 * me_s + f, totals[f], packed)
        coarse[k, 1, me_s] = packed
        for d in range(1, n):
            coarse_copy(k, 0, d).start()

        u_views = [padded(u, f) for f in range(3)]

        def damping_of(group):
            whole = jnp.sum(jnp.where(lane8 == 127, group, 0.0), axis=1, keepdims=True)[0:1]
            cells = 3.0 * n * m * E * E * E
            return 1.0 / (1.0 + jnp.sqrt(whole / cells + 1e-6))

        def group_sum(i):
            acc = coarse[k, i, 0]
            for d in range(1, n):
                acc = acc + coarse[k, i, d]
            return acc

        @pl.when(k < NEWTON - 1)
        def _():
            for dg in (-1, 1):
                @pl.when(there(0, dg))
                def _():
                    for d in range(n):
                        coarse_copy(k, dg, d).start()
            for side in range(2):
                tiles, fifth = [], None
                for f in range(3):
                    tile = None
                    for q in range(4):
                        t, first = spot(E - 4 + q if side == 0 else q)
                        part = roll(u_views[f].read(t), 32 * q - first)
                        tile = part if tile is None else jnp.where(quarter == q, part, tile)
                    tiles.append(tile)
                    t, first = spot(E - 5 if side == 0 else 4)
                    part = roll(u_views[f].read(t), 32 * f - first)
                    fifth = part if fifth is None else jnp.where(quarter == f, part, fifth)
                for i, tile in enumerate(tiles + [fifth]):
                    yu_out[side, E * i:E * (i + 1)] = tile
                start(update_messages["y", side])
                for over in range(2):
                    du_out[2 * side + over] = corner_pack(tiles, over)
                    start(update_messages["d", 2 * side + over])
            for side in range(2):
                for i, tile in enumerate(z_pack(u_views, side)):
                    zu_out[side, E * i:E * (i + 1)] = tile
                start(update_messages["z", side])
            for side in range(2):
                arrive(update_messages["z", side])
            z_unpack(u_views, lambda side, i: zu_in[side, E * i:E * (i + 1)])
            for c in range(4):
                arrive(update_messages["d", c])
            corner_unpack(u_views, lambda c: du_in[c])
            for side in range(2):
                arrive(update_messages["y", side])
            y_unpack(u_views, lambda side, a: yu_in[side, E * a:E * (a + 1)], lambda side: yu_in[side, 3 * E:], (0, 1, 2))

            for d in range(1, n):
                coarse_arrival(k, 0, d).wait_recv()
            for dg in (-1, 1):
                @pl.when(there(0, dg))
                def _():
                    for d in range(n):
                        coarse_arrival(k, dg, d).wait_recv()
            groups = [group_sum(i) for i in range(3)]
            damping = damping_of(groups[1])
            lifts = [[jnp.sum(near[3 * i + j] * groups[j], axis=1, keepdims=True) for j in range(3)] for i in range(3)]
            maps = [[by_region([[x[f:f + 1] for x in row] for row in lifts], i) for i in range(3)] for f in range(3)]
            for t in range(TILES):
                good = is_valid(label[t])
                for f in range(3):
                    value = state[f, t, PAD:PAD + E] + damping * (u[f, t, PAD:PAD + E] + maps[f][kind(t)])
                    state[f, t, PAD:PAD + E] = jnp.where(good, value, 0.0)

        @pl.when(k == NEWTON - 1)
        def _():
            for f in range(3):
                for i in range(RAW):
                    for view, where in ((padded(state, f), out), (u_views[f], last_u)):
                        tile = None
                        for q in range(4):
                            t, first = spot(4 * i + q)
                            part = roll(view.read(t), 32 * q - first)
                            tile = part if tile is None else jnp.where(quarter == q, part, tile)
                        where[f, :, i * 128:(i + 1) * 128] = tile
            for d in range(1, n):
                coarse_arrival(k, 0, d).wait_recv()
            group = group_sum(1)
            damping = damping_of(group)
            lift = mask * jnp.sum(near[4] * group, axis=1, keepdims=True)
            for f in range(3):
                out[f] = out[f] + damping * (last_u[f] + lift[f:f + 1])

        return carry

    lax.fori_loop(0, NEWTON, sweep, 0)

    for spec in list(first_messages.values()) + list(update_messages.values()):
        left(spec)
    for k in range(NEWTON):
        for d in range(1, m):
            square_copy(k, d).wait_send()
        for d in range(1, n):
            coarse_copy(k, 0, d).wait_send()
    for k in range(NEWTON - 1):
        for dg in (-1, 1):
            @pl.when(there(0, dg))
            def _():
                for d in range(n):
                    coarse_copy(k, dg, d).wait_send()


def shards(n, m, initial_state, phases, brick_coords, neighbours, source, coarse_inverse):
    anywhere = pl.BlockSpec(memory_space=pl.ANY)
    vmem = pl.BlockSpec(memory_space=pltpu.VMEM)
    padded = (3, TILES, E + 2 * PAD, 128)
    inner = (3, TILES, E, 128)
    dma = pltpu.SemaphoreType.DMA
    V = pltpu.VMEM
    result = pl.pallas_call(
        functools.partial(kernel, n, m),
        out_shape=jax.ShapeDtypeStruct((3, E, E * E), F32),
        in_specs=[anywhere] * 5,
        out_specs=vmem,
        scratch_shapes=[
            pltpu.SMEM((1, 3), jnp.int32),
            V((3, 1, 3 * n), F32),
            V((3, E, E * E), F32),
            V((E, E * E), jnp.int32),
            V((3, E, E * E), F32),
            dma((5,)),
            V(padded, F32),
            V((SMOOTH - 1,) + padded, F32),
            V(inner, F32),
            V(inner, F32),
            V(inner, F32),
            V(inner, F32),
            V(inner[1:], F32),
            V((3, E, E * E), F32),
            V((9, 8, 128), F32),
            V((2, 3, E, 128), F32), V((2, 3, E, 128), F32),
            V((2, 2 * E + 8, 128), F32), V((2, 2 * E + 8, 128), F32),
            V((4, E + 8, 128), F32), V((4, E + 8, 128), F32),
            V((2, 14 * E + 8, 128), F32), V((2, 14 * E + 8, 128), F32),
            dma((12,)), dma((12,)),
            V((2, 4 * E, 128), F32), V((2, 4 * E, 128), F32),
            V((4, E, 128), F32), V((4, E, 128), F32),
            V((2, 6 * E, 128), F32), V((2, 6 * E, 128), F32),
            dma((8,)), dma((8,)),
            V((NEWTON, m, 8, 128), F32),
            dma((NEWTON, m)), dma((NEWTON, m)),
            V((NEWTON, 3, n, 8, 128), F32),
            dma((NEWTON, 3, n)), dma((NEWTON, 3, n)),
        ],
        compiler_params=pltpu.CompilerParams(
            collective_id=0, has_side_effects=True, vmem_limit_bytes=56 * 1024 * 1024
        ),
    )(brick_coords, jnp.swapaxes(coarse_inverse, 0, 1), initial_state[0], phases[0], source[0])
    return result[None]


def solution(mesh):
    both = ("group", "space")
    return jax.shard_map(
        functools.partial(shards, mesh.shape["space"], mesh.shape["group"]),
        mesh=mesh,
        in_specs=(
            P(both, None, None, None),
            P(both, None, None),
            P(both, None),
            P(both, None),
            P(both, None, None, None),
            P("group", "space", None),
        ),
        out_specs=P(both, None, None, None),
        check_vma=False,
    )
```

```python
import functools

import jax
import jax.numpy as jnp
from jax import lax
from jax.experimental import pallas as pl
from jax.experimental.pallas import tpu as pltpu
from jax.sharding import PartitionSpec as P

NEWTON = 2
SMOOTH = 4
E = 32
RAW = 8
DEEP = 5
WIDE = E + 2 * DEEP
BLOCKS = 3
TILES = WIDE // BLOCKS
PAD = 8
OMEGA = 0.8
FAR = -1000.0
MESH = pl.DeviceIdType.MESH
F32 = jnp.float32


def roll(x, shift):
    shift = shift % 128
    return x if shift == 0 else pltpu.roll(x, shift, 1)


def reaches(n):
    steps, known = [], 1
    while known < n - 1:
        steps.append(known)
        known *= 2
    return steps


def spot(y):
    block, tile = divmod(y + DEEP, TILES)
    return tile, WIDE * block + DEEP


def kernel(
    n, m,
    coords_in, inverse_in, state_hbm, phase_hbm, source_hbm, out,
    coords, inverse, state_in, phase_in, source_in, fetch,
    state, upd, gain, mix, diag, source, label, last_u,
    near, y_state, y_source, y_misc_out, y_misc, d_out, d_in, z_out, z_in, in_send, in_recv,
    yu_out, yu_in, du_out, du_in, zu_out, zu_in, u_send, u_recv,
    squares, sq_send, sq_recv, coarse, c_send, c_recv, ready,
):
    me_s = lax.axis_index("space")
    me_g = lax.axis_index("group")
    lane = lax.broadcasted_iota(jnp.int32, (E, 128), 1)
    quarter = lane // 32
    block = jnp.where(lane < WIDE, 0, jnp.where(lane < 2 * WIDE, 1, 2))
    column = lane - WIDE * block
    slot = column // DEEP
    own_columns = (column >= DEEP) & (column < DEEP + E)
    low_columns = column < DEEP
    high_columns = (column >= DEEP + E) & (column < WIDE)
    own_rows = (block != 0, block >= 0, block != 2)
    lane8 = lax.broadcasted_iota(jnp.int32, (8, 128), 1)

    def kind(t):
        return 0 if t < DEEP else (1 if t < TILES - DEEP else 2)

    fetches = [
        pltpu.make_async_copy(a, b, fetch.at[i])
        for i, (a, b) in enumerate((
            (coords_in, coords), (state_hbm, state_in), (phase_hbm, phase_in),
            (source_hbm, source_in), (inverse_in, inverse),
        ))
    ]
    for copy in fetches:
        copy.start()

    def there(ds, dg):
        s, g = me_s + ds, me_g + dg
        return (s >= 0) & (s < n) & (g >= 0) & (g < m)

    def at(ds, dg):
        return {"space": jnp.clip(me_s + ds, 0, n - 1), "group": jnp.clip(me_g + dg, 0, m - 1)}

    barrier = pltpu.get_barrier_semaphore()

    def greet(s, g):
        pl.semaphore_signal(barrier, inc=1, device_id={"space": s, "group": g}, device_id_type=MESH)

    for ds in (-1, 0, 1):
        for dg in (-1, 0, 1):
            if ds or dg:
                @pl.when(there(ds, dg))
                def _():
                    greet(jnp.clip(me_s + ds, 0, n - 1), jnp.clip(me_g + dg, 0, m - 1))
    for d in range(1, m):
        other = lax.rem(me_g + d, m)

        @pl.when((other != me_g - 1) & (other != me_g + 1))
        def _():
            greet(me_s, other)
    beside_g = jnp.where(me_g > 0, 1, 0) + jnp.where(me_g < m - 1, 1, 0)
    beside_s = jnp.where(me_s > 0, 1, 0) + jnp.where(me_s < n - 1, 1, 0)
    greeted = beside_s * (1 + beside_g) + m - 1

    def tell(i):
        if i < len(reaches(n)):
            for side, step in enumerate((reaches(n)[i], -reaches(n)[i])):
                @pl.when(there(step, 0))
                def _():
                    pl.semaphore_signal(ready.at[i, side], inc=1, device_id=at(step, 0), device_id_type=MESH)

    def told(i):
        for side, step in enumerate((reaches(n)[i], -reaches(n)[i])):
            @pl.when(there(-step, 0))
            def _():
                pl.semaphore_wait(ready.at[i, side], 1)
        tell(i + 1)

    def message(src, dst, sems, i, ds, dg):
        return pltpu.make_async_remote_copy(
            src_ref=src, dst_ref=dst, send_sem=sems[0].at[i], recv_sem=sems[1].at[i],
            device_id=at(ds, dg), device_id_type=MESH)

    ins = (in_send, in_recv)
    us = (u_send, u_recv)
    steps = (1, -1)
    first_messages, update_messages = {}, {}
    for side in range(2):
        cut = pl.ds(128 * (RAW - 1), 128) if side == 0 else pl.ds(0, 128)
        step = steps[side]
        first_messages["state", side] = (state_hbm.at[:, :, cut], y_state.at[side], ins, side, step, 0)
        first_messages["source", side] = (source_hbm.at[:, :, cut], y_source.at[side], ins, 2 + side, step, 0)
        first_messages["misc", side] = (y_misc_out.at[side], y_misc.at[side], ins, 4 + side, step, 0)
        first_messages["z", side] = (z_out.at[side], z_in.at[side], ins, 6 + side, 0, step)
        update_messages["y", side] = (yu_out.at[side], yu_in.at[side], us, side, step, 0)
        update_messages["z", side] = (zu_out.at[side], zu_in.at[side], us, 2 + side, 0, step)
        for over in range(2):
            c = 2 * side + over
            first_messages["d", c] = (d_out.at[c], d_in.at[c], ins, 8 + c, step, steps[over])
            update_messages["d", c] = (du_out.at[c], du_in.at[c], us, 4 + c, step, steps[over])

    def start(spec):
        @pl.when(there(spec[4], spec[5]))
        def _():
            message(*spec).start()

    def arrive(spec):
        @pl.when(there(-spec[4], -spec[5]))
        def _():
            message(*spec).wait_recv()

    def left(spec):
        @pl.when(there(spec[4], spec[5]))
        def _():
            message(*spec).wait_send()

    fetches[0].wait()
    occupied = coords[0, 0] >= 0
    mask = jnp.where(occupied, 1.0, 0.0).astype(F32)
    place_x = coords[0, 0].astype(F32)
    offset = 4.0 * place_x
    compare = jnp.where(occupied, offset, 1000.0)

    fetches[4].wait()
    near[4] = jnp.zeros((8, 128), F32)
    for f in range(3):
        near[4, f:f + 1, 0:3 * n] = inverse[f]
    mine = near[4]

    fetches[1].wait()
    fetches[2].wait()

    def raw_state(f, t):
        return state_in[f, :, t * 128:(t + 1) * 128]

    def raw_source(f, t):
        return source_in[f, :, t * 128:(t + 1) * 128]

    def raw_label(t):
        return phase_in[:, t * 128:(t + 1) * 128].astype(F32) + offset

    for side in range(2):
        edge, inner, q = ((RAW - 1, RAW - 2, 3), (0, 1, 0))[side]
        y_misc_out[side, 0:E] = raw_label(edge)
        fifth = roll(raw_label(inner), 32 * (3 - q))
        for f in range(3):
            fifth = jnp.where(quarter == f, roll(raw_state(f, inner), 32 * (f - q)), fifth)
        y_misc_out[side, E:2 * E] = fifth
        y_misc_out[side, 2 * E:] = mine

    small = (lane % 32) // 4

    def corner_pack(tiles, over):
        out_tile = None
        for a, tile in enumerate(tiles):
            part = roll(tile, 4 * a - (28 if over == 0 else 0))
            out_tile = part if out_tile is None else jnp.where(small == a, part, out_tile)
        return out_tile

    fetches[3].wait()
    for side in range(2):
        edge = (RAW - 1, 0)[side]
        tiles = [raw_state(f, edge) for f in range(3)] + [raw_source(f, edge) for f in range(3)] + [raw_label(edge)]
        for over in range(2):
            c = 2 * side + over
            d_out[c, 0:E] = corner_pack(tiles, over)
            d_out[c, E:] = mine

    class View:
        def __init__(self, read, write):
            self.read, self.write = read, write

    def padded(ref, f):
        def write(t, v):
            ref[f, t, PAD:PAD + E] = v
        return View(lambda t: ref[f, t, PAD:PAD + E], write)

    def plain(ref, *index):
        def write(t, v):
            ref[(*index, t)] = v
        return View(lambda t: ref[(*index, t)], write)

    views = [padded(state, f) for f in range(3)] + [plain(source, f) for f in range(3)] + [plain(label)]
    raws = [functools.partial(raw_state, f) for f in range(3)] + [functools.partial(raw_source, f) for f in range(3)] + [raw_label]

    zero_rows = jnp.zeros((PAD, 128), F32)
    for t in range(TILES):
        for f in range(3):
            state[f, t, 0:PAD] = zero_rows
            state[f, t, PAD + E:] = zero_rows
            for b in range(SMOOTH - 1):
                upd[b, f, t, 0:PAD] = zero_rows
                upd[b, f, t, PAD + E:] = zero_rows
        for a, (view, raw) in enumerate(zip(views, raws)):
            tile = jnp.full((E, 128), FAR if a == 6 else 0.0, F32)
            for b in range(BLOCKS):
                y = TILES * b + t - DEEP
                if 0 <= y < E:
                    moved = roll(raw(y // 4), WIDE * b + DEEP - 32 * (y % 4))
                    tile = jnp.where(own_columns & (block == b), moved, tile)
            view.write(t, tile)

    half_slots = WIDE // DEEP

    def z_pack(parts, side):
        shift = -(E if side == 0 else DEEP)
        packed = []
        for view in parts:
            for low in (0, half_slots):
                acc = None
                for j in range(min(half_slots, TILES - low)):
                    part = roll(view.read(low + j), DEEP * j + shift)
                    acc = part if acc is None else jnp.where(slot == j, part, acc)
                packed.append(acc)
        return packed

    def z_unpack(parts, got):
        for a, view in enumerate(parts):
            for t in range(TILES):
                half, j = divmod(t, half_slots)
                rows = own_rows[kind(t)]
                tile = jnp.where(low_columns & rows, roll(got(0, 2 * a + half), -DEEP * j), view.read(t))
                view.write(t, jnp.where(high_columns & rows, roll(got(1, 2 * a + half), DEEP + E - DEEP * j), tile))

    def halo_tile(side, q):
        if side == 0:
            return (0 if q < 0 else 1 + q), 0
        return (TILES - 1 if q < 0 else TILES - DEEP + q), 2 * WIDE

    def corner_unpack(parts, got):
        for side in range(2):
            for q in range(4):
                t, first = halo_tile(side, q)
                for a, view in enumerate(parts):
                    tile = view.read(t)
                    for over in range(2):
                        begin = first + (1 if over == 0 else DEEP + E)
                        moved = roll(got(2 * side + over), begin - (32 * q + 4 * a))
                        tile = jnp.where((lane >= begin) & (lane < begin + 4), moved, tile)
                    view.write(t, tile)

    def y_unpack(parts, got, fifth, blocks):
        for side in range(2):
            for q in range(-1, 4):
                t, first = halo_tile(side, q)
                here = (lane >= first + DEEP) & (lane < first + DEEP + E)
                for a, view in enumerate(parts):
                    if q < 0 and blocks[a] is None:
                        continue
                    if q < 0:
                        moved = roll(fifth(side), first + DEEP - 32 * blocks[a])
                    else:
                        moved = roll(got(side, a), first + DEEP - 32 * q)
                    view.write(t, jnp.where(here, moved, view.read(t)))

    for side in range(2):
        for i, tile in enumerate(z_pack(views, side)):
            z_out[side, E * i:E * (i + 1)] = tile
        z_out[side, 14 * E:] = mine

    far = jnp.full((E, 128), FAR, F32)
    none = jnp.zeros((8, 128), F32)
    blank = jnp.zeros((E, 128), F32)
    for side in range(2):
        @pl.when(jnp.logical_not(there(-steps[side], 0)))
        def _():
            for f in range(3):
                y_state[side, f] = blank
                y_source[side, f] = blank
            for i in range(2):
                y_misc[side, E * i:E * (i + 1)] = far
            y_misc[side, 2 * E:] = none
            for i in range(4):
                yu_in[side, E * i:E * (i + 1)] = blank

        @pl.when(jnp.logical_not(there(0, -steps[side])))
        def _():
            for i in range(14):
                z_in[side, E * i:E * (i + 1)] = far
            z_in[side, 14 * E:] = none
            for i in range(6):
                zu_in[side, E * i:E * (i + 1)] = blank
            for k in range(NEWTON):
                for d in range(n):
                    coarse[k, 2 * side, d] = none

        for over in range(2):
            @pl.when(jnp.logical_not(there(-steps[side], -steps[over])))
            def _():
                d_in[2 * side + over, 0:E] = far
                d_in[2 * side + over, E:] = none
                du_in[2 * side + over] = blank

    pl.semaphore_wait(barrier, greeted)
    tell(0)
    for c in range(4):
        start(first_messages["d", c])
    for name in ("misc", "state", "source", "z"):
        for side in range(2):
            start(first_messages[name, side])

    for side in range(2):
        arrive(first_messages["z", side])
    z_unpack(views, lambda side, i: z_in[side, E * i:E * (i + 1)])
    for c in range(4):
        arrive(first_messages["d", c])
    corner_unpack(views, lambda c: d_in[c, 0:E])
    for side in range(2):
        for name in ("state", "source", "misc"):
            arrive(first_messages[name, side])

    steps_told = len(reaches(n))
    for i in range(min(1, steps_told)):
        told(i)

    def y_got(side, a):
        if a < 3:
            return y_state[side, a]
        return y_source[side, a - 3] if a < 6 else y_misc[side, 0:E]

    y_unpack(views, y_got, lambda side: y_misc[side, E:2 * E], (0, 1, 2, None, None, None, 3))

    for side in range(2):
        near[1 + 6 * side] = y_misc[side, 2 * E:]
        near[3 + 2 * side] = z_in[side, 14 * E:]
        for over in range(2):
            near[6 * side + 2 * over] = d_in[2 * side + over, E:]

    def by_region(values, t_kind):
        def row(i):
            return jnp.where(low_columns, values[i][0], jnp.where(own_columns, values[i][1], values[i][2]))
        middle = row(1)
        if t_kind == 0:
            return jnp.where(block == 0, row(0), middle)
        return jnp.where(block == 2, row(2), middle) if t_kind == 2 else middle

    walls = [[place_x + (me_s + i).astype(F32) / n + (me_g + j).astype(F32) / m - 1.0 for j in (-1, 0, 1)] for i in (-1, 0, 1)]
    wall_maps = [by_region(walls, i) for i in range(3)]
    row_index = lax.broadcasted_iota(jnp.int32, (E, 128), 0)
    x_open = jnp.where((row_index == 0) | (row_index == E - 1), 1.0, 0.0).astype(F32)

    def is_valid(rel):
        return (rel >= 0.0) & (rel <= 2.0)

    bricks = [jnp.where(is_valid(label[t, 0:8] - compare), 1.0, 0.0).astype(F32) for t in range(TILES)]
    for t in range(TILES):
        rel = label[t] - compare
        label[t] = rel
        good = is_valid(rel)
        for f in range(3):
            state[f, t, PAD:PAD + E] = jnp.where(good, state[f, t, PAD:PAD + E], 0.0)
        below = bricks[t - 1] if t > 0 else roll(bricks[TILES - 1], WIDE)
        above = bricks[t + 1] if t < TILES - 1 else roll(bricks[0], -WIDE)
        shut = 4.0 - (below + above + roll(bricks[t], 1) + roll(bricks[t], -1))
        missing = jnp.concatenate([shut] * 4, axis=0) + x_open
        solid = jnp.where(rel == 0.0, 0.05, jnp.where(rel == 1.0, 0.5, 1.5))
        source[2, t] = source[2, t] + solid * (wall_maps[kind(t)] * missing)

    for i in range(1, steps_told - 2):
        told(i)

    def around(ref, f, t):
        c = ref[f, t, PAD:PAD + E]
        total = ref[f, t, PAD - 1:PAD - 1 + E] + ref[f, t, PAD + 1:PAD + 1 + E]
        total = total + (roll(c, 1) + roll(c, -1))
        total = total + (ref[f, t - 1, PAD:PAD + E] if t > 0 else roll(ref[f, TILES - 1, PAD:PAD + E], WIDE))
        total = total + (ref[f, t + 1, PAD:PAD + E] if t < TILES - 1 else roll(ref[f, 0, PAD:PAD + E], -WIDE))
        return c, total

    def fold(x):
        return x[0:8] + x[8:16] + x[16:24] + x[24:32]

    def total_of(x):
        return jnp.sum(jnp.sum(x, axis=0, keepdims=True), axis=1, keepdims=True)

    def square_copy(k, d):
        return pltpu.make_async_remote_copy(
            src_ref=squares.at[k, 0], dst_ref=squares.at[k, d],
            send_sem=sq_send.at[k, d], recv_sem=sq_recv.at[k, d],
            device_id={"group": lax.rem(me_g + d, m)}, device_id_type=MESH)

    def coarse_copy(k, dg, d):
        return pltpu.make_async_remote_copy(
            src_ref=coarse.at[k, 1, me_s], dst_ref=coarse.at[k, 1 - dg, me_s],
            send_sem=c_send.at[k, 1 + dg, d], recv_sem=c_recv.at[k, 1 - dg, me_s],
            device_id={"space": lax.rem(me_s + d, n), "group": jnp.clip(me_g + dg, 0, m - 1)}, device_id_type=MESH)

    def coarse_arrival(k, dg, d):
        who = lax.rem(me_s + d, n)
        return pltpu.make_async_remote_copy(
            src_ref=coarse.at[k, 1 + dg, who], dst_ref=coarse.at[k, 1 + dg, who],
            send_sem=c_send.at[k, 1 + dg, d], recv_sem=c_recv.at[k, 1 + dg, who],
            device_id={"space": lax.rem(me_s + (1 if n > 1 else 0), n)}, device_id_type=MESH)

    def sweep(k, carry):
        square = jnp.zeros((E, 128), F32)
        for t in range(TILES):
            rel = label[t]
            pore = rel == 0.0
            active = rel == 1.0
            good = is_valid(rel)
            mine_here = good & own_columns & own_rows[kind(t)]
            conduct = (jnp.where(pore, 1.0, 0.2), jnp.where(pore, 1.0, 0.1),
                       jnp.where(pore, 0.05, jnp.where(active, 0.5, 1.5)))
            rates = jnp.where(pore, 0.0, jnp.where(active, 0.3, 0.02))
            pairs = [around(state, f, t) for f in range(3)]
            c, e, s = (p[0] for p in pairs)
            eta = s - e - 0.5 * c
            forward = jnp.exp(0.5 * eta)
            backward = jnp.exp(-0.5 * eta)
            current = rates * (forward - backward)
            slope = 0.5 * rates * (forward + backward)
            react = (-0.5 * current, -current, current)
            weight = jnp.where(good, OMEGA, 0.0)
            for f in range(3):
                v, total = pairs[f]
                misfit = 0.5 * v + conduct[f] * (6.0 * v - total) + react[f] - source[f, t]
                square = square + jnp.where(mine_here, misfit * misfit, 0.0)
                dg = 0.5 + 6.0 * conduct[f] + (0.25 * slope if f == 0 else slope)
                w = weight / dg
                upd[0, f, t, PAD:PAD + E] = -w * misfit
                gain[f, t] = w * conduct[f]
                mix[f, t] = w * slope * (0.5 if f == 0 else 1.0)
                diag[f, t] = jnp.where(mine_here, dg * (1.0 / OMEGA), 0.0)
        @pl.when(k == 0)
        def _():
            for i in range(max(1, steps_told - 2), steps_told - 1):
                told(i)

        squares[k, 0] = fold(square)
        for d in range(1, m):
            square_copy(k, d).start()

        def terms(u, t):
            pairs = [around(u, f, t) for f in range(3)]
            c, e, s = (p[0] for p in pairs)
            half = 0.5 * c
            cross = (s - e, s - half, e + half)
            return [(pairs[f][0], upd[0, f, t, PAD:PAD + E] + gain[f, t] * pairs[f][1] + mix[f, t] * cross[f]) for f in range(3)]

        def smooth(p, carry):
            u = upd.at[jnp.where(p == 0, 0, 1 + lax.rem(p + 1, 2))]
            later = upd.at[1 + lax.rem(p, 2)]
            for t in range(TILES):
                for f, (v, term) in enumerate(terms(u, t)):
                    later[f, t, PAD:PAD + E] = (1.0 - OMEGA) * v + term
            return carry

        lax.fori_loop(0, SMOOTH - 1, smooth, 0)
        final = 1 + (SMOOTH - 2) % 2
        u = upd.at[final]
        u_views = [padded(u, f) for f in range(3)]

        @pl.when(k < NEWTON - 1)
        def _():
            for side in range(2):
                tiles, fifth = [], None
                for f in range(3):
                    tile = None
                    for q in range(4):
                        t, first = spot(E - 4 + q if side == 0 else q)
                        part = roll(u_views[f].read(t), 32 * q - first)
                        tile = part if tile is None else jnp.where(quarter == q, part, tile)
                    tiles.append(tile)
                    t, first = spot(E - 5 if side == 0 else 4)
                    part = roll(u_views[f].read(t), 32 * f - first)
                    fifth = part if fifth is None else jnp.where(quarter == f, part, fifth)
                for i, tile in enumerate(tiles + [fifth]):
                    yu_out[side, E * i:E * (i + 1)] = tile
                start(update_messages["y", side])
                for over in range(2):
                    du_out[2 * side + over] = corner_pack(tiles, over)
                    start(update_messages["d", 2 * side + over])

        sums = [jnp.zeros((E, 128), F32) for _ in range(3)]
        for t in range(TILES):
            for f, (v, term) in enumerate(terms(u, t)):
                sums[f] = sums[f] + diag[f, t] * (term - OMEGA * v)
        totals = [total_of(x) for x in sums]
        for d in range(1, m):
            square_copy(k, d).wait_recv()
        part = squares[k, 0]
        for d in range(1, m):
            part = part + squares[k, d]
        packed = jnp.where(lane8 == 127, total_of(part), 0.0)
        for f in range(3):
            packed = jnp.where(lane8 == 3 * me_s + f, totals[f], packed)
        coarse[k, 1, me_s] = packed

        @pl.when(k == 0)
        def _():
            for i in range(max(1, steps_told - 1), steps_told):
                told(i)

        for d in range(1, n):
            coarse_copy(k, 0, d).start()

        def damping_of(group):
            whole = jnp.sum(jnp.where(lane8 == 127, group, 0.0), axis=1, keepdims=True)[0:1]
            cells = 3.0 * n * m * E * E * E
            return 1.0 / (1.0 + jnp.sqrt(whole / cells + 1e-6))

        def group_sum(i):
            acc = coarse[k, i, 0]
            for d in range(1, n):
                acc = acc + coarse[k, i, d]
            return acc

        @pl.when(k < NEWTON - 1)
        def _():
            for dg in (-1, 1):
                @pl.when(there(0, dg))
                def _():
                    for d in range(n):
                        coarse_copy(k, dg, d).start()
            for side in range(2):
                for i, tile in enumerate(z_pack(u_views, side)):
                    zu_out[side, E * i:E * (i + 1)] = tile
                start(update_messages["z", side])
            for side in range(2):
                arrive(update_messages["z", side])
            z_unpack(u_views, lambda side, i: zu_in[side, E * i:E * (i + 1)])
            for c in range(4):
                arrive(update_messages["d", c])
            corner_unpack(u_views, lambda c: du_in[c])
            for side in range(2):
                arrive(update_messages["y", side])
            y_unpack(u_views, lambda side, a: yu_in[side, E * a:E * (a + 1)], lambda side: yu_in[side, 3 * E:], (0, 1, 2))

            for d in range(1, n):
                coarse_arrival(k, 0, d).wait_recv()
            for dg in (-1, 1):
                @pl.when(there(0, dg))
                def _():
                    for d in range(n):
                        coarse_arrival(k, dg, d).wait_recv()
            groups = [group_sum(i) for i in range(3)]
            damping = damping_of(groups[1])
            lifts = [[jnp.sum(near[3 * i + j] * groups[j], axis=1, keepdims=True) for j in range(3)] for i in range(3)]
            maps = [[by_region([[x[f:f + 1] for x in row] for row in lifts], i) for i in range(3)] for f in range(3)]
            for t in range(TILES):
                good = is_valid(label[t])
                for f in range(3):
                    value = state[f, t, PAD:PAD + E] + damping * (u[f, t, PAD:PAD + E] + maps[f][kind(t)])
                    state[f, t, PAD:PAD + E] = jnp.where(good, value, 0.0)

        @pl.when(k == NEWTON - 1)
        def _():
            for f in range(3):
                for i in range(RAW):
                    for view, where in ((padded(state, f), out), (u_views[f], last_u)):
                        tile = None
                        for q in range(4):
                            t, first = spot(4 * i + q)
                            part = roll(view.read(t), 32 * q - first)
                            tile = part if tile is None else jnp.where(quarter == q, part, tile)
                        where[f, :, i * 128:(i + 1) * 128] = tile
            for d in range(1, n):
                coarse_arrival(k, 0, d).wait_recv()
            group = group_sum(1)
            damping = damping_of(group)
            lift = mask * jnp.sum(near[4] * group, axis=1, keepdims=True)
            for f in range(3):
                out[f] = out[f] + damping * (last_u[f] + lift[f:f + 1])

        return carry

    lax.fori_loop(0, NEWTON, sweep, 0)

    for spec in list(first_messages.values()) + list(update_messages.values()):
        left(spec)
    for k in range(NEWTON):
        for d in range(1, m):
            square_copy(k, d).wait_send()
        for d in range(1, n):
            coarse_copy(k, 0, d).wait_send()
    for k in range(NEWTON - 1):
        for dg in (-1, 1):
            @pl.when(there(0, dg))
            def _():
                for d in range(n):
                    coarse_copy(k, dg, d).wait_send()


def shards(n, m, initial_state, phases, brick_coords, neighbours, source, coarse_inverse):
    anywhere = pl.BlockSpec(memory_space=pl.ANY)
    vmem = pl.BlockSpec(memory_space=pltpu.VMEM)
    padded = (3, TILES, E + 2 * PAD, 128)
    inner = (3, TILES, E, 128)
    dma = pltpu.SemaphoreType.DMA
    V = pltpu.VMEM
    result = pl.pallas_call(
        functools.partial(kernel, n, m),
        out_shape=V((3, E, E * E), F32),
        in_specs=[anywhere] * 5,
        out_specs=vmem,
        scratch_shapes=[
            pltpu.SMEM((1, 3), jnp.int32),
            V((3, 1, 3 * n), F32),
            V((3, E, E * E), F32),
            V((E, E * E), jnp.int32),
            V((3, E, E * E), F32),
            dma((5,)),
            V(padded, F32),
            V((SMOOTH - 1,) + padded, F32),
            V(inner, F32),
            V(inner, F32),
            V(inner, F32),
            V(inner, F32),
            V(inner[1:], F32),
            V((3, E, E * E), F32),
            V((9, 8, 128), F32),
            V((2, 3, E, 128), F32), V((2, 3, E, 128), F32),
            V((2, 2 * E + 8, 128), F32), V((2, 2 * E + 8, 128), F32),
            V((4, E + 8, 128), F32), V((4, E + 8, 128), F32),
            V((2, 14 * E + 8, 128), F32), V((2, 14 * E + 8, 128), F32),
            dma((12,)), dma((12,)),
            V((2, 4 * E, 128), F32), V((2, 4 * E, 128), F32),
            V((4, E, 128), F32), V((4, E, 128), F32),
            V((2, 6 * E, 128), F32), V((2, 6 * E, 128), F32),
            dma((8,)), dma((8,)),
            V((NEWTON, m, 8, 128), F32),
            dma((NEWTON, m)), dma((NEWTON, m)),
            V((NEWTON, 3, n, 8, 128), F32),
            dma((NEWTON, 3, n)), dma((NEWTON, 3, n)),
            pltpu.SemaphoreType.REGULAR((max(1, len(reaches(n))), 2)),
        ],
        compiler_params=pltpu.CompilerParams(
            collective_id=0, has_side_effects=True, vmem_limit_bytes=56 * 1024 * 1024
        ),
    )(brick_coords, jnp.swapaxes(coarse_inverse, 0, 1), initial_state[0], phases[0], source[0])
    return result[None]


def solution(mesh):
    both = ("group", "space")
    return jax.shard_map(
        functools.partial(shards, mesh.shape["space"], mesh.shape["group"]),
        mesh=mesh,
        in_specs=(
            P(both, None, None, None),
            P(both, None, None),
            P(both, None),
            P(both, None),
            P(both, None, None, None),
            P("group", "space", None),
        ),
        out_specs=P(both, None, None, None),
        check_vma=False,
    )
```

```python
import functools

import jax
import jax.numpy as jnp
from jax import lax
from jax.experimental import pallas as pl
from jax.experimental.pallas import tpu as pltpu
from jax.sharding import PartitionSpec as P

NEWTON = 2
SMOOTH = 4
E = 32
RAW = 8
DEEP = 5
WIDE = E + 2 * DEEP
BLOCKS = 3
TILES = WIDE // BLOCKS
PAD = 8
OMEGA = 0.8
FAR = -1000.0
MESH = pl.DeviceIdType.MESH
F32 = jnp.float32


def roll(x, shift):
    shift = shift % 128
    return x if shift == 0 else pltpu.roll(x, shift, 1)


def reaches(n):
    steps, known = [], 1
    while known < n - 1:
        steps.append(known)
        known *= 2
    return steps


def spot(y):
    block, tile = divmod(y + DEEP, TILES)
    return tile, WIDE * block + DEEP


def kernel(
    n, m,
    coords_in, inverse_in, state_hbm, phase_hbm, source_hbm, out,
    coords, inverse, state_in, phase_in, source_in, fetch,
    state, upd, gain, mix, diag, scale, source, label, last_u,
    near, y_state, y_source, y_misc_out, y_misc, d_out, d_in, z_out, z_in, zs_out, zs_in, in_send, in_recv,
    yu_out, yu_in, du_out, du_in, zu_out, zu_in, u_send, u_recv,
    squares, sq_send, sq_recv, coarse, c_send, c_recv, ready,
):
    me_s = lax.axis_index("space")
    me_g = lax.axis_index("group")
    lane = lax.broadcasted_iota(jnp.int32, (E, 128), 1)
    quarter = lane // 32
    block = jnp.where(lane < WIDE, 0, jnp.where(lane < 2 * WIDE, 1, 2))
    column = lane - WIDE * block
    slot = column // DEEP
    own_columns = (column >= DEEP) & (column < DEEP + E)
    low_columns = column < DEEP
    high_columns = (column >= DEEP + E) & (column < WIDE)
    own_rows = (block != 0, block >= 0, block != 2)
    lane8 = lax.broadcasted_iota(jnp.int32, (8, 128), 1)

    def kind(t):
        return 0 if t < DEEP else (1 if t < TILES - DEEP else 2)

    fetches = [
        pltpu.make_async_copy(a, b, fetch.at[i])
        for i, (a, b) in enumerate((
            (coords_in, coords), (state_hbm, state_in), (phase_hbm, phase_in),
            (source_hbm, source_in), (inverse_in, inverse),
        ))
    ]
    for copy in fetches:
        copy.start()

    def there(ds, dg):
        s, g = me_s + ds, me_g + dg
        return (s >= 0) & (s < n) & (g >= 0) & (g < m)

    def at(ds, dg):
        return {"space": jnp.clip(me_s + ds, 0, n - 1), "group": jnp.clip(me_g + dg, 0, m - 1)}

    barrier = pltpu.get_barrier_semaphore()

    def greet(s, g):
        pl.semaphore_signal(barrier, inc=1, device_id={"space": s, "group": g}, device_id_type=MESH)

    for ds in (-1, 0, 1):
        for dg in (-1, 0, 1):
            if ds or dg:
                @pl.when(there(ds, dg))
                def _():
                    greet(jnp.clip(me_s + ds, 0, n - 1), jnp.clip(me_g + dg, 0, m - 1))
    for d in range(1, m):
        other = lax.rem(me_g + d, m)

        @pl.when((other != me_g - 1) & (other != me_g + 1))
        def _():
            greet(me_s, other)
    beside_g = jnp.where(me_g > 0, 1, 0) + jnp.where(me_g < m - 1, 1, 0)
    beside_s = jnp.where(me_s > 0, 1, 0) + jnp.where(me_s < n - 1, 1, 0)
    greeted = beside_s * (1 + beside_g) + m - 1

    def tell(i):
        if i < len(reaches(n)):
            for side, step in enumerate((reaches(n)[i], -reaches(n)[i])):
                @pl.when(there(step, 0))
                def _():
                    pl.semaphore_signal(ready.at[i, side], inc=1, device_id=at(step, 0), device_id_type=MESH)

    def told(i):
        for side, step in enumerate((reaches(n)[i], -reaches(n)[i])):
            @pl.when(there(-step, 0))
            def _():
                pl.semaphore_wait(ready.at[i, side], 1)
        tell(i + 1)

    def message(src, dst, sems, i, ds, dg):
        return pltpu.make_async_remote_copy(
            src_ref=src, dst_ref=dst, send_sem=sems[0].at[i], recv_sem=sems[1].at[i],
            device_id=at(ds, dg), device_id_type=MESH)

    ins = (in_send, in_recv)
    us = (u_send, u_recv)
    steps = (1, -1)
    first_messages, update_messages = {}, {}
    for side in range(2):
        cut = pl.ds(128 * (RAW - 1), 128) if side == 0 else pl.ds(0, 128)
        step = steps[side]
        first_messages["state", side] = (state_hbm.at[:, :, cut], y_state.at[side], ins, side, step, 0)
        first_messages["source", side] = (source_hbm.at[:, :, cut], y_source.at[side], ins, 2 + side, step, 0)
        first_messages["misc", side] = (y_misc_out.at[side], y_misc.at[side], ins, 4 + side, step, 0)
        first_messages["z", side] = (z_out.at[side], z_in.at[side], ins, 6 + side, 0, step)
        first_messages["zs", side] = (zs_out.at[side], zs_in.at[side], ins, 12 + side, 0, step)
        update_messages["y", side] = (yu_out.at[side], yu_in.at[side], us, side, step, 0)
        update_messages["z", side] = (zu_out.at[side], zu_in.at[side], us, 2 + side, 0, step)
        for over in range(2):
            c = 2 * side + over
            first_messages["d", c] = (d_out.at[c], d_in.at[c], ins, 8 + c, step, steps[over])
            update_messages["d", c] = (du_out.at[c], du_in.at[c], us, 4 + c, step, steps[over])

    def start(spec):
        @pl.when(there(spec[4], spec[5]))
        def _():
            message(*spec).start()

    def arrive(spec):
        @pl.when(there(-spec[4], -spec[5]))
        def _():
            message(*spec).wait_recv()

    def left(spec):
        @pl.when(there(spec[4], spec[5]))
        def _():
            message(*spec).wait_send()

    fetches[0].wait()
    occupied = coords[0, 0] >= 0
    mask = jnp.where(occupied, 1.0, 0.0).astype(F32)
    place_x = coords[0, 0].astype(F32)
    offset = 4.0 * place_x
    compare = jnp.where(occupied, offset, 1000.0)

    fetches[4].wait()
    near[4] = jnp.zeros((8, 128), F32)
    for f in range(3):
        near[4, f:f + 1, 0:3 * n] = inverse[f]
    mine = near[4]

    fetches[1].wait()
    fetches[2].wait()

    def raw_state(f, t):
        return state_in[f, :, t * 128:(t + 1) * 128]

    def raw_source(f, t):
        return source_in[f, :, t * 128:(t + 1) * 128]

    def raw_label(t):
        return phase_in[:, t * 128:(t + 1) * 128].astype(F32) + offset

    for side in range(2):
        edge, inner, q = ((RAW - 1, RAW - 2, 3), (0, 1, 0))[side]
        y_misc_out[side, 0:E] = raw_label(edge)
        fifth = roll(raw_label(inner), 32 * (3 - q))
        for f in range(3):
            fifth = jnp.where(quarter == f, roll(raw_state(f, inner), 32 * (f - q)), fifth)
        y_misc_out[side, E:2 * E] = fifth
        y_misc_out[side, 2 * E:] = mine

    small = (lane % 32) // 4

    def corner_pack(tiles, over):
        out_tile = None
        for a, tile in enumerate(tiles):
            part = roll(tile, 4 * a - (28 if over == 0 else 0))
            out_tile = part if out_tile is None else jnp.where(small == a, part, out_tile)
        return out_tile

    fetches[3].wait()
    for side in range(2):
        edge = (RAW - 1, 0)[side]
        tiles = [raw_state(f, edge) for f in range(3)] + [raw_label(edge)] + [raw_source(f, edge) for f in range(3)]
        for over in range(2):
            c = 2 * side + over
            d_out[c, 0:E] = corner_pack(tiles, over)
            d_out[c, E:] = mine

    class View:
        def __init__(self, read, write):
            self.read, self.write = read, write

    def padded(ref, f):
        def write(t, v):
            ref[f, t, PAD:PAD + E] = v
        return View(lambda t: ref[f, t, PAD:PAD + E], write)

    def plain(ref, *index):
        def write(t, v):
            ref[(*index, t)] = v
        return View(lambda t: ref[(*index, t)], write)

    views = [padded(state, f) for f in range(3)] + [plain(label)] + [plain(source, f) for f in range(3)]
    raws = [functools.partial(raw_state, f) for f in range(3)] + [raw_label] + [functools.partial(raw_source, f) for f in range(3)]

    zero_rows = jnp.zeros((PAD, 128), F32)
    for t in range(TILES):
        for f in range(3):
            state[f, t, 0:PAD] = zero_rows
            state[f, t, PAD + E:] = zero_rows
            for b in range(SMOOTH - 1):
                upd[b, f, t, 0:PAD] = zero_rows
                upd[b, f, t, PAD + E:] = zero_rows
        for a, (view, raw) in enumerate(zip(views, raws)):
            tile = jnp.full((E, 128), FAR if a == 3 else 0.0, F32)
            for b in range(BLOCKS):
                y = TILES * b + t - DEEP
                if 0 <= y < E:
                    moved = roll(raw(y // 4), WIDE * b + DEEP - 32 * (y % 4))
                    tile = jnp.where(own_columns & (block == b), moved, tile)
            view.write(t, tile)

    half_slots = WIDE // DEEP

    def z_pack(parts, side):
        shift = -(E if side == 0 else DEEP)
        packed = []
        for view in parts:
            for low in (0, half_slots):
                acc = None
                for j in range(min(half_slots, TILES - low)):
                    part = roll(view.read(low + j), DEEP * j + shift)
                    acc = part if acc is None else jnp.where(slot == j, part, acc)
                packed.append(acc)
        return packed

    def z_unpack(parts, got):
        for a, view in enumerate(parts):
            for t in range(TILES):
                half, j = divmod(t, half_slots)
                rows = own_rows[kind(t)]
                tile = jnp.where(low_columns & rows, roll(got(0, 2 * a + half), -DEEP * j), view.read(t))
                view.write(t, jnp.where(high_columns & rows, roll(got(1, 2 * a + half), DEEP + E - DEEP * j), tile))

    def halo_tile(side, q):
        if side == 0:
            return (0 if q < 0 else 1 + q), 0
        return (TILES - 1 if q < 0 else TILES - DEEP + q), 2 * WIDE

    def corner_unpack(parts, got):
        for side in range(2):
            for q in range(4):
                t, first = halo_tile(side, q)
                for a, view in enumerate(parts):
                    tile = view.read(t)
                    for over in range(2):
                        begin = first + (1 if over == 0 else DEEP + E)
                        moved = roll(got(2 * side + over), begin - (32 * q + 4 * a))
                        tile = jnp.where((lane >= begin) & (lane < begin + 4), moved, tile)
                    view.write(t, tile)

    def y_unpack(parts, got, fifth, blocks):
        for side in range(2):
            for q in range(-1, 4):
                t, first = halo_tile(side, q)
                here = (lane >= first + DEEP) & (lane < first + DEEP + E)
                for a, view in enumerate(parts):
                    if q < 0 and blocks[a] is None:
                        continue
                    if q < 0:
                        moved = roll(fifth(side), first + DEEP - 32 * blocks[a])
                    else:
                        moved = roll(got(side, a), first + DEEP - 32 * q)
                    view.write(t, jnp.where(here, moved, view.read(t)))

    for side in range(2):
        for i, tile in enumerate(z_pack(views[:4], side)):
            z_out[side, E * i:E * (i + 1)] = tile
        z_out[side, 8 * E:] = mine
        for i, tile in enumerate(z_pack(views[4:], side)):
            zs_out[side, E * i:E * (i + 1)] = tile

    far = jnp.full((E, 128), FAR, F32)
    none = jnp.zeros((8, 128), F32)
    blank = jnp.zeros((E, 128), F32)
    for side in range(2):
        @pl.when(jnp.logical_not(there(-steps[side], 0)))
        def _():
            for f in range(3):
                y_state[side, f] = blank
                y_source[side, f] = blank
            for i in range(2):
                y_misc[side, E * i:E * (i + 1)] = far
            y_misc[side, 2 * E:] = none
            for i in range(4):
                yu_in[side, E * i:E * (i + 1)] = blank

        @pl.when(jnp.logical_not(there(0, -steps[side])))
        def _():
            for i in range(8):
                z_in[side, E * i:E * (i + 1)] = far
            z_in[side, 8 * E:] = none
            for i in range(6):
                zs_in[side, E * i:E * (i + 1)] = blank
                zu_in[side, E * i:E * (i + 1)] = blank
            for k in range(NEWTON):
                for d in range(n):
                    coarse[k, 2 * side, d] = none

        for over in range(2):
            @pl.when(jnp.logical_not(there(-steps[side], -steps[over])))
            def _():
                d_in[2 * side + over, 0:E] = far
                d_in[2 * side + over, E:] = none
                du_in[2 * side + over] = blank

    pl.semaphore_wait(barrier, greeted)
    tell(0)
    for c in range(4):
        start(first_messages["d", c])
    for name in ("misc", "state", "z", "zs"):
        for side in range(2):
            start(first_messages[name, side])

    for side in range(2):
        arrive(first_messages["z", side])
    for side in range(2):
        start(first_messages["source", side])
    z_unpack(views[:4], lambda side, i: z_in[side, E * i:E * (i + 1)])
    for side in range(2):
        arrive(first_messages["zs", side])
    z_unpack(views[4:], lambda side, i: zs_in[side, E * i:E * (i + 1)])
    for c in range(4):
        arrive(first_messages["d", c])
    corner_unpack(views, lambda c: d_in[c, 0:E])
    for side in range(2):
        for name in ("state", "misc"):
            arrive(first_messages[name, side])

    steps_told = len(reaches(n))
    for i in range(min(1, steps_told)):
        told(i)

    y_unpack(views[:4], lambda side, a: y_state[side, a] if a < 3 else y_misc[side, 0:E], lambda side: y_misc[side, E:2 * E], (0, 1, 2, 3))

    for side in range(2):
        near[1 + 6 * side] = y_misc[side, 2 * E:]
        near[3 + 2 * side] = z_in[side, 8 * E:]
        for over in range(2):
            near[6 * side + 2 * over] = d_in[2 * side + over, E:]

    def by_region(values, t_kind):
        def row(i):
            return jnp.where(low_columns, values[i][0], jnp.where(own_columns, values[i][1], values[i][2]))
        middle = row(1)
        if t_kind == 0:
            return jnp.where(block == 0, row(0), middle)
        return jnp.where(block == 2, row(2), middle) if t_kind == 2 else middle

    walls = [[place_x + (me_s + i).astype(F32) / n + (me_g + j).astype(F32) / m - 1.0 for j in (-1, 0, 1)] for i in (-1, 0, 1)]
    wall_maps = [by_region(walls, i) for i in range(3)]
    row_index = lax.broadcasted_iota(jnp.int32, (E, 128), 0)
    x_open = jnp.where((row_index == 0) | (row_index == E - 1), 1.0, 0.0).astype(F32)

    def is_valid(rel):
        return (rel >= 0.0) & (rel <= 2.0)

    bricks = [jnp.where(is_valid(label[t, 0:8] - compare), 1.0, 0.0).astype(F32) for t in range(TILES)]
    for t in range(TILES):
        rel = label[t] - compare
        label[t] = rel
        good = is_valid(rel)
        for f in range(3):
            state[f, t, PAD:PAD + E] = jnp.where(good, state[f, t, PAD:PAD + E], 0.0)
        below = bricks[t - 1] if t > 0 else roll(bricks[TILES - 1], WIDE)
        above = bricks[t + 1] if t < TILES - 1 else roll(bricks[0], -WIDE)
        shut = 4.0 - (below + above + roll(bricks[t], 1) + roll(bricks[t], -1))
        missing = jnp.concatenate([shut] * 4, axis=0) + x_open
        solid = jnp.where(rel == 0.0, 0.05, jnp.where(rel == 1.0, 0.5, 1.5))
        source[2, t] = source[2, t] + solid * (wall_maps[kind(t)] * missing)

    for i in range(1, steps_told - 2):
        told(i)

    def tiles_of(ref):
        return [[ref[f, t, PAD:PAD + E] for t in range(TILES)] for f in range(3)]

    def around(ref, tiles, f, t):
        c = tiles[f][t]
        total = ref[f, t, PAD - 1:PAD - 1 + E] + ref[f, t, PAD + 1:PAD + 1 + E]
        total = total + (roll(c, 1) + roll(c, -1))
        total = total + (tiles[f][t - 1] if t > 0 else roll(tiles[f][TILES - 1], WIDE))
        total = total + (tiles[f][t + 1] if t < TILES - 1 else roll(tiles[f][0], -WIDE))
        return c, total

    def fold(x):
        return x[0:8] + x[8:16] + x[16:24] + x[24:32]

    def total_of(x):
        return jnp.sum(jnp.sum(x, axis=0, keepdims=True), axis=1, keepdims=True)

    def square_copy(k, d):
        return pltpu.make_async_remote_copy(
            src_ref=squares.at[k, 0], dst_ref=squares.at[k, d],
            send_sem=sq_send.at[k, d], recv_sem=sq_recv.at[k, d],
            device_id={"group": lax.rem(me_g + d, m)}, device_id_type=MESH)

    def coarse_copy(k, dg, d):
        return pltpu.make_async_remote_copy(
            src_ref=coarse.at[k, 1, me_s], dst_ref=coarse.at[k, 1 - dg, me_s],
            send_sem=c_send.at[k, 1 + dg, d], recv_sem=c_recv.at[k, 1 - dg, me_s],
            device_id={"space": lax.rem(me_s + d, n), "group": jnp.clip(me_g + dg, 0, m - 1)}, device_id_type=MESH)

    def coarse_arrival(k, dg, d):
        who = lax.rem(me_s + d, n)
        return pltpu.make_async_remote_copy(
            src_ref=coarse.at[k, 1 + dg, who], dst_ref=coarse.at[k, 1 + dg, who],
            send_sem=c_send.at[k, 1 + dg, d], recv_sem=c_recv.at[k, 1 + dg, who],
            device_id={"space": lax.rem(me_s + (1 if n > 1 else 0), n)}, device_id_type=MESH)

    def sweep(k, carry):
        square = jnp.zeros((E, 128), F32)
        tiles = tiles_of(state)
        for t in range(TILES):
            rel = label[t]
            pore = rel == 0.0
            active = rel == 1.0
            good = is_valid(rel)
            mine_here = good & own_columns & own_rows[kind(t)]
            conduct = (jnp.where(pore, 1.0, 0.2), jnp.where(pore, 1.0, 0.1),
                       jnp.where(pore, 0.05, jnp.where(active, 0.5, 1.5)))
            rates = jnp.where(pore, 0.0, jnp.where(active, 0.3, 0.02))
            pairs = [around(state, tiles, f, t) for f in range(3)]
            c, e, s = (p[0] for p in pairs)
            eta = s - e - 0.5 * c
            forward = jnp.exp(0.5 * eta)
            backward = jnp.exp(-0.5 * eta)
            current = rates * (forward - backward)
            slope = 0.5 * rates * (forward + backward)
            react = (-0.5 * current, -current, current)
            weight = jnp.where(good, OMEGA, 0.0)
            for f in range(3):
                v, total = pairs[f]
                misfit = 0.5 * v + conduct[f] * (6.0 * v - total) + react[f] - source[f, t]
                square = square + jnp.where(mine_here, misfit * misfit, 0.0)
                dg = 0.5 + 6.0 * conduct[f] + (0.25 * slope if f == 0 else slope)
                w = weight / dg
                if kind(t) != 1:
                    scale[f, t] = w
                upd[0, f, t, PAD:PAD + E] = -w * misfit
                gain[f, t] = w * conduct[f]
                mix[f, t] = w * slope * (0.5 if f == 0 else 1.0)
                diag[f, t] = jnp.where(mine_here, dg * (1.0 / OMEGA), 0.0)
        squares[k, 0] = fold(square)
        for d in range(1, m):
            square_copy(k, d).start()

        @pl.when(k == 0)
        def _():
            for i in range(max(1, steps_told - 2), steps_told - 1):
                told(i)
            for side in range(2):
                arrive(first_messages["source", side])
            for side in range(2):
                for q in range(4):
                    t, first = halo_tile(side, q)
                    here = (lane >= first + DEEP) & (lane < first + DEEP + E)
                    for f in range(3):
                        late = jnp.where(here, roll(y_source[side, f], first + DEEP - 32 * q), 0.0)
                        source[f, t] = source[f, t] + late
                        upd[0, f, t, PAD:PAD + E] = upd[0, f, t, PAD:PAD + E] + scale[f, t] * late

        def terms(u, tiles, t):
            pairs = [around(u, tiles, f, t) for f in range(3)]
            c, e, s = (p[0] for p in pairs)
            half = 0.5 * c
            cross = (s - e, s - half, e + half)
            return [(pairs[f][0], upd[0, f, t, PAD:PAD + E] + gain[f, t] * pairs[f][1] + mix[f, t] * cross[f]) for f in range(3)]

        def smooth(p, carry):
            u = upd.at[jnp.where(p == 0, 0, 1 + lax.rem(p + 1, 2))]
            later = upd.at[1 + lax.rem(p, 2)]
            tiles = tiles_of(u)
            for t in range(TILES):
                for f, (v, term) in enumerate(terms(u, tiles, t)):
                    later[f, t, PAD:PAD + E] = (1.0 - OMEGA) * v + term
            return carry

        lax.fori_loop(0, SMOOTH - 1, smooth, 0)
        final = 1 + (SMOOTH - 2) % 2
        u = upd.at[final]
        u_views = [padded(u, f) for f in range(3)]

        @pl.when(k < NEWTON - 1)
        def _():
            for side in range(2):
                tiles, fifth = [], None
                for f in range(3):
                    tile = None
                    for q in range(4):
                        t, first = spot(E - 4 + q if side == 0 else q)
                        part = roll(u_views[f].read(t), 32 * q - first)
                        tile = part if tile is None else jnp.where(quarter == q, part, tile)
                    tiles.append(tile)
                    t, first = spot(E - 5 if side == 0 else 4)
                    part = roll(u_views[f].read(t), 32 * f - first)
                    fifth = part if fifth is None else jnp.where(quarter == f, part, fifth)
                for i, tile in enumerate(tiles + [fifth]):
                    yu_out[side, E * i:E * (i + 1)] = tile
                start(update_messages["y", side])
                for over in range(2):
                    du_out[2 * side + over] = corner_pack(tiles, over)
                    start(update_messages["d", 2 * side + over])

        sums = [jnp.zeros((E, 128), F32) for _ in range(3)]
        tiles = tiles_of(u)
        for t in range(TILES):
            for f, (v, term) in enumerate(terms(u, tiles, t)):
                sums[f] = sums[f] + diag[f, t] * (term - OMEGA * v)
        totals = [total_of(x) for x in sums]
        for d in range(1, m):
            square_copy(k, d).wait_recv()
        part = squares[k, 0]
        for d in range(1, m):
            part = part + squares[k, d]
        packed = jnp.where(lane8 == 127, total_of(part), 0.0)
        for f in range(3):
            packed = jnp.where(lane8 == 3 * me_s + f, totals[f], packed)
        coarse[k, 1, me_s] = packed

        @pl.when(k == 0)
        def _():
            for i in range(max(1, steps_told - 1), steps_told):
                told(i)

        for d in range(1, n):
            coarse_copy(k, 0, d).start()

        def damping_of(group):
            whole = jnp.sum(jnp.where(lane8 == 127, group, 0.0), axis=1, keepdims=True)[0:1]
            cells = 3.0 * n * m * E * E * E
            return 1.0 / (1.0 + jnp.sqrt(whole / cells + 1e-6))

        def group_sum(i):
            acc = coarse[k, i, 0]
            for d in range(1, n):
                acc = acc + coarse[k, i, d]
            return acc

        @pl.when(k < NEWTON - 1)
        def _():
            for dg in (-1, 1):
                @pl.when(there(0, dg))
                def _():
                    for d in range(n):
                        coarse_copy(k, dg, d).start()
            for side in range(2):
                for i, tile in enumerate(z_pack(u_views, side)):
                    zu_out[side, E * i:E * (i + 1)] = tile
                start(update_messages["z", side])
            for side in range(2):
                arrive(update_messages["z", side])
            z_unpack(u_views, lambda side, i: zu_in[side, E * i:E * (i + 1)])
            for c in range(4):
                arrive(update_messages["d", c])
            corner_unpack(u_views, lambda c: du_in[c])
            for side in range(2):
                arrive(update_messages["y", side])
            y_unpack(u_views, lambda side, a: yu_in[side, E * a:E * (a + 1)], lambda side: yu_in[side, 3 * E:], (0, 1, 2))

            for d in range(1, n):
                coarse_arrival(k, 0, d).wait_recv()
            for dg in (-1, 1):
                @pl.when(there(0, dg))
                def _():
                    for d in range(n):
                        coarse_arrival(k, dg, d).wait_recv()
            groups = [group_sum(i) for i in range(3)]
            damping = damping_of(groups[1])
            lifts = [[jnp.sum(near[3 * i + j] * groups[j], axis=1, keepdims=True) for j in range(3)] for i in range(3)]
            maps = [[by_region([[x[f:f + 1] for x in row] for row in lifts], i) for i in range(3)] for f in range(3)]
            for t in range(TILES):
                good = is_valid(label[t])
                for f in range(3):
                    value = state[f, t, PAD:PAD + E] + damping * (u[f, t, PAD:PAD + E] + maps[f][kind(t)])
                    state[f, t, PAD:PAD + E] = jnp.where(good, value, 0.0)

        @pl.when(k == NEWTON - 1)
        def _():
            for f in range(3):
                for i in range(RAW):
                    for view, where in ((padded(state, f), out), (u_views[f], last_u)):
                        tile = None
                        for q in range(4):
                            t, first = spot(4 * i + q)
                            part = roll(view.read(t), 32 * q - first)
                            tile = part if tile is None else jnp.where(quarter == q, part, tile)
                        where[f, :, i * 128:(i + 1) * 128] = tile
            for d in range(1, n):
                coarse_arrival(k, 0, d).wait_recv()
            group = group_sum(1)
            damping = damping_of(group)
            lift = mask * jnp.sum(near[4] * group, axis=1, keepdims=True)
            for f in range(3):
                out[f] = out[f] + damping * (last_u[f] + lift[f:f + 1])

        return carry

    lax.fori_loop(0, NEWTON, sweep, 0)

    for spec in list(first_messages.values()) + list(update_messages.values()):
        left(spec)
    for k in range(NEWTON):
        for d in range(1, m):
            square_copy(k, d).wait_send()
        for d in range(1, n):
            coarse_copy(k, 0, d).wait_send()
    for k in range(NEWTON - 1):
        for dg in (-1, 1):
            @pl.when(there(0, dg))
            def _():
                for d in range(n):
                    coarse_copy(k, dg, d).wait_send()


def shards(n, m, initial_state, phases, brick_coords, neighbours, source, coarse_inverse):
    anywhere = pl.BlockSpec(memory_space=pl.ANY)
    vmem = pl.BlockSpec(memory_space=pltpu.VMEM)
    padded = (3, TILES, E + 2 * PAD, 128)
    inner = (3, TILES, E, 128)
    dma = pltpu.SemaphoreType.DMA
    V = pltpu.VMEM
    result = pl.pallas_call(
        functools.partial(kernel, n, m),
        out_shape=V((3, E, E * E), F32),
        in_specs=[anywhere] * 5,
        out_specs=vmem,
        scratch_shapes=[
            pltpu.SMEM((1, 3), jnp.int32),
            V((3, 1, 3 * n), F32),
            V((3, E, E * E), F32),
            V((E, E * E), jnp.int32),
            V((3, E, E * E), F32),
            dma((5,)),
            V(padded, F32),
            V((SMOOTH - 1,) + padded, F32),
            V(inner, F32),
            V(inner, F32),
            V(inner, F32),
            V(inner, F32),
            V(inner, F32),
            V(inner[1:], F32),
            V((3, E, E * E), F32),
            V((9, 8, 128), F32),
            V((2, 3, E, 128), F32), V((2, 3, E, 128), F32),
            V((2, 2 * E + 8, 128), F32), V((2, 2 * E + 8, 128), F32),
            V((4, E + 8, 128), F32), V((4, E + 8, 128), F32),
            V((2, 8 * E + 8, 128), F32), V((2, 8 * E + 8, 128), F32),
            V((2, 6 * E, 128), F32), V((2, 6 * E, 128), F32),
            dma((14,)), dma((14,)),
            V((2, 4 * E, 128), F32), V((2, 4 * E, 128), F32),
            V((4, E, 128), F32), V((4, E, 128), F32),
            V((2, 6 * E, 128), F32), V((2, 6 * E, 128), F32),
            dma((8,)), dma((8,)),
            V((NEWTON, m, 8, 128), F32),
            dma((NEWTON, m)), dma((NEWTON, m)),
            V((NEWTON, 3, n, 8, 128), F32),
            dma((NEWTON, 3, n)), dma((NEWTON, 3, n)),
            pltpu.SemaphoreType.REGULAR((max(1, len(reaches(n))), 2)),
        ],
        compiler_params=pltpu.CompilerParams(
            collective_id=0, has_side_effects=True, vmem_limit_bytes=56 * 1024 * 1024
        ),
    )(brick_coords, jnp.swapaxes(coarse_inverse, 0, 1), initial_state[0], phases[0], source[0])
    return result[None]


def solution(mesh):
    both = ("group", "space")
    return jax.shard_map(
        functools.partial(shards, mesh.shape["space"], mesh.shape["group"]),
        mesh=mesh,
        in_specs=(
            P(both, None, None, None),
            P(both, None, None),
            P(both, None),
            P(both, None),
            P(both, None, None, None),
            P("group", "space", None),
        ),
        out_specs=P(both, None, None, None),
        check_vma=False,
    )
```

```python
import functools

import jax
import jax.numpy as jnp
from jax import lax
from jax.experimental import pallas as pl
from jax.experimental.pallas import tpu as pltpu
from jax.sharding import PartitionSpec as P

NEWTON = 2
SMOOTH = 4
E = 32
RAW = 8
DEEP = 5
WIDE = E + 2 * DEEP
BLOCKS = 3
TILES = WIDE // BLOCKS
PAD = 8
OMEGA = 0.8
FAR = -1000.0
MESH = pl.DeviceIdType.MESH
F32 = jnp.float32


def roll(x, shift):
    shift = shift % 128
    return x if shift == 0 else pltpu.roll(x, shift, 1)


def reaches(n):
    steps, known = [], 1
    while known < n - 1:
        steps.append(known)
        known *= 2
    return steps


def spot(y):
    block, tile = divmod(y + DEEP, TILES)
    return tile, WIDE * block + DEEP


def kernel(
    n, m,
    coords_in, inverse_in, state_hbm, phase_hbm, source_hbm, out,
    coords, inverse, state_in, phase_in, source_in, fetch,
    state, upd, gain, mix, diag, scale, source, label, last_u,
    near, y_state, y_source, y_misc_out, y_misc, d_out, d_in, z_out, z_in, zs_out, zs_in, in_send, in_recv,
    yu_out, yu_in, du_out, du_in, zu_out, zu_in, u_send, u_recv,
    squares, sq_send, sq_recv, coarse, c_send, c_recv, ready,
):
    me_s = lax.axis_index("space")
    me_g = lax.axis_index("group")
    lane = lax.broadcasted_iota(jnp.int32, (E, 128), 1)
    quarter = lane // 32
    block = jnp.where(lane < WIDE, 0, jnp.where(lane < 2 * WIDE, 1, 2))
    column = lane - WIDE * block
    slot = column // DEEP
    own_columns = (column >= DEEP) & (column < DEEP + E)
    low_columns = column < DEEP
    high_columns = (column >= DEEP + E) & (column < WIDE)
    own_rows = (block != 0, block >= 0, block != 2)
    lane8 = lax.broadcasted_iota(jnp.int32, (8, 128), 1)

    def kind(t):
        return 0 if t < DEEP else (1 if t < TILES - DEEP else 2)

    fetches = [
        pltpu.make_async_copy(a, b, fetch.at[i])
        for i, (a, b) in enumerate((
            (coords_in, coords), (state_hbm, state_in), (phase_hbm, phase_in),
            (source_hbm, source_in), (inverse_in, inverse),
        ))
    ]
    for copy in fetches:
        copy.start()

    def there(ds, dg):
        s, g = me_s + ds, me_g + dg
        return (s >= 0) & (s < n) & (g >= 0) & (g < m)

    def at(ds, dg):
        return {"space": jnp.clip(me_s + ds, 0, n - 1), "group": jnp.clip(me_g + dg, 0, m - 1)}

    barrier = pltpu.get_barrier_semaphore()

    def greet(s, g):
        pl.semaphore_signal(barrier, inc=1, device_id={"space": s, "group": g}, device_id_type=MESH)

    for ds in (-1, 0, 1):
        for dg in (-1, 0, 1):
            if ds or dg:
                @pl.when(there(ds, dg))
                def _():
                    greet(jnp.clip(me_s + ds, 0, n - 1), jnp.clip(me_g + dg, 0, m - 1))
    for d in range(1, m):
        other = lax.rem(me_g + d, m)

        @pl.when((other != me_g - 1) & (other != me_g + 1))
        def _():
            greet(me_s, other)
    beside_g = jnp.where(me_g > 0, 1, 0) + jnp.where(me_g < m - 1, 1, 0)
    beside_s = jnp.where(me_s > 0, 1, 0) + jnp.where(me_s < n - 1, 1, 0)
    greeted = beside_s * (1 + beside_g) + m - 1

    def tell(i):
        if i < len(reaches(n)):
            for side, step in enumerate((reaches(n)[i], -reaches(n)[i])):
                @pl.when(there(step, 0))
                def _():
                    pl.semaphore_signal(ready.at[i, side], inc=1, device_id=at(step, 0), device_id_type=MESH)

    def told(i):
        for side, step in enumerate((reaches(n)[i], -reaches(n)[i])):
            @pl.when(there(-step, 0))
            def _():
                pl.semaphore_wait(ready.at[i, side], 1)
        tell(i + 1)

    def message(src, dst, sems, i, ds, dg):
        return pltpu.make_async_remote_copy(
            src_ref=src, dst_ref=dst, send_sem=sems[0].at[i], recv_sem=sems[1].at[i],
            device_id=at(ds, dg), device_id_type=MESH)

    ins = (in_send, in_recv)
    us = (u_send, u_recv)
    steps = (1, -1)
    first_messages, update_messages = {}, {}
    for side in range(2):
        cut = pl.ds(128 * (RAW - 1), 128) if side == 0 else pl.ds(0, 128)
        step = steps[side]
        first_messages["state", side] = (state_hbm.at[:, :, cut], y_state.at[side], ins, side, step, 0)
        first_messages["source", side] = (source_hbm.at[:, :, cut], y_source.at[side], ins, 2 + side, step, 0)
        first_messages["misc", side] = (y_misc_out.at[side], y_misc.at[side], ins, 4 + side, step, 0)
        first_messages["z", side] = (z_out.at[side], z_in.at[side], ins, 6 + side, 0, step)
        first_messages["zs", side] = (zs_out.at[side], zs_in.at[side], ins, 12 + side, 0, step)
        update_messages["y", side] = (yu_out.at[side], yu_in.at[side], us, side, step, 0)
        update_messages["z", side] = (zu_out.at[side], zu_in.at[side], us, 2 + side, 0, step)
        for over in range(2):
            c = 2 * side + over
            first_messages["d", c] = (d_out.at[c], d_in.at[c], ins, 8 + c, step, steps[over])
            update_messages["d", c] = (du_out.at[c], du_in.at[c], us, 4 + c, step, steps[over])

    def start(spec):
        @pl.when(there(spec[4], spec[5]))
        def _():
            message(*spec).start()

    def arrive(spec):
        @pl.when(there(-spec[4], -spec[5]))
        def _():
            message(*spec).wait_recv()

    def left(spec):
        @pl.when(there(spec[4], spec[5]))
        def _():
            message(*spec).wait_send()

    fetches[0].wait()
    occupied = coords[0, 0] >= 0
    mask = jnp.where(occupied, 1.0, 0.0).astype(F32)
    place_x = coords[0, 0].astype(F32)
    offset = 4.0 * place_x
    compare = jnp.where(occupied, offset, 1000.0)

    fetches[4].wait()
    near[...] = jnp.zeros((8, 128), F32)
    for f in range(3):
        near[f:f + 1, 0:3 * n] = inverse[f]
    mine = near[...]

    fetches[1].wait()
    fetches[2].wait()

    def raw_state(f, t):
        return state_in[f, :, t * 128:(t + 1) * 128]

    def raw_source(f, t):
        return source_in[f, :, t * 128:(t + 1) * 128]

    def raw_label(t):
        return phase_in[:, t * 128:(t + 1) * 128].astype(F32) + offset

    for side in range(2):
        edge, inner, q = ((RAW - 1, RAW - 2, 3), (0, 1, 0))[side]
        y_misc_out[side, 0:E] = raw_label(edge)
        fifth = roll(raw_label(inner), 32 * (3 - q))
        for f in range(3):
            fifth = jnp.where(quarter == f, roll(raw_state(f, inner), 32 * (f - q)), fifth)
        y_misc_out[side, E:2 * E] = fifth
        yu_out[side, 3 * E:] = mine

    small = (lane % 32) // 4

    def corner_pack(tiles, over):
        out_tile = None
        for a, tile in enumerate(tiles):
            part = roll(tile, 4 * a - (28 if over == 0 else 0))
            out_tile = part if out_tile is None else jnp.where(small == a, part, out_tile)
        return out_tile

    fetches[3].wait()
    for side in range(2):
        edge = (RAW - 1, 0)[side]
        tiles = [raw_state(f, edge) for f in range(3)] + [raw_label(edge)] + [raw_source(f, edge) for f in range(3)]
        for over in range(2):
            c = 2 * side + over
            d_out[c] = corner_pack(tiles, over)
            du_out[c, E:] = mine

    class View:
        def __init__(self, read, write):
            self.read, self.write = read, write

    def padded(ref, f):
        def write(t, v):
            ref[f, t, PAD:PAD + E] = v
        return View(lambda t: ref[f, t, PAD:PAD + E], write)

    def plain(ref, *index):
        def write(t, v):
            ref[(*index, t)] = v
        return View(lambda t: ref[(*index, t)], write)

    views = [padded(state, f) for f in range(3)] + [plain(label)] + [plain(source, f) for f in range(3)]
    raws = [functools.partial(raw_state, f) for f in range(3)] + [raw_label] + [functools.partial(raw_source, f) for f in range(3)]

    zero_rows = jnp.zeros((PAD, 128), F32)
    for t in range(TILES):
        for f in range(3):
            state[f, t, 0:PAD] = zero_rows
            state[f, t, PAD + E:] = zero_rows
            for b in range(SMOOTH - 1):
                upd[b, f, t, 0:PAD] = zero_rows
                upd[b, f, t, PAD + E:] = zero_rows
        for a, (view, raw) in enumerate(zip(views, raws)):
            tile = jnp.full((E, 128), FAR if a == 3 else 0.0, F32)
            for b in range(BLOCKS):
                y = TILES * b + t - DEEP
                if 0 <= y < E:
                    moved = roll(raw(y // 4), WIDE * b + DEEP - 32 * (y % 4))
                    tile = jnp.where(own_columns & (block == b), moved, tile)
            view.write(t, tile)

    half_slots = WIDE // DEEP

    def z_pack(parts, side):
        shift = -(E if side == 0 else DEEP)
        packed = []
        for view in parts:
            for low in (0, half_slots):
                acc = None
                for j in range(min(half_slots, TILES - low)):
                    part = roll(view.read(low + j), DEEP * j + shift)
                    acc = part if acc is None else jnp.where(slot == j, part, acc)
                packed.append(acc)
        return packed

    def z_unpack(parts, got):
        for a, view in enumerate(parts):
            for t in range(TILES):
                half, j = divmod(t, half_slots)
                rows = own_rows[kind(t)]
                tile = jnp.where(low_columns & rows, roll(got(0, 2 * a + half), -DEEP * j), view.read(t))
                view.write(t, jnp.where(high_columns & rows, roll(got(1, 2 * a + half), DEEP + E - DEEP * j), tile))

    def halo_tile(side, q):
        if side == 0:
            return (0 if q < 0 else 1 + q), 0
        return (TILES - 1 if q < 0 else TILES - DEEP + q), 2 * WIDE

    def corner_unpack(parts, got):
        for side in range(2):
            for q in range(4):
                t, first = halo_tile(side, q)
                for a, view in enumerate(parts):
                    tile = view.read(t)
                    for over in range(2):
                        begin = first + (1 if over == 0 else DEEP + E)
                        moved = roll(got(2 * side + over), begin - (32 * q + 4 * a))
                        tile = jnp.where((lane >= begin) & (lane < begin + 4), moved, tile)
                    view.write(t, tile)

    def y_unpack(parts, got, fifth, blocks):
        for side in range(2):
            for q in range(-1, 4):
                t, first = halo_tile(side, q)
                here = (lane >= first + DEEP) & (lane < first + DEEP + E)
                for a, view in enumerate(parts):
                    if q < 0 and blocks[a] is None:
                        continue
                    if q < 0:
                        moved = roll(fifth(side), first + DEEP - 32 * blocks[a])
                    else:
                        moved = roll(got(side, a), first + DEEP - 32 * q)
                    view.write(t, jnp.where(here, moved, view.read(t)))

    for side in range(2):
        for i, tile in enumerate(z_pack(views[:4], side)):
            z_out[side, E * i:E * (i + 1)] = tile
        zu_out[side, 6 * E:] = mine
        for i, tile in enumerate(z_pack(views[4:], side)):
            zs_out[side, E * i:E * (i + 1)] = tile

    far = jnp.full((E, 128), FAR, F32)
    none = jnp.zeros((8, 128), F32)
    blank = jnp.zeros((E, 128), F32)
    for side in range(2):
        @pl.when(jnp.logical_not(there(-steps[side], 0)))
        def _():
            for f in range(3):
                y_state[side, f] = blank
                y_source[side, f] = blank
            for i in range(2):
                y_misc[side, E * i:E * (i + 1)] = far
            yu_in[side, 3 * E:] = none
            for i in range(3):
                yu_in[side, E * i:E * (i + 1)] = blank

        @pl.when(jnp.logical_not(there(0, -steps[side])))
        def _():
            for i in range(8):
                z_in[side, E * i:E * (i + 1)] = far
            zu_in[side, 6 * E:] = none
            for i in range(6):
                zs_in[side, E * i:E * (i + 1)] = blank
                zu_in[side, E * i:E * (i + 1)] = blank
            for k in range(NEWTON):
                for d in range(n):
                    coarse[k, 2 * side, d] = none

        for over in range(2):
            @pl.when(jnp.logical_not(there(-steps[side], -steps[over])))
            def _():
                d_in[2 * side + over] = far
                du_in[2 * side + over, 0:E] = blank
                du_in[2 * side + over, E:] = none

    pl.semaphore_wait(barrier, greeted)
    tell(0)
    for c in range(4):
        start(first_messages["d", c])
    for name in ("misc", "state", "z", "zs"):
        for side in range(2):
            start(first_messages[name, side])

    for side in range(2):
        arrive(first_messages["z", side])
    for side in range(2):
        start(first_messages["source", side])
    z_unpack(views[:4], lambda side, i: z_in[side, E * i:E * (i + 1)])
    for side in range(2):
        arrive(first_messages["zs", side])
    z_unpack(views[4:], lambda side, i: zs_in[side, E * i:E * (i + 1)])
    for c in range(4):
        arrive(first_messages["d", c])
    corner_unpack(views, lambda c: d_in[c])
    for side in range(2):
        for name in ("state", "misc"):
            arrive(first_messages[name, side])

    steps_told = len(reaches(n))
    for i in range(min(1, steps_told)):
        told(i)

    y_unpack(views[:4], lambda side, a: y_state[side, a] if a < 3 else y_misc[side, 0:E], lambda side: y_misc[side, E:2 * E], (0, 1, 2, 3))

    def by_region(values, t_kind):
        def row(i):
            return jnp.where(low_columns, values[i][0], jnp.where(own_columns, values[i][1], values[i][2]))
        middle = row(1)
        if t_kind == 0:
            return jnp.where(block == 0, row(0), middle)
        return jnp.where(block == 2, row(2), middle) if t_kind == 2 else middle

    walls = [[place_x + (me_s + i).astype(F32) / n + (me_g + j).astype(F32) / m - 1.0 for j in (-1, 0, 1)] for i in (-1, 0, 1)]
    wall_maps = [by_region(walls, i) for i in range(3)]
    row_index = lax.broadcasted_iota(jnp.int32, (E, 128), 0)
    x_open = jnp.where((row_index == 0) | (row_index == E - 1), 1.0, 0.0).astype(F32)

    def is_valid(rel):
        return (rel >= 0.0) & (rel <= 2.0)

    bricks = [jnp.where(is_valid(label[t, 0:8] - compare), 1.0, 0.0).astype(F32) for t in range(TILES)]
    for t in range(TILES):
        rel = label[t] - compare
        label[t] = rel
        good = is_valid(rel)
        for f in range(3):
            state[f, t, PAD:PAD + E] = jnp.where(good, state[f, t, PAD:PAD + E], 0.0)
        below = bricks[t - 1] if t > 0 else roll(bricks[TILES - 1], WIDE)
        above = bricks[t + 1] if t < TILES - 1 else roll(bricks[0], -WIDE)
        shut = 4.0 - (below + above + roll(bricks[t], 1) + roll(bricks[t], -1))
        missing = jnp.concatenate([shut] * 4, axis=0) + x_open
        solid = jnp.where(rel == 0.0, 0.05, jnp.where(rel == 1.0, 0.5, 1.5))
        source[2, t] = source[2, t] + solid * (wall_maps[kind(t)] * missing)

    for i in range(1, steps_told - 2):
        told(i)

    def tiles_of(ref):
        return [[ref[f, t, PAD:PAD + E] for t in range(TILES)] for f in range(3)]

    def around(ref, tiles, f, t):
        c = tiles[f][t]
        total = ref[f, t, PAD - 1:PAD - 1 + E] + ref[f, t, PAD + 1:PAD + 1 + E]
        total = total + (roll(c, 1) + roll(c, -1))
        total = total + (tiles[f][t - 1] if t > 0 else roll(tiles[f][TILES - 1], WIDE))
        total = total + (tiles[f][t + 1] if t < TILES - 1 else roll(tiles[f][0], -WIDE))
        return c, total

    def fold(x):
        return x[0:8] + x[8:16] + x[16:24] + x[24:32]

    def total_of(x):
        return jnp.sum(jnp.sum(x, axis=0, keepdims=True), axis=1, keepdims=True)

    def square_copy(k, d):
        return pltpu.make_async_remote_copy(
            src_ref=squares.at[k, 0], dst_ref=squares.at[k, d],
            send_sem=sq_send.at[k, d], recv_sem=sq_recv.at[k, d],
            device_id={"group": lax.rem(me_g + d, m)}, device_id_type=MESH)

    def coarse_copy(k, dg, d):
        return pltpu.make_async_remote_copy(
            src_ref=coarse.at[k, 1, me_s], dst_ref=coarse.at[k, 1 - dg, me_s],
            send_sem=c_send.at[k, 1 + dg, d], recv_sem=c_recv.at[k, 1 - dg, me_s],
            device_id={"space": lax.rem(me_s + d, n), "group": jnp.clip(me_g + dg, 0, m - 1)}, device_id_type=MESH)

    def coarse_arrival(k, dg, d):
        who = lax.rem(me_s + d, n)
        return pltpu.make_async_remote_copy(
            src_ref=coarse.at[k, 1 + dg, who], dst_ref=coarse.at[k, 1 + dg, who],
            send_sem=c_send.at[k, 1 + dg, d], recv_sem=c_recv.at[k, 1 + dg, who],
            device_id={"space": lax.rem(me_s + (1 if n > 1 else 0), n)}, device_id_type=MESH)

    def sweep(k, carry):
        square = jnp.zeros((E, 128), F32)
        tiles = tiles_of(state)
        for t in range(TILES):
            rel = label[t]
            pore = rel == 0.0
            active = rel == 1.0
            good = is_valid(rel)
            mine_here = good & own_columns & own_rows[kind(t)]
            conduct = (jnp.where(pore, 1.0, 0.2), jnp.where(pore, 1.0, 0.1),
                       jnp.where(pore, 0.05, jnp.where(active, 0.5, 1.5)))
            rates = jnp.where(pore, 0.0, jnp.where(active, 0.3, 0.02))
            pairs = [around(state, tiles, f, t) for f in range(3)]
            c, e, s = (p[0] for p in pairs)
            eta = s - e - 0.5 * c
            forward = jnp.exp(0.5 * eta)
            backward = jnp.exp(-0.5 * eta)
            current = rates * (forward - backward)
            slope = 0.5 * rates * (forward + backward)
            react = (-0.5 * current, -current, current)
            weight = jnp.where(good, OMEGA, 0.0)
            for f in range(3):
                v, total = pairs[f]
                misfit = 0.5 * v + conduct[f] * (6.0 * v - total) + react[f] - source[f, t]
                square = square + jnp.where(mine_here, misfit * misfit, 0.0)
                dg = 0.5 + 6.0 * conduct[f] + (0.25 * slope if f == 0 else slope)
                w = weight / dg
                if kind(t) != 1:
                    scale[f, t] = w
                upd[0, f, t, PAD:PAD + E] = -w * misfit
                gain[f, t] = w * conduct[f]
                mix[f, t] = w * slope * (0.5 if f == 0 else 1.0)
                diag[f, t] = jnp.where(mine_here, dg * (1.0 / OMEGA), 0.0)
        squares[k, 0] = fold(square)
        for d in range(1, m):
            square_copy(k, d).start()

        @pl.when(k == 0)
        def _():
            for i in range(max(1, steps_told - 2), steps_told - 1):
                told(i)
            for side in range(2):
                arrive(first_messages["source", side])
            for side in range(2):
                for q in range(4):
                    t, first = halo_tile(side, q)
                    here = (lane >= first + DEEP) & (lane < first + DEEP + E)
                    for f in range(3):
                        late = jnp.where(here, roll(y_source[side, f], first + DEEP - 32 * q), 0.0)
                        source[f, t] = source[f, t] + late
                        upd[0, f, t, PAD:PAD + E] = upd[0, f, t, PAD:PAD + E] + scale[f, t] * late

        def terms(u, tiles, t):
            pairs = [around(u, tiles, f, t) for f in range(3)]
            c, e, s = (p[0] for p in pairs)
            half = 0.5 * c
            cross = (s - e, s - half, e + half)
            return [(pairs[f][0], upd[0, f, t, PAD:PAD + E] + gain[f, t] * pairs[f][1] + mix[f, t] * cross[f]) for f in range(3)]

        def smooth_tiles(u, later, which):
            tiles = tiles_of(u)
            for t in which:
                for f, (v, term) in enumerate(terms(u, tiles, t)):
                    later[f, t, PAD:PAD + E] = (1.0 - OMEGA) * v + term

        def smooth(p, carry):
            smooth_tiles(upd.at[jnp.where(p == 0, 0, 1 + lax.rem(p + 1, 2))], upd.at[1 + lax.rem(p, 2)], range(TILES))
            return carry

        lax.fori_loop(0, SMOOTH - 2, smooth, 0)
        u_last = upd.at[1 + (SMOOTH - 3) % 2]
        u = upd.at[1 + (SMOOTH - 2) % 2]
        u_views = [padded(u, f) for f in range(3)]
        sent_rows = range(DEEP - 1, TILES - DEEP + 1)
        smooth_tiles(u_last, u, sent_rows)

        @pl.when(k < NEWTON - 1)
        def _():
            for side in range(2):
                corner_tiles = []
                for f in range(3):
                    tile = None
                    for q in range(4):
                        t, first = spot(E - 4 + q if side == 0 else q)
                        part = roll(u_views[f].read(t), 32 * q - first)
                        tile = part if tile is None else jnp.where(quarter == q, part, tile)
                    corner_tiles.append(tile)
                    t, first = spot(E - 5 if side == 0 else 4)
                    q = (0, 3)[side]
                    deepest = roll(u_views[f].read(t), 32 * q - first)
                    yu_out[side, E * f:E * (f + 1)] = jnp.where(quarter == q, deepest, roll(tile, (32, -32)[side]))
                start(update_messages["y", side])
                for over in range(2):
                    du_out[2 * side + over, 0:E] = corner_pack(corner_tiles, over)
                    start(update_messages["d", 2 * side + over])

        smooth_tiles(u_last, u, [t for t in range(TILES) if t not in sent_rows])
        sums = [jnp.zeros((E, 128), F32) for _ in range(3)]
        tiles = tiles_of(u)
        for t in range(TILES):
            for f, (v, term) in enumerate(terms(u, tiles, t)):
                sums[f] = sums[f] + diag[f, t] * (term - OMEGA * v)
        totals = [total_of(x) for x in sums]
        for d in range(1, m):
            square_copy(k, d).wait_recv()
        part = squares[k, 0]
        for d in range(1, m):
            part = part + squares[k, d]
        packed = jnp.where(lane8 == 127, total_of(part), 0.0)
        for f in range(3):
            packed = jnp.where(lane8 == 3 * me_s + f, totals[f], packed)
        coarse[k, 1, me_s] = packed

        @pl.when(k == 0)
        def _():
            for i in range(max(1, steps_told - 1), steps_told):
                told(i)

        for d in range(1, n):
            coarse_copy(k, 0, d).start()

        def damping_of(group):
            whole = jnp.sum(jnp.where(lane8 == 127, group, 0.0), axis=1, keepdims=True)[0:1]
            cells = 3.0 * n * m * E * E * E
            return 1.0 / (1.0 + jnp.sqrt(whole / cells + 1e-6))

        def group_sum(i):
            acc = coarse[k, i, 0]
            for d in range(1, n):
                acc = acc + coarse[k, i, d]
            return acc

        @pl.when(k < NEWTON - 1)
        def _():
            for dg in (-1, 1):
                @pl.when(there(0, dg))
                def _():
                    for d in range(n):
                        coarse_copy(k, dg, d).start()
            for side in range(2):
                for i, tile in enumerate(z_pack(u_views, side)):
                    zu_out[side, E * i:E * (i + 1)] = tile
                start(update_messages["z", side])
            for side in range(2):
                arrive(update_messages["z", side])
            z_unpack(u_views, lambda side, i: zu_in[side, E * i:E * (i + 1)])
            for c in range(4):
                arrive(update_messages["d", c])
            corner_unpack(u_views, lambda c: du_in[c, 0:E])
            for side in range(2):
                arrive(update_messages["y", side])
            for side in range(2):
                for q in range(4):
                    t, first = (q, 0) if side == 0 else (TILES - 4 + q, 2 * WIDE)
                    here = (lane >= first + DEEP) & (lane < first + DEEP + E)
                    for f in range(3):
                        moved = roll(yu_in[side, E * f:E * (f + 1)], first + DEEP - 32 * q)
                        u[f, t, PAD:PAD + E] = jnp.where(here, moved, u[f, t, PAD:PAD + E])

            for d in range(1, n):
                coarse_arrival(k, 0, d).wait_recv()
            for dg in (-1, 1):
                @pl.when(there(0, dg))
                def _():
                    for d in range(n):
                        coarse_arrival(k, dg, d).wait_recv()
            groups = [group_sum(i) for i in range(3)]
            damping = damping_of(groups[1])
            around_me = [[None] * 3 for _ in range(3)]
            around_me[1][1] = near[...]
            for side in range(2):
                around_me[2 * side][1] = yu_in[side, 3 * E:]
                around_me[1][2 * side] = zu_in[side, 6 * E:]
                for over in range(2):
                    around_me[2 * side][2 * over] = du_in[2 * side + over, E:]
            lifts = [[jnp.sum(around_me[i][j] * groups[j], axis=1, keepdims=True) for j in range(3)] for i in range(3)]
            maps = [[by_region([[x[f:f + 1] for x in row] for row in lifts], i) for i in range(3)] for f in range(3)]
            for t in range(TILES):
                good = is_valid(label[t])
                for f in range(3):
                    value = state[f, t, PAD:PAD + E] + damping * (u[f, t, PAD:PAD + E] + maps[f][kind(t)])
                    state[f, t, PAD:PAD + E] = jnp.where(good, value, 0.0)

        @pl.when(k == NEWTON - 1)
        def _():
            for f in range(3):
                for i in range(RAW):
                    for view, where in ((padded(state, f), out), (u_views[f], last_u)):
                        tile = None
                        for q in range(4):
                            t, first = spot(4 * i + q)
                            part = roll(view.read(t), 32 * q - first)
                            tile = part if tile is None else jnp.where(quarter == q, part, tile)
                        where[f, :, i * 128:(i + 1) * 128] = tile
            for d in range(1, n):
                coarse_arrival(k, 0, d).wait_recv()
            group = group_sum(1)
            damping = damping_of(group)
            lift = mask * jnp.sum(near[...] * group, axis=1, keepdims=True)
            for f in range(3):
                out[f] = out[f] + damping * (last_u[f] + lift[f:f + 1])

        return carry

    lax.fori_loop(0, NEWTON, sweep, 0)

    for spec in list(first_messages.values()) + list(update_messages.values()):
        left(spec)
    for k in range(NEWTON):
        for d in range(1, m):
            square_copy(k, d).wait_send()
        for d in range(1, n):
            coarse_copy(k, 0, d).wait_send()
    for k in range(NEWTON - 1):
        for dg in (-1, 1):
            @pl.when(there(0, dg))
            def _():
                for d in range(n):
                    coarse_copy(k, dg, d).wait_send()


def shards(n, m, initial_state, phases, brick_coords, neighbours, source, coarse_inverse):
    anywhere = pl.BlockSpec(memory_space=pl.ANY)
    vmem = pl.BlockSpec(memory_space=pltpu.VMEM)
    padded = (3, TILES, E + 2 * PAD, 128)
    inner = (3, TILES, E, 128)
    dma = pltpu.SemaphoreType.DMA
    V = pltpu.VMEM
    result = pl.pallas_call(
        functools.partial(kernel, n, m),
        out_shape=V((3, E, E * E), F32),
        in_specs=[anywhere] * 5,
        out_specs=vmem,
        scratch_shapes=[
            pltpu.SMEM((1, 3), jnp.int32),
            V((3, 1, 3 * n), F32),
            V((3, E, E * E), F32),
            V((E, E * E), jnp.int32),
            V((3, E, E * E), F32),
            dma((5,)),
            V(padded, F32),
            V((SMOOTH - 1,) + padded, F32),
            V(inner, F32),
            V(inner, F32),
            V(inner, F32),
            V(inner, F32),
            V(inner, F32),
            V(inner[1:], F32),
            V((3, E, E * E), F32),
            V((8, 128), F32),
            V((2, 3, E, 128), F32), V((2, 3, E, 128), F32),
            V((2, 2 * E, 128), F32), V((2, 2 * E, 128), F32),
            V((4, E, 128), F32), V((4, E, 128), F32),
            V((2, 8 * E, 128), F32), V((2, 8 * E, 128), F32),
            V((2, 6 * E, 128), F32), V((2, 6 * E, 128), F32),
            dma((14,)), dma((14,)),
            V((2, 3 * E + 8, 128), F32), V((2, 3 * E + 8, 128), F32),
            V((4, E + 8, 128), F32), V((4, E + 8, 128), F32),
            V((2, 6 * E + 8, 128), F32), V((2, 6 * E + 8, 128), F32),
            dma((8,)), dma((8,)),
            V((NEWTON, m, 8, 128), F32),
            dma((NEWTON, m)), dma((NEWTON, m)),
            V((NEWTON, 3, n, 8, 128), F32),
            dma((NEWTON, 3, n)), dma((NEWTON, 3, n)),
            pltpu.SemaphoreType.REGULAR((max(1, len(reaches(n))), 2)),
        ],
        compiler_params=pltpu.CompilerParams(
            collective_id=0, has_side_effects=True, vmem_limit_bytes=56 * 1024 * 1024
        ),
    )(brick_coords, jnp.swapaxes(coarse_inverse, 0, 1), initial_state[0], phases[0], source[0])
    return result[None]


def solution(mesh):
    both = ("group", "space")
    return jax.shard_map(
        functools.partial(shards, mesh.shape["space"], mesh.shape["group"]),
        mesh=mesh,
        in_specs=(
            P(both, None, None, None),
            P(both, None, None),
            P(both, None),
            P(both, None),
            P(both, None, None, None),
            P("group", "space", None),
        ),
        out_specs=P(both, None, None, None),
        check_vma=False,
    )
```

```python
import functools

import jax
import jax.numpy as jnp
from jax import lax
from jax.experimental import pallas as pl
from jax.experimental.pallas import tpu as pltpu
from jax.sharding import PartitionSpec as P

NEWTON = 2
SMOOTH = 4
E = 32
RAW = 8
DEEP = 5
WIDE = E + 2 * DEEP
BLOCKS = 3
TILES = WIDE // BLOCKS
PAD = 8
OMEGA = 0.8
FAR = -1000.0
MESH = pl.DeviceIdType.MESH
F32 = jnp.float32


def roll(x, shift):
    shift = shift % 128
    return x if shift == 0 else pltpu.roll(x, shift, 1)


def reaches(n):
    steps, known = [], 1
    while known < n - 1:
        steps.append(known)
        known *= 2
    return steps


def spot(y):
    block, tile = divmod(y + DEEP, TILES)
    return tile, WIDE * block + DEEP


def kernel(
    n, m,
    coords_in, inverse_in, state_hbm, phase_hbm, source_hbm, out,
    coords, inverse, state_in, phase_in, source_in, fetch,
    state, upd, gain, mix, diag, scale, source, label, last_u,
    near, y_state, y_source, y_misc_out, y_misc, d_out, d_in, z_out, z_in, zs_out, zs_in, in_send, in_recv,
    yu_out, yu_in, du_out, du_in, zu_out, zu_in, u_send, u_recv,
    squares, sq_send, sq_recv, coarse, c_send, c_recv, ready,
):
    me_s = lax.axis_index("space")
    me_g = lax.axis_index("group")
    lane = lax.broadcasted_iota(jnp.int32, (E, 128), 1)
    quarter = lane // 32
    block = jnp.where(lane < WIDE, 0, jnp.where(lane < 2 * WIDE, 1, 2))
    column = lane - WIDE * block
    slot = column // DEEP
    own_columns = (column >= DEEP) & (column < DEEP + E)
    low_columns = column < DEEP
    high_columns = (column >= DEEP + E) & (column < WIDE)
    own_rows = (block != 0, block >= 0, block != 2)
    lane8 = lax.broadcasted_iota(jnp.int32, (8, 128), 1)

    def kind(t):
        return 0 if t < DEEP else (1 if t < TILES - DEEP else 2)

    fetches = [
        pltpu.make_async_copy(a, b, fetch.at[i])
        for i, (a, b) in enumerate((
            (coords_in, coords), (state_hbm, state_in), (phase_hbm, phase_in),
            (source_hbm, source_in), (inverse_in, inverse),
        ))
    ]
    for copy in fetches:
        copy.start()

    def there(ds, dg):
        s, g = me_s + ds, me_g + dg
        return (s >= 0) & (s < n) & (g >= 0) & (g < m)

    def at(ds, dg):
        return {"space": jnp.clip(me_s + ds, 0, n - 1), "group": jnp.clip(me_g + dg, 0, m - 1)}

    barrier = pltpu.get_barrier_semaphore()

    def greet(s, g):
        pl.semaphore_signal(barrier, inc=1, device_id={"space": s, "group": g}, device_id_type=MESH)

    for ds in (-1, 0, 1):
        for dg in (-1, 0, 1):
            if ds or dg:
                @pl.when(there(ds, dg))
                def _():
                    greet(jnp.clip(me_s + ds, 0, n - 1), jnp.clip(me_g + dg, 0, m - 1))
    for d in range(1, m):
        other = lax.rem(me_g + d, m)

        @pl.when((other != me_g - 1) & (other != me_g + 1))
        def _():
            greet(me_s, other)
    beside_g = jnp.where(me_g > 0, 1, 0) + jnp.where(me_g < m - 1, 1, 0)
    beside_s = jnp.where(me_s > 0, 1, 0) + jnp.where(me_s < n - 1, 1, 0)
    greeted = beside_s * (1 + beside_g) + m - 1

    def tell(i):
        if i < len(reaches(n)):
            for side, step in enumerate((reaches(n)[i], -reaches(n)[i])):
                @pl.when(there(step, 0))
                def _():
                    pl.semaphore_signal(ready.at[i, side], inc=1, device_id=at(step, 0), device_id_type=MESH)

    def told(i):
        for side, step in enumerate((reaches(n)[i], -reaches(n)[i])):
            @pl.when(there(-step, 0))
            def _():
                pl.semaphore_wait(ready.at[i, side], 1)
        tell(i + 1)

    def message(src, dst, sems, i, ds, dg):
        return pltpu.make_async_remote_copy(
            src_ref=src, dst_ref=dst, send_sem=sems[0].at[i], recv_sem=sems[1].at[i],
            device_id=at(ds, dg), device_id_type=MESH)

    ins = (in_send, in_recv)
    us = (u_send, u_recv)
    steps = (1, -1)
    first_messages, update_messages = {}, {}
    for side in range(2):
        cut = pl.ds(128 * (RAW - 1), 128) if side == 0 else pl.ds(0, 128)
        step = steps[side]
        first_messages["state", side] = (state_hbm.at[:, :, cut], y_state.at[side], ins, side, step, 0)
        first_messages["source", side] = (source_hbm.at[:, :, cut], y_source.at[side], ins, 2 + side, step, 0)
        first_messages["misc", side] = (y_misc_out.at[side], y_misc.at[side], ins, 4 + side, step, 0)
        first_messages["z", side] = (z_out.at[side], z_in.at[side], ins, 6 + side, 0, step)
        first_messages["zs", side] = (zs_out.at[side], zs_in.at[side], ins, 12 + side, 0, step)
        update_messages["y", side] = (yu_out.at[side], yu_in.at[side], us, side, step, 0)
        update_messages["z", side] = (zu_out.at[side], zu_in.at[side], us, 2 + side, 0, step)
        for over in range(2):
            c = 2 * side + over
            first_messages["d", c] = (d_out.at[c], d_in.at[c], ins, 8 + c, step, steps[over])
            update_messages["d", c] = (du_out.at[c], du_in.at[c], us, 4 + c, step, steps[over])

    def start(spec):
        @pl.when(there(spec[4], spec[5]))
        def _():
            message(*spec).start()

    def arrive(spec):
        @pl.when(there(-spec[4], -spec[5]))
        def _():
            message(*spec).wait_recv()

    def left(spec):
        @pl.when(there(spec[4], spec[5]))
        def _():
            message(*spec).wait_send()

    fetches[0].wait()
    occupied = coords[0, 0] >= 0
    mask = jnp.where(occupied, 1.0, 0.0).astype(F32)
    place_x = coords[0, 0].astype(F32)
    offset = 4.0 * place_x
    compare = jnp.where(occupied, offset, 1000.0)

    fetches[4].wait()
    near[...] = jnp.zeros((8, 128), F32)
    for f in range(3):
        near[f:f + 1, 0:3 * n] = inverse[f]
    mine = near[...]

    fetches[1].wait()
    fetches[2].wait()

    def raw_state(f, t):
        return state_in[f, :, t * 128:(t + 1) * 128]

    def raw_source(f, t):
        return source_in[f, :, t * 128:(t + 1) * 128]

    def raw_label(t):
        return phase_in[:, t * 128:(t + 1) * 128].astype(F32) + offset

    for side in range(2):
        edge, inner, q = ((RAW - 1, RAW - 2, 3), (0, 1, 0))[side]
        y_misc_out[side, 0:E] = raw_label(edge)
        fifth = roll(raw_label(inner), 32 * (3 - q))
        for f in range(3):
            fifth = jnp.where(quarter == f, roll(raw_state(f, inner), 32 * (f - q)), fifth)
        y_misc_out[side, E:2 * E] = fifth
        yu_out[side, 3 * E:] = mine

    small = (lane % 32) // 4

    def corner_pack(tiles, over):
        out_tile = None
        for a, tile in enumerate(tiles):
            part = roll(tile, 4 * a - (28 if over == 0 else 0))
            out_tile = part if out_tile is None else jnp.where(small == a, part, out_tile)
        return out_tile

    fetches[3].wait()
    for side in range(2):
        edge = (RAW - 1, 0)[side]
        tiles = [raw_state(f, edge) for f in range(3)] + [raw_label(edge)] + [raw_source(f, edge) for f in range(3)]
        for over in range(2):
            c = 2 * side + over
            d_out[c] = corner_pack(tiles, over)
            du_out[c, E:] = mine

    pl.semaphore_wait(barrier, greeted)
    tell(0)
    for c in range(4):
        start(first_messages["d", c])
    for name in ("misc", "state"):
        for side in range(2):
            start(first_messages[name, side])

    class View:
        def __init__(self, read, write):
            self.read, self.write = read, write

    def padded(ref, f):
        def write(t, v):
            ref[f, t, PAD:PAD + E] = v
        return View(lambda t: ref[f, t, PAD:PAD + E], write)

    def plain(ref, *index):
        def write(t, v):
            ref[(*index, t)] = v
        return View(lambda t: ref[(*index, t)], write)

    views = [padded(state, f) for f in range(3)] + [plain(label)] + [plain(source, f) for f in range(3)]
    raws = [functools.partial(raw_state, f) for f in range(3)] + [raw_label] + [functools.partial(raw_source, f) for f in range(3)]

    zero_rows = jnp.zeros((PAD, 128), F32)
    for t in range(TILES):
        for f in range(3):
            state[f, t, 0:PAD] = zero_rows
            state[f, t, PAD + E:] = zero_rows
            for b in range(SMOOTH - 1):
                upd[b, f, t, 0:PAD] = zero_rows
                upd[b, f, t, PAD + E:] = zero_rows

    half_slots = WIDE // DEEP

    def z_pack(parts, side):
        shift = -(E if side == 0 else DEEP)
        packed = []
        for view in parts:
            for low in (0, half_slots):
                acc = None
                for j in range(min(half_slots, TILES - low)):
                    part = roll(view.read(low + j), DEEP * j + shift)
                    acc = part if acc is None else jnp.where(slot == j, part, acc)
                packed.append(acc)
        return packed

    def z_unpack(parts, got):
        for a, view in enumerate(parts):
            for t in range(TILES):
                half, j = divmod(t, half_slots)
                rows = own_rows[kind(t)]
                tile = jnp.where(low_columns & rows, roll(got(0, 2 * a + half), -DEEP * j), view.read(t))
                view.write(t, jnp.where(high_columns & rows, roll(got(1, 2 * a + half), DEEP + E - DEEP * j), tile))

    def halo_tile(side, q):
        if side == 0:
            return (0 if q < 0 else 1 + q), 0
        return (TILES - 1 if q < 0 else TILES - DEEP + q), 2 * WIDE

    def corner_unpack(parts, got):
        for side in range(2):
            for q in range(4):
                t, first = halo_tile(side, q)
                for a, view in enumerate(parts):
                    tile = view.read(t)
                    for over in range(2):
                        begin = first + (1 if over == 0 else DEEP + E)
                        moved = roll(got(2 * side + over), begin - (32 * q + 4 * a))
                        tile = jnp.where((lane >= begin) & (lane < begin + 4), moved, tile)
                    view.write(t, tile)

    def y_unpack(parts, got, fifth, blocks):
        for side in range(2):
            for q in range(-1, 4):
                t, first = halo_tile(side, q)
                here = (lane >= first + DEEP) & (lane < first + DEEP + E)
                for a, view in enumerate(parts):
                    if q < 0 and blocks[a] is None:
                        continue
                    if q < 0:
                        moved = roll(fifth(side), first + DEEP - 32 * blocks[a])
                    else:
                        moved = roll(got(side, a), first + DEEP - 32 * q)
                    view.write(t, jnp.where(here, moved, view.read(t)))

    def widen(which):
        for t in range(TILES):
            for a in which:
                tile = jnp.full((E, 128), FAR if a == 3 else 0.0, F32)
                for b in range(BLOCKS):
                    y = TILES * b + t - DEEP
                    if 0 <= y < E:
                        moved = roll(raws[a](y // 4), WIDE * b + DEEP - 32 * (y % 4))
                        tile = jnp.where(own_columns & (block == b), moved, tile)
                views[a].write(t, tile)

    widen(range(4))
    for side in range(2):
        for i, tile in enumerate(z_pack(views[:4], side)):
            z_out[side, E * i:E * (i + 1)] = tile
        start(first_messages["z", side])
    widen(range(4, 7))
    for side in range(2):
        for i, tile in enumerate(z_pack(views[4:], side)):
            zs_out[side, E * i:E * (i + 1)] = tile
        start(first_messages["zs", side])
        zu_out[side, 6 * E:] = mine

    far = jnp.full((E, 128), FAR, F32)
    none = jnp.zeros((8, 128), F32)
    blank = jnp.zeros((E, 128), F32)
    for side in range(2):
        @pl.when(jnp.logical_not(there(-steps[side], 0)))
        def _():
            for f in range(3):
                y_state[side, f] = blank
                y_source[side, f] = blank
            for i in range(2):
                y_misc[side, E * i:E * (i + 1)] = far
            yu_in[side, 3 * E:] = none
            for i in range(3):
                yu_in[side, E * i:E * (i + 1)] = blank

        @pl.when(jnp.logical_not(there(0, -steps[side])))
        def _():
            for i in range(8):
                z_in[side, E * i:E * (i + 1)] = far
            zu_in[side, 6 * E:] = none
            for i in range(6):
                zs_in[side, E * i:E * (i + 1)] = blank
                zu_in[side, E * i:E * (i + 1)] = blank
            for k in range(NEWTON):
                for d in range(n):
                    coarse[k, 2 * side, d] = none

        for over in range(2):
            @pl.when(jnp.logical_not(there(-steps[side], -steps[over])))
            def _():
                d_in[2 * side + over] = far
                du_in[2 * side + over, 0:E] = blank
                du_in[2 * side + over, E:] = none


    for side in range(2):
        arrive(first_messages["z", side])
    for side in range(2):
        start(first_messages["source", side])
    z_unpack(views[:4], lambda side, i: z_in[side, E * i:E * (i + 1)])
    for side in range(2):
        arrive(first_messages["zs", side])
    z_unpack(views[4:], lambda side, i: zs_in[side, E * i:E * (i + 1)])
    for c in range(4):
        arrive(first_messages["d", c])
    corner_unpack(views, lambda c: d_in[c])
    for side in range(2):
        for name in ("state", "misc"):
            arrive(first_messages[name, side])

    steps_told = len(reaches(n))
    for i in range(min(1, steps_told)):
        told(i)

    y_unpack(views[:4], lambda side, a: y_state[side, a] if a < 3 else y_misc[side, 0:E], lambda side: y_misc[side, E:2 * E], (0, 1, 2, 3))

    def by_region(values, t_kind):
        def row(i):
            return jnp.where(low_columns, values[i][0], jnp.where(own_columns, values[i][1], values[i][2]))
        middle = row(1)
        if t_kind == 0:
            return jnp.where(block == 0, row(0), middle)
        return jnp.where(block == 2, row(2), middle) if t_kind == 2 else middle

    walls = [[place_x + (me_s + i).astype(F32) / n + (me_g + j).astype(F32) / m - 1.0 for j in (-1, 0, 1)] for i in (-1, 0, 1)]
    wall_maps = [by_region(walls, i) for i in range(3)]
    row_index = lax.broadcasted_iota(jnp.int32, (E, 128), 0)
    x_open = jnp.where((row_index == 0) | (row_index == E - 1), 1.0, 0.0).astype(F32)

    def is_valid(rel):
        return (rel >= 0.0) & (rel <= 2.0)

    bricks = [jnp.where(is_valid(label[t, 0:8] - compare), 1.0, 0.0).astype(F32) for t in range(TILES)]
    for t in range(TILES):
        rel = label[t] - compare
        label[t] = rel
        good = is_valid(rel)
        for f in range(3):
            state[f, t, PAD:PAD + E] = jnp.where(good, state[f, t, PAD:PAD + E], 0.0)
        below = bricks[t - 1] if t > 0 else roll(bricks[TILES - 1], WIDE)
        above = bricks[t + 1] if t < TILES - 1 else roll(bricks[0], -WIDE)
        shut = 4.0 - (below + above + roll(bricks[t], 1) + roll(bricks[t], -1))
        missing = jnp.concatenate([shut] * 4, axis=0) + x_open
        solid = jnp.where(rel == 0.0, 0.05, jnp.where(rel == 1.0, 0.5, 1.5))
        source[2, t] = source[2, t] + solid * (wall_maps[kind(t)] * missing)

    for i in range(1, steps_told - 2):
        told(i)

    def tiles_of(ref):
        return [[ref[f, t, PAD:PAD + E] for t in range(TILES)] for f in range(3)]

    def around(ref, tiles, f, t):
        c = tiles[f][t]
        total = ref[f, t, PAD - 1:PAD - 1 + E] + ref[f, t, PAD + 1:PAD + 1 + E]
        total = total + (roll(c, 1) + roll(c, -1))
        total = total + (tiles[f][t - 1] if t > 0 else roll(tiles[f][TILES - 1], WIDE))
        total = total + (tiles[f][t + 1] if t < TILES - 1 else roll(tiles[f][0], -WIDE))
        return c, total

    def fold(x):
        return x[0:8] + x[8:16] + x[16:24] + x[24:32]

    def total_of(x):
        return jnp.sum(jnp.sum(x, axis=0, keepdims=True), axis=1, keepdims=True)

    def square_copy(k, d):
        return pltpu.make_async_remote_copy(
            src_ref=squares.at[k, 0], dst_ref=squares.at[k, d],
            send_sem=sq_send.at[k, d], recv_sem=sq_recv.at[k, d],
            device_id={"group": lax.rem(me_g + d, m)}, device_id_type=MESH)

    def coarse_copy(k, dg, d):
        return pltpu.make_async_remote_copy(
            src_ref=coarse.at[k, 1, me_s], dst_ref=coarse.at[k, 1 - dg, me_s],
            send_sem=c_send.at[k, 1 + dg, d], recv_sem=c_recv.at[k, 1 - dg, me_s],
            device_id={"space": lax.rem(me_s + d, n), "group": jnp.clip(me_g + dg, 0, m - 1)}, device_id_type=MESH)

    def coarse_arrival(k, dg, d):
        who = lax.rem(me_s + d, n)
        return pltpu.make_async_remote_copy(
            src_ref=coarse.at[k, 1 + dg, who], dst_ref=coarse.at[k, 1 + dg, who],
            send_sem=c_send.at[k, 1 + dg, d], recv_sem=c_recv.at[k, 1 + dg, who],
            device_id={"space": lax.rem(me_s + (1 if n > 1 else 0), n)}, device_id_type=MESH)

    def sweep(k, carry):
        square = jnp.zeros((E, 128), F32)
        tiles = tiles_of(state)
        for t in range(TILES):
            rel = label[t]
            pore = rel == 0.0
            active = rel == 1.0
            good = is_valid(rel)
            mine_here = good & own_columns & own_rows[kind(t)]
            conduct = (jnp.where(pore, 1.0, 0.2), jnp.where(pore, 1.0, 0.1),
                       jnp.where(pore, 0.05, jnp.where(active, 0.5, 1.5)))
            rates = jnp.where(pore, 0.0, jnp.where(active, 0.3, 0.02))
            pairs = [around(state, tiles, f, t) for f in range(3)]
            c, e, s = (p[0] for p in pairs)
            eta = s - e - 0.5 * c
            forward = jnp.exp(0.5 * eta)
            backward = jnp.exp(-0.5 * eta)
            current = rates * (forward - backward)
            slope = 0.5 * rates * (forward + backward)
            react = (-0.5 * current, -current, current)
            weight = jnp.where(good, OMEGA, 0.0)
            for f in range(3):
                v, total = pairs[f]
                misfit = 0.5 * v + conduct[f] * (6.0 * v - total) + react[f] - source[f, t]
                square = square + jnp.where(mine_here, misfit * misfit, 0.0)
                dg = 0.5 + 6.0 * conduct[f] + (0.25 * slope if f == 0 else slope)
                w = weight / dg
                if kind(t) != 1:
                    scale[f, t] = w
                upd[0, f, t, PAD:PAD + E] = -w * misfit
                gain[f, t] = w * conduct[f]
                mix[f, t] = w * slope * (0.5 if f == 0 else 1.0)
                diag[f, t] = jnp.where(mine_here, dg * (1.0 / OMEGA), 0.0)
        squares[k, 0] = fold(square)
        for d in range(1, m):
            square_copy(k, d).start()

        @pl.when(k == 0)
        def _():
            for i in range(max(1, steps_told - 2), steps_told - 1):
                told(i)
            for side in range(2):
                arrive(first_messages["source", side])
            for side in range(2):
                for q in range(4):
                    t, first = halo_tile(side, q)
                    here = (lane >= first + DEEP) & (lane < first + DEEP + E)
                    for f in range(3):
                        late = jnp.where(here, roll(y_source[side, f], first + DEEP - 32 * q), 0.0)
                        source[f, t] = source[f, t] + late
                        upd[0, f, t, PAD:PAD + E] = upd[0, f, t, PAD:PAD + E] + scale[f, t] * late

        def terms(u, tiles, t):
            pairs = [around(u, tiles, f, t) for f in range(3)]
            c, e, s = (p[0] for p in pairs)
            half = 0.5 * c
            cross = (s - e, s - half, e + half)
            return [(pairs[f][0], upd[0, f, t, PAD:PAD + E] + gain[f, t] * pairs[f][1] + mix[f, t] * cross[f]) for f in range(3)]

        def smooth_tiles(u, later, which):
            tiles = tiles_of(u)
            for t in which:
                for f, (v, term) in enumerate(terms(u, tiles, t)):
                    later[f, t, PAD:PAD + E] = (1.0 - OMEGA) * v + term

        def smooth(p, carry):
            smooth_tiles(upd.at[jnp.where(p == 0, 0, 1 + lax.rem(p + 1, 2))], upd.at[1 + lax.rem(p, 2)], range(TILES))
            return carry

        lax.fori_loop(0, SMOOTH - 2, smooth, 0)
        u_last = upd.at[1 + (SMOOTH - 3) % 2]
        u = upd.at[1 + (SMOOTH - 2) % 2]
        u_views = [padded(u, f) for f in range(3)]
        sent_rows = range(DEEP - 1, TILES - DEEP + 1)
        smooth_tiles(u_last, u, sent_rows)

        @pl.when(k < NEWTON - 1)
        def _():
            for side in range(2):
                corner_tiles = []
                for f in range(3):
                    tile = None
                    for q in range(4):
                        t, first = spot(E - 4 + q if side == 0 else q)
                        part = roll(u_views[f].read(t), 32 * q - first)
                        tile = part if tile is None else jnp.where(quarter == q, part, tile)
                    corner_tiles.append(tile)
                    t, first = spot(E - 5 if side == 0 else 4)
                    q = (0, 3)[side]
                    deepest = roll(u_views[f].read(t), 32 * q - first)
                    yu_out[side, E * f:E * (f + 1)] = jnp.where(quarter == q, deepest, roll(tile, (32, -32)[side]))
                start(update_messages["y", side])
                for over in range(2):
                    du_out[2 * side + over, 0:E] = corner_pack(corner_tiles, over)
                    start(update_messages["d", 2 * side + over])

        smooth_tiles(u_last, u, [t for t in range(TILES) if t not in sent_rows])
        sums = [jnp.zeros((E, 128), F32) for _ in range(3)]
        tiles = tiles_of(u)
        for t in range(TILES):
            for f, (v, term) in enumerate(terms(u, tiles, t)):
                sums[f] = sums[f] + diag[f, t] * (term - OMEGA * v)
        totals = [total_of(x) for x in sums]
        for d in range(1, m):
            square_copy(k, d).wait_recv()
        part = squares[k, 0]
        for d in range(1, m):
            part = part + squares[k, d]
        packed = jnp.where(lane8 == 127, total_of(part), 0.0)
        for f in range(3):
            packed = jnp.where(lane8 == 3 * me_s + f, totals[f], packed)
        coarse[k, 1, me_s] = packed

        @pl.when(k == 0)
        def _():
            for i in range(max(1, steps_told - 1), steps_told):
                told(i)

        for d in range(1, n):
            coarse_copy(k, 0, d).start()

        def damping_of(group):
            whole = jnp.sum(jnp.where(lane8 == 127, group, 0.0), axis=1, keepdims=True)[0:1]
            cells = 3.0 * n * m * E * E * E
            return 1.0 / (1.0 + jnp.sqrt(whole / cells + 1e-6))

        def group_sum(i):
            acc = coarse[k, i, 0]
            for d in range(1, n):
                acc = acc + coarse[k, i, d]
            return acc

        @pl.when(k < NEWTON - 1)
        def _():
            for dg in (-1, 1):
                @pl.when(there(0, dg))
                def _():
                    for d in range(n):
                        coarse_copy(k, dg, d).start()
            for side in range(2):
                for i, tile in enumerate(z_pack(u_views, side)):
                    zu_out[side, E * i:E * (i + 1)] = tile
                start(update_messages["z", side])
            for side in range(2):
                arrive(update_messages["z", side])
            z_unpack(u_views, lambda side, i: zu_in[side, E * i:E * (i + 1)])
            for c in range(4):
                arrive(update_messages["d", c])
            corner_unpack(u_views, lambda c: du_in[c, 0:E])
            for side in range(2):
                arrive(update_messages["y", side])
            for side in range(2):
                for q in range(4):
                    t, first = (q, 0) if side == 0 else (TILES - 4 + q, 2 * WIDE)
                    here = (lane >= first + DEEP) & (lane < first + DEEP + E)
                    for f in range(3):
                        moved = roll(yu_in[side, E * f:E * (f + 1)], first + DEEP - 32 * q)
                        u[f, t, PAD:PAD + E] = jnp.where(here, moved, u[f, t, PAD:PAD + E])

            for d in range(1, n):
                coarse_arrival(k, 0, d).wait_recv()
            for dg in (-1, 1):
                @pl.when(there(0, dg))
                def _():
                    for d in range(n):
                        coarse_arrival(k, dg, d).wait_recv()
            groups = [group_sum(i) for i in range(3)]
            damping = damping_of(groups[1])
            around_me = [[None] * 3 for _ in range(3)]
            around_me[1][1] = near[...]
            for side in range(2):
                around_me[2 * side][1] = yu_in[side, 3 * E:]
                around_me[1][2 * side] = zu_in[side, 6 * E:]
                for over in range(2):
                    around_me[2 * side][2 * over] = du_in[2 * side + over, E:]
            lifts = [[jnp.sum(around_me[i][j] * groups[j], axis=1, keepdims=True) for j in range(3)] for i in range(3)]
            maps = [[by_region([[x[f:f + 1] for x in row] for row in lifts], i) for i in range(3)] for f in range(3)]
            for t in range(TILES):
                good = is_valid(label[t])
                for f in range(3):
                    value = state[f, t, PAD:PAD + E] + damping * (u[f, t, PAD:PAD + E] + maps[f][kind(t)])
                    state[f, t, PAD:PAD + E] = jnp.where(good, value, 0.0)

        @pl.when(k == NEWTON - 1)
        def _():
            for f in range(3):
                for i in range(RAW):
                    for view, where in ((padded(state, f), out), (u_views[f], last_u)):
                        tile = None
                        for q in range(4):
                            t, first = spot(4 * i + q)
                            part = roll(view.read(t), 32 * q - first)
                            tile = part if tile is None else jnp.where(quarter == q, part, tile)
                        where[f, :, i * 128:(i + 1) * 128] = tile
            for d in range(1, n):
                coarse_arrival(k, 0, d).wait_recv()
            group = group_sum(1)
            damping = damping_of(group)
            lift = mask * jnp.sum(near[...] * group, axis=1, keepdims=True)
            for f in range(3):
                out[f] = out[f] + damping * (last_u[f] + lift[f:f + 1])

        return carry

    lax.fori_loop(0, NEWTON, sweep, 0)

    for spec in list(first_messages.values()) + list(update_messages.values()):
        left(spec)
    for k in range(NEWTON):
        for d in range(1, m):
            square_copy(k, d).wait_send()
        for d in range(1, n):
            coarse_copy(k, 0, d).wait_send()
    for k in range(NEWTON - 1):
        for dg in (-1, 1):
            @pl.when(there(0, dg))
            def _():
                for d in range(n):
                    coarse_copy(k, dg, d).wait_send()


def shards(n, m, initial_state, phases, brick_coords, neighbours, source, coarse_inverse):
    anywhere = pl.BlockSpec(memory_space=pl.ANY)
    vmem = pl.BlockSpec(memory_space=pltpu.VMEM)
    padded = (3, TILES, E + 2 * PAD, 128)
    inner = (3, TILES, E, 128)
    dma = pltpu.SemaphoreType.DMA
    V = pltpu.VMEM
    result = pl.pallas_call(
        functools.partial(kernel, n, m),
        out_shape=V((3, E, E * E), F32),
        in_specs=[anywhere] * 5,
        out_specs=vmem,
        scratch_shapes=[
            pltpu.SMEM((1, 3), jnp.int32),
            V((3, 1, 3 * n), F32),
            V((3, E, E * E), F32),
            V((E, E * E), jnp.int32),
            V((3, E, E * E), F32),
            dma((5,)),
            V(padded, F32),
            V((SMOOTH - 1,) + padded, F32),
            V(inner, F32),
            V(inner, F32),
            V(inner, F32),
            V(inner, F32),
            V(inner, F32),
            V(inner[1:], F32),
            V((3, E, E * E), F32),
            V((8, 128), F32),
            V((2, 3, E, 128), F32), V((2, 3, E, 128), F32),
            V((2, 2 * E, 128), F32), V((2, 2 * E, 128), F32),
            V((4, E, 128), F32), V((4, E, 128), F32),
            V((2, 8 * E, 128), F32), V((2, 8 * E, 128), F32),
            V((2, 6 * E, 128), F32), V((2, 6 * E, 128), F32),
            dma((14,)), dma((14,)),
            V((2, 3 * E + 8, 128), F32), V((2, 3 * E + 8, 128), F32),
            V((4, E + 8, 128), F32), V((4, E + 8, 128), F32),
            V((2, 6 * E + 8, 128), F32), V((2, 6 * E + 8, 128), F32),
            dma((8,)), dma((8,)),
            V((NEWTON, m, 8, 128), F32),
            dma((NEWTON, m)), dma((NEWTON, m)),
            V((NEWTON, 3, n, 8, 128), F32),
            dma((NEWTON, 3, n)), dma((NEWTON, 3, n)),
            pltpu.SemaphoreType.REGULAR((max(1, len(reaches(n))), 2)),
        ],
        compiler_params=pltpu.CompilerParams(
            collective_id=0, has_side_effects=True, vmem_limit_bytes=56 * 1024 * 1024
        ),
    )(brick_coords, jnp.swapaxes(coarse_inverse, 0, 1), initial_state[0], phases[0], source[0])
    return result[None]


def solution(mesh):
    both = ("group", "space")
    return jax.shard_map(
        functools.partial(shards, mesh.shape["space"], mesh.shape["group"]),
        mesh=mesh,
        in_specs=(
            P(both, None, None, None),
            P(both, None, None),
            P(both, None),
            P(both, None),
            P(both, None, None, None),
            P("group", "space", None),
        ),
        out_specs=P(both, None, None, None),
        check_vma=False,
    )
```

```python
import functools

import jax
import jax.numpy as jnp
from jax import lax
from jax.experimental import pallas as pl
from jax.experimental.pallas import tpu as pltpu
from jax.sharding import PartitionSpec as P

NEWTON = 2
SMOOTH = 4
E = 32
RAW = 8
DEEP = 5
WIDE = E + 2 * DEEP
BLOCKS = 3
TILES = WIDE // BLOCKS
PAD = 8
OMEGA = 0.8
FAR = -1000.0
MESH = pl.DeviceIdType.MESH
F32 = jnp.float32


def roll(x, shift):
    shift = shift % 128
    return x if shift == 0 else pltpu.roll(x, shift, 1)


def reaches(n):
    steps, known = [], 1
    while known < n - 1:
        steps.append(known)
        known *= 2
    return steps


def spot(y):
    block, tile = divmod(y + DEEP, TILES)
    return tile, WIDE * block + DEEP


def kernel(
    n, m,
    coords_in, inverse_in, state_hbm, phase_hbm, source_hbm, out,
    coords, inverse, state_in, phase_in, source_in, fetch,
    state, upd, gain, mix, diag, scale, source, label, last_u,
    near, y_state, y_source, y_misc_out, y_misc, d_out, d_in, z_out, z_in, zs_out, zs_in, in_send, in_recv,
    yu_out, yu_in, du_out, du_in, zu_out, zu_in, u_send, u_recv,
    squares, sq_send, sq_recv, coarse, c_send, c_recv, ready,
):
    me_s = lax.axis_index("space")
    me_g = lax.axis_index("group")
    lane = lax.broadcasted_iota(jnp.int32, (E, 128), 1)
    quarter = lane // 32
    block = jnp.where(lane < WIDE, 0, jnp.where(lane < 2 * WIDE, 1, 2))
    column = lane - WIDE * block
    slot = column // DEEP
    own_columns = (column >= DEEP) & (column < DEEP + E)
    low_columns = column < DEEP
    high_columns = (column >= DEEP + E) & (column < WIDE)
    own_rows = (block != 0, block >= 0, block != 2)
    lane8 = lax.broadcasted_iota(jnp.int32, (8, 128), 1)

    def kind(t):
        return 0 if t < DEEP else (1 if t < TILES - DEEP else 2)

    fetches = [
        pltpu.make_async_copy(a, b, fetch.at[i])
        for i, (a, b) in enumerate((
            (coords_in, coords), (state_hbm, state_in), (phase_hbm, phase_in),
            (source_hbm, source_in), (inverse_in, inverse),
        ))
    ]
    for copy in fetches:
        copy.start()

    def there(ds, dg):
        s, g = me_s + ds, me_g + dg
        return (s >= 0) & (s < n) & (g >= 0) & (g < m)

    def at(ds, dg):
        return {"space": jnp.clip(me_s + ds, 0, n - 1), "group": jnp.clip(me_g + dg, 0, m - 1)}

    barrier = pltpu.get_barrier_semaphore()

    def greet(s, g):
        pl.semaphore_signal(barrier, inc=1, device_id={"space": s, "group": g}, device_id_type=MESH)

    for ds in (-1, 0, 1):
        for dg in (-1, 0, 1):
            if ds or dg:
                @pl.when(there(ds, dg))
                def _():
                    greet(jnp.clip(me_s + ds, 0, n - 1), jnp.clip(me_g + dg, 0, m - 1))
    for d in range(1, m):
        other = lax.rem(me_g + d, m)

        @pl.when((other != me_g - 1) & (other != me_g + 1))
        def _():
            greet(me_s, other)
    beside_g = jnp.where(me_g > 0, 1, 0) + jnp.where(me_g < m - 1, 1, 0)
    beside_s = jnp.where(me_s > 0, 1, 0) + jnp.where(me_s < n - 1, 1, 0)
    greeted = beside_s * (1 + beside_g) + m - 1

    def tell(i):
        if i < len(reaches(n)):
            for side, step in enumerate((reaches(n)[i], -reaches(n)[i])):
                @pl.when(there(step, 0))
                def _():
                    pl.semaphore_signal(ready.at[i, side], inc=1, device_id=at(step, 0), device_id_type=MESH)

    def told(i):
        for side, step in enumerate((reaches(n)[i], -reaches(n)[i])):
            @pl.when(there(-step, 0))
            def _():
                pl.semaphore_wait(ready.at[i, side], 1)
        tell(i + 1)

    def message(src, dst, sems, i, ds, dg):
        return pltpu.make_async_remote_copy(
            src_ref=src, dst_ref=dst, send_sem=sems[0].at[i], recv_sem=sems[1].at[i],
            device_id=at(ds, dg), device_id_type=MESH)

    ins = (in_send, in_recv)
    us = (u_send, u_recv)
    steps = (1, -1)
    first_messages, update_messages = {}, {}
    for side in range(2):
        cut = pl.ds(128 * (RAW - 1), 128) if side == 0 else pl.ds(0, 128)
        step = steps[side]
        first_messages["state", side] = (state_hbm.at[:, :, cut], y_state.at[side], ins, side, step, 0)
        first_messages["source", side] = (source_hbm.at[:, :, cut], y_source.at[side], ins, 2 + side, step, 0)
        first_messages["misc", side] = (y_misc_out.at[side], y_misc.at[side], ins, 4 + side, step, 0)
        first_messages["z", side] = (z_out.at[side], z_in.at[side], ins, 6 + side, 0, step)
        first_messages["zs", side] = (zs_out.at[side], zs_in.at[side], ins, 12 + side, 0, step)
        update_messages["y", side] = (yu_out.at[side], yu_in.at[side], us, side, step, 0)
        update_messages["z", side] = (zu_out.at[side], zu_in.at[side], us, 2 + side, 0, step)
        for over in range(2):
            c = 2 * side + over
            first_messages["d", c] = (d_out.at[c], d_in.at[c], ins, 8 + c, step, steps[over])
            update_messages["d", c] = (du_out.at[c], du_in.at[c], us, 4 + c, step, steps[over])

    def start(spec):
        @pl.when(there(spec[4], spec[5]))
        def _():
            message(*spec).start()

    def arrive(spec):
        @pl.when(there(-spec[4], -spec[5]))
        def _():
            message(*spec).wait_recv()

    def left(spec):
        @pl.when(there(spec[4], spec[5]))
        def _():
            message(*spec).wait_send()

    fetches[0].wait()
    occupied = coords[0, 0] >= 0
    mask = jnp.where(occupied, 1.0, 0.0).astype(F32)
    place_x = coords[0, 0].astype(F32)
    offset = 4.0 * place_x
    compare = jnp.where(occupied, offset, 1000.0)

    fetches[4].wait()
    near[...] = jnp.zeros((8, 128), F32)
    for f in range(3):
        near[f:f + 1, 0:3 * n] = inverse[f]
    mine = near[...]

    fetches[1].wait()
    fetches[2].wait()

    def raw_state(f, t):
        return state_in[f, :, t * 128:(t + 1) * 128]

    def raw_source(f, t):
        return source_in[f, :, t * 128:(t + 1) * 128]

    def raw_label(t):
        return phase_in[:, t * 128:(t + 1) * 128].astype(F32) + offset

    for side in range(2):
        edge, inner, q = ((RAW - 1, RAW - 2, 3), (0, 1, 0))[side]
        y_misc_out[side, 0:E] = raw_label(edge)
        fifth = roll(raw_label(inner), 32 * (3 - q))
        for f in range(3):
            fifth = jnp.where(quarter == f, roll(raw_state(f, inner), 32 * (f - q)), fifth)
        y_misc_out[side, E:2 * E] = fifth
        yu_out[side, 3 * E:] = mine

    small = (lane % 32) // 4

    def corner_pack(tiles, over):
        out_tile = None
        for a, tile in enumerate(tiles):
            part = roll(tile, 4 * a - (28 if over == 0 else 0))
            out_tile = part if out_tile is None else jnp.where(small == a, part, out_tile)
        return out_tile

    fetches[3].wait()
    for side in range(2):
        edge = (RAW - 1, 0)[side]
        tiles = [raw_state(f, edge) for f in range(3)] + [raw_label(edge)] + [raw_source(f, edge) for f in range(3)]
        for over in range(2):
            c = 2 * side + over
            d_out[c] = corner_pack(tiles, over)
            du_out[c, E:] = mine

    pl.semaphore_wait(barrier, greeted)
    tell(0)
    for c in range(4):
        start(first_messages["d", c])
    for name in ("misc", "state"):
        for side in range(2):
            start(first_messages[name, side])

    class View:
        def __init__(self, read, write):
            self.read, self.write = read, write

    def padded(ref, f):
        def write(t, v):
            ref[f, t, PAD:PAD + E] = v
        return View(lambda t: ref[f, t, PAD:PAD + E], write)

    def plain(ref, *index):
        def write(t, v):
            ref[(*index, t)] = v
        return View(lambda t: ref[(*index, t)], write)

    views = [padded(state, f) for f in range(3)] + [plain(label)] + [plain(source, f) for f in range(3)]
    raws = [functools.partial(raw_state, f) for f in range(3)] + [raw_label] + [functools.partial(raw_source, f) for f in range(3)]

    zero_rows = jnp.zeros((PAD, 128), F32)
    for t in range(TILES):
        for f in range(3):
            state[f, t, 0:PAD] = zero_rows
            state[f, t, PAD + E:] = zero_rows
            for b in range(SMOOTH - 1):
                upd[b, f, t, 0:PAD] = zero_rows
                upd[b, f, t, PAD + E:] = zero_rows

    half_slots = WIDE // DEEP

    def z_pack(parts, side):
        shift = -(E if side == 0 else DEEP)
        packed = []
        for view in parts:
            for low in (0, half_slots):
                acc = None
                for j in range(min(half_slots, TILES - low)):
                    part = roll(view.read(low + j), DEEP * j + shift)
                    acc = part if acc is None else jnp.where(slot == j, part, acc)
                packed.append(acc)
        return packed

    def z_unpack(parts, got):
        for a, view in enumerate(parts):
            for t in range(TILES):
                half, j = divmod(t, half_slots)
                rows = own_rows[kind(t)]
                tile = jnp.where(low_columns & rows, roll(got(0, 2 * a + half), -DEEP * j), view.read(t))
                view.write(t, jnp.where(high_columns & rows, roll(got(1, 2 * a + half), DEEP + E - DEEP * j), tile))

    def halo_tile(side, q):
        if side == 0:
            return (0 if q < 0 else 1 + q), 0
        return (TILES - 1 if q < 0 else TILES - DEEP + q), 2 * WIDE

    def corner_unpack(parts, got):
        for side in range(2):
            for q in range(4):
                t, first = halo_tile(side, q)
                for a, view in enumerate(parts):
                    tile = view.read(t)
                    for over in range(2):
                        begin = first + (1 if over == 0 else DEEP + E)
                        moved = roll(got(2 * side + over), begin - (32 * q + 4 * a))
                        tile = jnp.where((lane >= begin) & (lane < begin + 4), moved, tile)
                    view.write(t, tile)

    def y_unpack(parts, got, fifth, blocks):
        for side in range(2):
            for q in range(-1, 4):
                t, first = halo_tile(side, q)
                here = (lane >= first + DEEP) & (lane < first + DEEP + E)
                for a, view in enumerate(parts):
                    if q < 0 and blocks[a] is None:
                        continue
                    if q < 0:
                        moved = roll(fifth(side), first + DEEP - 32 * blocks[a])
                    else:
                        moved = roll(got(side, a), first + DEEP - 32 * q)
                    view.write(t, jnp.where(here, moved, view.read(t)))

    def widen(which):
        for t in range(TILES):
            for a in which:
                tile = jnp.full((E, 128), FAR if a == 3 else 0.0, F32)
                for b in range(BLOCKS):
                    y = TILES * b + t - DEEP
                    if 0 <= y < E:
                        moved = roll(raws[a](y // 4), WIDE * b + DEEP - 32 * (y % 4))
                        tile = jnp.where(own_columns & (block == b), moved, tile)
                views[a].write(t, tile)

    widen(range(4))
    for side in range(2):
        for i, tile in enumerate(z_pack(views[:4], side)):
            z_out[side, E * i:E * (i + 1)] = tile
        start(first_messages["z", side])
    widen(range(4, 7))
    for side in range(2):
        for i, tile in enumerate(z_pack(views[4:], side)):
            zs_out[side, E * i:E * (i + 1)] = tile
        start(first_messages["zs", side])
        zu_out[side, 6 * E:] = mine

    far = jnp.full((E, 128), FAR, F32)
    none = jnp.zeros((8, 128), F32)
    blank = jnp.zeros((E, 128), F32)
    for side in range(2):
        @pl.when(jnp.logical_not(there(-steps[side], 0)))
        def _():
            for f in range(3):
                y_state[side, f] = blank
                y_source[side, f] = blank
            for i in range(2):
                y_misc[side, E * i:E * (i + 1)] = far
            yu_in[side, 3 * E:] = none
            for i in range(3):
                yu_in[side, E * i:E * (i + 1)] = blank

        @pl.when(jnp.logical_not(there(0, -steps[side])))
        def _():
            for i in range(8):
                z_in[side, E * i:E * (i + 1)] = far
            zu_in[side, 6 * E:] = none
            for i in range(6):
                zs_in[side, E * i:E * (i + 1)] = blank
                zu_in[side, E * i:E * (i + 1)] = blank
            for k in range(NEWTON):
                for d in range(n):
                    coarse[k, 2 * side, d] = none

        for over in range(2):
            @pl.when(jnp.logical_not(there(-steps[side], -steps[over])))
            def _():
                d_in[2 * side + over] = far
                du_in[2 * side + over, 0:E] = blank
                du_in[2 * side + over, E:] = none


    for side in range(2):
        arrive(first_messages["z", side])
    for side in range(2):
        start(first_messages["source", side])
    z_unpack(views[:4], lambda side, i: z_in[side, E * i:E * (i + 1)])
    for side in range(2):
        arrive(first_messages["zs", side])
    z_unpack(views[4:], lambda side, i: zs_in[side, E * i:E * (i + 1)])
    for c in range(4):
        arrive(first_messages["d", c])
    corner_unpack(views, lambda c: d_in[c])
    for side in range(2):
        for name in ("state", "misc"):
            arrive(first_messages[name, side])

    steps_told = len(reaches(n))
    for i in range(min(1, steps_told)):
        told(i)

    y_unpack(views[:4], lambda side, a: y_state[side, a] if a < 3 else y_misc[side, 0:E], lambda side: y_misc[side, E:2 * E], (0, 1, 2, 3))

    def by_region(values, t_kind):
        def row(i):
            return jnp.where(low_columns, values[i][0], jnp.where(own_columns, values[i][1], values[i][2]))
        middle = row(1)
        if t_kind == 0:
            return jnp.where(block == 0, row(0), middle)
        return jnp.where(block == 2, row(2), middle) if t_kind == 2 else middle

    walls = [[place_x + (me_s + i).astype(F32) / n + (me_g + j).astype(F32) / m - 1.0 for j in (-1, 0, 1)] for i in (-1, 0, 1)]
    wall_maps = [by_region(walls, i) for i in range(3)]
    row_index = lax.broadcasted_iota(jnp.int32, (E, 128), 0)
    x_open = jnp.where((row_index == 0) | (row_index == E - 1), 1.0, 0.0).astype(F32)

    def is_valid(rel):
        return (rel >= 0.0) & (rel <= 2.0)

    bricks = [jnp.where(is_valid(label[t, 0:8] - compare), 1.0, 0.0).astype(F32) for t in range(TILES)]
    for t in range(TILES):
        rel = label[t] - compare
        label[t] = rel
        good = is_valid(rel)
        for f in range(3):
            state[f, t, PAD:PAD + E] = jnp.where(good, state[f, t, PAD:PAD + E], 0.0)
        below = bricks[t - 1] if t > 0 else roll(bricks[TILES - 1], WIDE)
        above = bricks[t + 1] if t < TILES - 1 else roll(bricks[0], -WIDE)
        shut = 4.0 - (below + above + roll(bricks[t], 1) + roll(bricks[t], -1))
        missing = jnp.concatenate([shut] * 4, axis=0) + x_open
        solid = jnp.where(rel == 0.0, 0.05, jnp.where(rel == 1.0, 0.5, 1.5))
        source[2, t] = source[2, t] + solid * (wall_maps[kind(t)] * missing)

    for i in range(1, steps_told - 2):
        told(i)

    def tiles_of(ref):
        return [[ref[f, t, PAD:PAD + E] for t in range(TILES)] for f in range(3)]

    def around(ref, tiles, f, t):
        c = tiles[f][t]
        total = ref[f, t, PAD - 1:PAD - 1 + E] + ref[f, t, PAD + 1:PAD + 1 + E]
        total = total + (roll(c, 1) + roll(c, -1))
        total = total + (tiles[f][t - 1] if t > 0 else roll(tiles[f][TILES - 1], WIDE))
        total = total + (tiles[f][t + 1] if t < TILES - 1 else roll(tiles[f][0], -WIDE))
        return c, total

    def fold(x):
        return x[0:8] + x[8:16] + x[16:24] + x[24:32]

    def total_of(x):
        return jnp.sum(jnp.sum(x, axis=0, keepdims=True), axis=1, keepdims=True)

    def square_copy(k, d):
        return pltpu.make_async_remote_copy(
            src_ref=squares.at[k, 0], dst_ref=squares.at[k, d],
            send_sem=sq_send.at[k, d], recv_sem=sq_recv.at[k, d],
            device_id={"group": lax.rem(me_g + d, m)}, device_id_type=MESH)

    def coarse_copy(k, dg, d):
        return pltpu.make_async_remote_copy(
            src_ref=coarse.at[k, 1, me_s], dst_ref=coarse.at[k, 1 - dg, me_s],
            send_sem=c_send.at[k, 1 + dg, d], recv_sem=c_recv.at[k, 1 - dg, me_s],
            device_id={"space": lax.rem(me_s + d, n), "group": jnp.clip(me_g + dg, 0, m - 1)}, device_id_type=MESH)

    def coarse_arrival(k, dg, d):
        who = lax.rem(me_s + d, n)
        return pltpu.make_async_remote_copy(
            src_ref=coarse.at[k, 1 + dg, who], dst_ref=coarse.at[k, 1 + dg, who],
            send_sem=c_send.at[k, 1 + dg, d], recv_sem=c_recv.at[k, 1 + dg, who],
            device_id={"space": lax.rem(me_s + (1 if n > 1 else 0), n)}, device_id_type=MESH)

    def sweep(k, carry):
        square = jnp.zeros((E, 128), F32)
        tiles = tiles_of(state)
        for t in range(TILES):
            rel = label[t]
            pore = rel == 0.0
            active = rel == 1.0
            good = is_valid(rel)
            mine_here = good & own_columns & own_rows[kind(t)]
            conduct = (jnp.where(pore, 1.0, 0.2), jnp.where(pore, 1.0, 0.1),
                       jnp.where(pore, 0.05, jnp.where(active, 0.5, 1.5)))
            rates = jnp.where(pore, 0.0, jnp.where(active, 0.3, 0.02))
            pairs = [around(state, tiles, f, t) for f in range(3)]
            c, e, s = (p[0] for p in pairs)
            eta = s - e - 0.5 * c
            forward = jnp.exp(0.5 * eta)
            backward = jnp.exp(-0.5 * eta)
            current = rates * (forward - backward)
            slope = 0.5 * rates * (forward + backward)
            react = (-0.5 * current, -current, current)
            weight = jnp.where(good, OMEGA, 0.0)
            for f in range(3):
                v, total = pairs[f]
                misfit = 0.5 * v + conduct[f] * (6.0 * v - total) + react[f] - source[f, t]
                square = square + jnp.where(mine_here, misfit * misfit, 0.0)
                dg = 0.5 + 6.0 * conduct[f] + (0.25 * slope if f == 0 else slope)
                w = weight / dg
                if kind(t) != 1:
                    scale[f, t] = w
                upd[0, f, t, PAD:PAD + E] = -w * misfit
                gain[f, t] = w * conduct[f]
                mix[f, t] = w * slope * (0.5 if f == 0 else 1.0)
                diag[f, t] = jnp.where(mine_here, dg * (1.0 / OMEGA), 0.0)
        squares[k, 0] = fold(square)
        for d in range(1, m):
            square_copy(k, d).start()

        @pl.when(k == 0)
        def _():
            for i in range(max(1, steps_told - 2), steps_told - 1):
                told(i)
            for side in range(2):
                arrive(first_messages["source", side])
            for side in range(2):
                for q in range(4):
                    t, first = halo_tile(side, q)
                    here = (lane >= first + DEEP) & (lane < first + DEEP + E)
                    for f in range(3):
                        late = jnp.where(here, roll(y_source[side, f], first + DEEP - 32 * q), 0.0)
                        source[f, t] = source[f, t] + late
                        upd[0, f, t, PAD:PAD + E] = upd[0, f, t, PAD:PAD + E] + scale[f, t] * late

        def terms(u, tiles, t):
            pairs = [around(u, tiles, f, t) for f in range(3)]
            c, e, s = (p[0] for p in pairs)
            half = 0.5 * c
            cross = (s - e, s - half, e + half)
            return [(pairs[f][0], upd[0, f, t, PAD:PAD + E] + gain[f, t] * pairs[f][1] + mix[f, t] * cross[f]) for f in range(3)]

        def smooth_tiles(u, later, which):
            tiles = tiles_of(u)
            for t in which:
                for f, (v, term) in enumerate(terms(u, tiles, t)):
                    later[f, t, PAD:PAD + E] = (1.0 - OMEGA) * v + term

        for p in range(SMOOTH - 2):
            smooth_tiles(upd.at[0 if p == 0 else 1 + (p + 1) % 2], upd.at[1 + p % 2], range(TILES))
        u_last = upd.at[1 + (SMOOTH - 3) % 2]
        u = upd.at[1 + (SMOOTH - 2) % 2]
        u_views = [padded(u, f) for f in range(3)]
        sent_rows = range(DEEP - 1, TILES - DEEP + 1)
        smooth_tiles(u_last, u, sent_rows)

        @pl.when(k < NEWTON - 1)
        def _():
            for side in range(2):
                corner_tiles = []
                for f in range(3):
                    tile = None
                    for q in range(4):
                        t, first = spot(E - 4 + q if side == 0 else q)
                        part = roll(u_views[f].read(t), 32 * q - first)
                        tile = part if tile is None else jnp.where(quarter == q, part, tile)
                    corner_tiles.append(tile)
                    t, first = spot(E - 5 if side == 0 else 4)
                    q = (0, 3)[side]
                    deepest = roll(u_views[f].read(t), 32 * q - first)
                    yu_out[side, E * f:E * (f + 1)] = jnp.where(quarter == q, deepest, roll(tile, (32, -32)[side]))
                start(update_messages["y", side])
                for over in range(2):
                    du_out[2 * side + over, 0:E] = corner_pack(corner_tiles, over)
                    start(update_messages["d", 2 * side + over])

        smooth_tiles(u_last, u, [t for t in range(TILES) if t not in sent_rows])
        sums = [jnp.zeros((E, 128), F32) for _ in range(3)]
        tiles = tiles_of(u)
        for t in range(TILES):
            for f, (v, term) in enumerate(terms(u, tiles, t)):
                sums[f] = sums[f] + diag[f, t] * (term - OMEGA * v)
        totals = [total_of(x) for x in sums]
        for d in range(1, m):
            square_copy(k, d).wait_recv()
        part = squares[k, 0]
        for d in range(1, m):
            part = part + squares[k, d]
        packed = jnp.where(lane8 == 127, total_of(part), 0.0)
        for f in range(3):
            packed = jnp.where(lane8 == 3 * me_s + f, totals[f], packed)
        coarse[k, 1, me_s] = packed

        @pl.when(k == 0)
        def _():
            for i in range(max(1, steps_told - 1), steps_told):
                told(i)

        for d in range(1, n):
            coarse_copy(k, 0, d).start()

        def damping_of(group):
            whole = jnp.sum(jnp.where(lane8 == 127, group, 0.0), axis=1, keepdims=True)[0:1]
            cells = 3.0 * n * m * E * E * E
            return 1.0 / (1.0 + jnp.sqrt(whole / cells + 1e-6))

        def group_sum(i):
            acc = coarse[k, i, 0]
            for d in range(1, n):
                acc = acc + coarse[k, i, d]
            return acc

        @pl.when(k < NEWTON - 1)
        def _():
            for dg in (-1, 1):
                @pl.when(there(0, dg))
                def _():
                    for d in range(n):
                        coarse_copy(k, dg, d).start()
            for side in range(2):
                for i, tile in enumerate(z_pack(u_views, side)):
                    zu_out[side, E * i:E * (i + 1)] = tile
                start(update_messages["z", side])
            for side in range(2):
                arrive(update_messages["z", side])
            z_unpack(u_views, lambda side, i: zu_in[side, E * i:E * (i + 1)])
            for c in range(4):
                arrive(update_messages["d", c])
            corner_unpack(u_views, lambda c: du_in[c, 0:E])
            for side in range(2):
                arrive(update_messages["y", side])
            for side in range(2):
                for q in range(4):
                    t, first = (q, 0) if side == 0 else (TILES - 4 + q, 2 * WIDE)
                    here = (lane >= first + DEEP) & (lane < first + DEEP + E)
                    for f in range(3):
                        moved = roll(yu_in[side, E * f:E * (f + 1)], first + DEEP - 32 * q)
                        u[f, t, PAD:PAD + E] = jnp.where(here, moved, u[f, t, PAD:PAD + E])

            for d in range(1, n):
                coarse_arrival(k, 0, d).wait_recv()
            for dg in (-1, 1):
                @pl.when(there(0, dg))
                def _():
                    for d in range(n):
                        coarse_arrival(k, dg, d).wait_recv()
            groups = [group_sum(i) for i in range(3)]
            damping = damping_of(groups[1])
            around_me = [[None] * 3 for _ in range(3)]
            around_me[1][1] = near[...]
            for side in range(2):
                around_me[2 * side][1] = yu_in[side, 3 * E:]
                around_me[1][2 * side] = zu_in[side, 6 * E:]
                for over in range(2):
                    around_me[2 * side][2 * over] = du_in[2 * side + over, E:]
            lifts = [[jnp.sum(around_me[i][j] * groups[j], axis=1, keepdims=True) for j in range(3)] for i in range(3)]
            maps = [[by_region([[x[f:f + 1] for x in row] for row in lifts], i) for i in range(3)] for f in range(3)]
            for t in range(TILES):
                good = is_valid(label[t])
                for f in range(3):
                    value = state[f, t, PAD:PAD + E] + damping * (u[f, t, PAD:PAD + E] + maps[f][kind(t)])
                    state[f, t, PAD:PAD + E] = jnp.where(good, value, 0.0)

        @pl.when(k == NEWTON - 1)
        def _():
            for f in range(3):
                for i in range(RAW):
                    for view, where in ((padded(state, f), out), (u_views[f], last_u)):
                        tile = None
                        for q in range(4):
                            t, first = spot(4 * i + q)
                            part = roll(view.read(t), 32 * q - first)
                            tile = part if tile is None else jnp.where(quarter == q, part, tile)
                        where[f, :, i * 128:(i + 1) * 128] = tile
            for d in range(1, n):
                coarse_arrival(k, 0, d).wait_recv()
            group = group_sum(1)
            damping = damping_of(group)
            lift = mask * jnp.sum(near[...] * group, axis=1, keepdims=True)
            for f in range(3):
                out[f] = out[f] + damping * (last_u[f] + lift[f:f + 1])

        return carry

    lax.fori_loop(0, NEWTON, sweep, 0)

    for spec in list(first_messages.values()) + list(update_messages.values()):
        left(spec)
    for k in range(NEWTON):
        for d in range(1, m):
            square_copy(k, d).wait_send()
        for d in range(1, n):
            coarse_copy(k, 0, d).wait_send()
    for k in range(NEWTON - 1):
        for dg in (-1, 1):
            @pl.when(there(0, dg))
            def _():
                for d in range(n):
                    coarse_copy(k, dg, d).wait_send()


def shards(n, m, initial_state, phases, brick_coords, neighbours, source, coarse_inverse):
    anywhere = pl.BlockSpec(memory_space=pl.ANY)
    vmem = pl.BlockSpec(memory_space=pltpu.VMEM)
    padded = (3, TILES, E + 2 * PAD, 128)
    inner = (3, TILES, E, 128)
    dma = pltpu.SemaphoreType.DMA
    V = pltpu.VMEM
    result = pl.pallas_call(
        functools.partial(kernel, n, m),
        out_shape=V((3, E, E * E), F32),
        in_specs=[anywhere] * 5,
        out_specs=vmem,
        scratch_shapes=[
            pltpu.SMEM((1, 3), jnp.int32),
            V((3, 1, 3 * n), F32),
            V((3, E, E * E), F32),
            V((E, E * E), jnp.int32),
            V((3, E, E * E), F32),
            dma((5,)),
            V(padded, F32),
            V((SMOOTH - 1,) + padded, F32),
            V(inner, F32),
            V(inner, F32),
            V(inner, F32),
            V(inner, F32),
            V(inner, F32),
            V(inner[1:], F32),
            V((3, E, E * E), F32),
            V((8, 128), F32),
            V((2, 3, E, 128), F32), V((2, 3, E, 128), F32),
            V((2, 2 * E, 128), F32), V((2, 2 * E, 128), F32),
            V((4, E, 128), F32), V((4, E, 128), F32),
            V((2, 8 * E, 128), F32), V((2, 8 * E, 128), F32),
            V((2, 6 * E, 128), F32), V((2, 6 * E, 128), F32),
            dma((14,)), dma((14,)),
            V((2, 3 * E + 8, 128), F32), V((2, 3 * E + 8, 128), F32),
            V((4, E + 8, 128), F32), V((4, E + 8, 128), F32),
            V((2, 6 * E + 8, 128), F32), V((2, 6 * E + 8, 128), F32),
            dma((8,)), dma((8,)),
            V((NEWTON, m, 8, 128), F32),
            dma((NEWTON, m)), dma((NEWTON, m)),
            V((NEWTON, 3, n, 8, 128), F32),
            dma((NEWTON, 3, n)), dma((NEWTON, 3, n)),
            pltpu.SemaphoreType.REGULAR((max(1, len(reaches(n))), 2)),
        ],
        compiler_params=pltpu.CompilerParams(
            collective_id=0, has_side_effects=True, vmem_limit_bytes=56 * 1024 * 1024
        ),
    )(brick_coords, jnp.swapaxes(coarse_inverse, 0, 1), initial_state[0], phases[0], source[0])
    return result[None]


def solution(mesh):
    both = ("group", "space")
    return jax.shard_map(
        functools.partial(shards, mesh.shape["space"], mesh.shape["group"]),
        mesh=mesh,
        in_specs=(
            P(both, None, None, None),
            P(both, None, None),
            P(both, None),
            P(both, None),
            P(both, None, None, None),
            P("group", "space", None),
        ),
        out_specs=P(both, None, None, None),
        check_vma=False,
    )
```

```python
import functools

import jax
import jax.numpy as jnp
from jax import lax
from jax.experimental import pallas as pl
from jax.experimental.pallas import tpu as pltpu
from jax.sharding import PartitionSpec as P

NEWTON = 2
SMOOTH = 4
E = 32
RAW = 8
DEEP = 5
WIDE = E + 2 * DEEP
BLOCKS = 3
TILES = WIDE // BLOCKS
PAD = 8
OMEGA = 0.8
FAR = -1000.0
MESH = pl.DeviceIdType.MESH
F32 = jnp.float32


def roll(x, shift):
    shift = shift % 128
    return x if shift == 0 else pltpu.roll(x, shift, 1)


def reaches(n):
    steps, known = [], 1
    while known < n - 1:
        steps.append(known)
        known *= 2
    return steps


def spot(y):
    block, tile = divmod(y + DEEP, TILES)
    return tile, WIDE * block + DEEP


def kernel(
    n, m,
    coords_in, inverse_in, state_hbm, phase_hbm, source_hbm, out,
    coords, inverse, state_in, phase_in, source_in, fetch,
    state, upd, gain, mix, diag, scale, source, label, last_u,
    near, y_state, y_source, y_misc_out, y_misc, d_out, d_in, z_out, z_in, zs_out, zs_in, in_send, in_recv,
    yu_out, yu_in, du_out, du_in, zu_out, zu_in, u_send, u_recv,
    squares, sq_send, sq_recv, coarse, c_send, c_recv, ready,
):
    me_s = lax.axis_index("space")
    me_g = lax.axis_index("group")
    lane = lax.broadcasted_iota(jnp.int32, (E, 128), 1)
    quarter = lane // 32
    block = jnp.where(lane < WIDE, 0, jnp.where(lane < 2 * WIDE, 1, 2))
    column = lane - WIDE * block
    slot = column // DEEP
    own_columns = (column >= DEEP) & (column < DEEP + E)
    low_columns = column < DEEP
    high_columns = (column >= DEEP + E) & (column < WIDE)
    own_rows = (block != 0, block >= 0, block != 2)
    lane8 = lax.broadcasted_iota(jnp.int32, (8, 128), 1)

    def kind(t):
        return 0 if t < DEEP else (1 if t < TILES - DEEP else 2)

    fetches = [
        pltpu.make_async_copy(a, b, fetch.at[i])
        for i, (a, b) in enumerate((
            (coords_in, coords), (state_hbm, state_in), (phase_hbm, phase_in),
            (source_hbm, source_in), (inverse_in, inverse),
        ))
    ]
    for copy in fetches:
        copy.start()

    def there(ds, dg):
        s, g = me_s + ds, me_g + dg
        return (s >= 0) & (s < n) & (g >= 0) & (g < m)

    def at(ds, dg):
        return {"space": jnp.clip(me_s + ds, 0, n - 1), "group": jnp.clip(me_g + dg, 0, m - 1)}

    barrier = pltpu.get_barrier_semaphore()

    def greet(s, g):
        pl.semaphore_signal(barrier, inc=1, device_id={"space": s, "group": g}, device_id_type=MESH)

    for ds in (-1, 0, 1):
        for dg in (-1, 0, 1):
            if ds or dg:
                @pl.when(there(ds, dg))
                def _():
                    greet(jnp.clip(me_s + ds, 0, n - 1), jnp.clip(me_g + dg, 0, m - 1))
    for d in range(1, m):
        other = lax.rem(me_g + d, m)

        @pl.when((other != me_g - 1) & (other != me_g + 1))
        def _():
            greet(me_s, other)
    beside_g = jnp.where(me_g > 0, 1, 0) + jnp.where(me_g < m - 1, 1, 0)
    beside_s = jnp.where(me_s > 0, 1, 0) + jnp.where(me_s < n - 1, 1, 0)
    greeted = beside_s * (1 + beside_g) + m - 1

    def tell(i):
        if i < len(reaches(n)):
            for side, step in enumerate((reaches(n)[i], -reaches(n)[i])):
                @pl.when(there(step, 0))
                def _():
                    pl.semaphore_signal(ready.at[i, side], inc=1, device_id=at(step, 0), device_id_type=MESH)

    def told(i):
        for side, step in enumerate((reaches(n)[i], -reaches(n)[i])):
            @pl.when(there(-step, 0))
            def _():
                pl.semaphore_wait(ready.at[i, side], 1)
        tell(i + 1)

    def message(src, dst, sems, i, ds, dg):
        return pltpu.make_async_remote_copy(
            src_ref=src, dst_ref=dst, send_sem=sems[0].at[i], recv_sem=sems[1].at[i],
            device_id=at(ds, dg), device_id_type=MESH)

    ins = (in_send, in_recv)
    us = (u_send, u_recv)
    steps = (1, -1)
    first_messages, update_messages = {}, {}
    for side in range(2):
        cut = pl.ds(128 * (RAW - 1), 128) if side == 0 else pl.ds(0, 128)
        step = steps[side]
        first_messages["state", side] = (state_hbm.at[:, :, cut], y_state.at[side], ins, side, step, 0)
        first_messages["source", side] = (source_hbm.at[:, :, cut], y_source.at[side], ins, 2 + side, step, 0)
        first_messages["misc", side] = (y_misc_out.at[side], y_misc.at[side], ins, 4 + side, step, 0)
        first_messages["z", side] = (z_out.at[side], z_in.at[side], ins, 6 + side, 0, step)
        first_messages["zs", side] = (zs_out.at[side], zs_in.at[side], ins, 12 + side, 0, step)
        update_messages["y", side] = (yu_out.at[side], yu_in.at[side], us, side, step, 0)
        update_messages["z", side] = (zu_out.at[side], zu_in.at[side], us, 2 + side, 0, step)
        for over in range(2):
            c = 2 * side + over
            first_messages["d", c] = (d_out.at[c], d_in.at[c], ins, 8 + c, step, steps[over])
            update_messages["d", c] = (du_out.at[c], du_in.at[c], us, 4 + c, step, steps[over])

    def start(spec):
        @pl.when(there(spec[4], spec[5]))
        def _():
            message(*spec).start()

    def arrive(spec):
        @pl.when(there(-spec[4], -spec[5]))
        def _():
            message(*spec).wait_recv()

    def left(spec):
        @pl.when(there(spec[4], spec[5]))
        def _():
            message(*spec).wait_send()

    fetches[0].wait()
    occupied = coords[0, 0] >= 0
    mask = jnp.where(occupied, 1.0, 0.0).astype(F32)
    place_x = coords[0, 0].astype(F32)
    offset = 4.0 * place_x
    compare = jnp.where(occupied, offset, 1000.0)

    fetches[4].wait()
    near[...] = jnp.zeros((8, 128), F32)
    for f in range(3):
        near[f:f + 1, 0:3 * n] = inverse[f]
    mine = near[...]

    fetches[1].wait()
    fetches[2].wait()

    def raw_state(f, t):
        return state_in[f, :, t * 128:(t + 1) * 128]

    def raw_source(f, t):
        return source_in[f, :, t * 128:(t + 1) * 128]

    def raw_label(t):
        return phase_in[:, t * 128:(t + 1) * 128].astype(F32) + offset

    for side in range(2):
        edge, inner, q = ((RAW - 1, RAW - 2, 3), (0, 1, 0))[side]
        y_misc_out[side, 0:E] = raw_label(edge)
        fifth = roll(raw_label(inner), 32 * (3 - q))
        for f in range(3):
            fifth = jnp.where(quarter == f, roll(raw_state(f, inner), 32 * (f - q)), fifth)
        y_misc_out[side, E:2 * E] = fifth
        yu_out[side, 3 * E:] = mine

    small = (lane % 32) // 4

    def corner_pack(tiles, over):
        out_tile = None
        for a, tile in enumerate(tiles):
            part = roll(tile, 4 * a - (28 if over == 0 else 0))
            out_tile = part if out_tile is None else jnp.where(small == a, part, out_tile)
        return out_tile

    fetches[3].wait()
    for side in range(2):
        edge = (RAW - 1, 0)[side]
        tiles = [raw_state(f, edge) for f in range(3)] + [raw_label(edge)] + [raw_source(f, edge) for f in range(3)]
        for over in range(2):
            c = 2 * side + over
            d_out[c] = corner_pack(tiles, over)
            du_out[c, E:] = mine

    pl.semaphore_wait(barrier, greeted)
    tell(0)
    for c in range(4):
        start(first_messages["d", c])
    for name in ("misc", "state"):
        for side in range(2):
            start(first_messages[name, side])

    class View:
        def __init__(self, read, write):
            self.read, self.write = read, write

    def padded(ref, f):
        def write(t, v):
            ref[f, t, PAD:PAD + E] = v
        return View(lambda t: ref[f, t, PAD:PAD + E], write)

    def plain(ref, *index):
        def write(t, v):
            ref[(*index, t)] = v
        return View(lambda t: ref[(*index, t)], write)

    views = [padded(state, f) for f in range(3)] + [plain(label)] + [plain(source, f) for f in range(3)]
    raws = [functools.partial(raw_state, f) for f in range(3)] + [raw_label] + [functools.partial(raw_source, f) for f in range(3)]

    zero_rows = jnp.zeros((PAD, 128), F32)
    for t in range(TILES):
        for f in range(3):
            state[f, t, 0:PAD] = zero_rows
            state[f, t, PAD + E:] = zero_rows
            for b in range(SMOOTH - 1):
                upd[b, f, t, 0:PAD] = zero_rows
                upd[b, f, t, PAD + E:] = zero_rows

    half_slots = WIDE // DEEP

    def z_pack(parts, side):
        shift = -(E if side == 0 else DEEP)
        packed = []
        for view in parts:
            for low in (0, half_slots):
                acc = None
                for j in range(min(half_slots, TILES - low)):
                    part = roll(view.read(low + j), DEEP * j + shift)
                    acc = part if acc is None else jnp.where(slot == j, part, acc)
                packed.append(acc)
        return packed

    def z_unpack(parts, got):
        for a, view in enumerate(parts):
            for t in range(TILES):
                half, j = divmod(t, half_slots)
                rows = own_rows[kind(t)]
                tile = jnp.where(low_columns & rows, roll(got(0, 2 * a + half), -DEEP * j), view.read(t))
                view.write(t, jnp.where(high_columns & rows, roll(got(1, 2 * a + half), DEEP + E - DEEP * j), tile))

    def halo_tile(side, q):
        if side == 0:
            return (0 if q < 0 else 1 + q), 0
        return (TILES - 1 if q < 0 else TILES - DEEP + q), 2 * WIDE

    def corner_unpack(parts, got):
        for side in range(2):
            for q in range(4):
                t, first = halo_tile(side, q)
                for a, view in enumerate(parts):
                    tile = view.read(t)
                    for over in range(2):
                        begin = first + (1 if over == 0 else DEEP + E)
                        moved = roll(got(2 * side + over), begin - (32 * q + 4 * a))
                        tile = jnp.where((lane >= begin) & (lane < begin + 4), moved, tile)
                    view.write(t, tile)

    def y_unpack(parts, got, fifth, blocks):
        for side in range(2):
            for q in range(-1, 4):
                t, first = halo_tile(side, q)
                here = (lane >= first + DEEP) & (lane < first + DEEP + E)
                for a, view in enumerate(parts):
                    if q < 0 and blocks[a] is None:
                        continue
                    if q < 0:
                        moved = roll(fifth(side), first + DEEP - 32 * blocks[a])
                    else:
                        moved = roll(got(side, a), first + DEEP - 32 * q)
                    view.write(t, jnp.where(here, moved, view.read(t)))

    def widen(which):
        for t in range(TILES):
            for a in which:
                tile = jnp.full((E, 128), FAR if a == 3 else 0.0, F32)
                for b in range(BLOCKS):
                    y = TILES * b + t - DEEP
                    if 0 <= y < E:
                        moved = roll(raws[a](y // 4), WIDE * b + DEEP - 32 * (y % 4))
                        tile = jnp.where(own_columns & (block == b), moved, tile)
                views[a].write(t, tile)

    widen(range(4))
    for side in range(2):
        for i, tile in enumerate(z_pack(views[:4], side)):
            z_out[side, E * i:E * (i + 1)] = tile
        start(first_messages["z", side])
    widen(range(4, 7))
    for side in range(2):
        for i, tile in enumerate(z_pack(views[4:], side)):
            zs_out[side, E * i:E * (i + 1)] = tile
        start(first_messages["zs", side])
        zu_out[side, 6 * E:] = mine

    far = jnp.full((E, 128), FAR, F32)
    none = jnp.zeros((8, 128), F32)
    blank = jnp.zeros((E, 128), F32)
    for side in range(2):
        @pl.when(jnp.logical_not(there(-steps[side], 0)))
        def _():
            for f in range(3):
                y_state[side, f] = blank
                y_source[side, f] = blank
            for i in range(2):
                y_misc[side, E * i:E * (i + 1)] = far
            yu_in[side, 3 * E:] = none
            for i in range(3):
                yu_in[side, E * i:E * (i + 1)] = blank

        @pl.when(jnp.logical_not(there(0, -steps[side])))
        def _():
            for i in range(8):
                z_in[side, E * i:E * (i + 1)] = far
            zu_in[side, 6 * E:] = none
            for i in range(6):
                zs_in[side, E * i:E * (i + 1)] = blank
                zu_in[side, E * i:E * (i + 1)] = blank
            for k in range(NEWTON):
                for d in range(n):
                    coarse[k, 2 * side, d] = none

        for over in range(2):
            @pl.when(jnp.logical_not(there(-steps[side], -steps[over])))
            def _():
                d_in[2 * side + over] = far
                du_in[2 * side + over, 0:E] = blank
                du_in[2 * side + over, E:] = none


    for side in range(2):
        arrive(first_messages["z", side])
    for side in range(2):
        start(first_messages["source", side])
    z_unpack(views[:4], lambda side, i: z_in[side, E * i:E * (i + 1)])
    for side in range(2):
        arrive(first_messages["zs", side])
    z_unpack(views[4:], lambda side, i: zs_in[side, E * i:E * (i + 1)])
    for c in range(4):
        arrive(first_messages["d", c])
    corner_unpack(views, lambda c: d_in[c])
    for side in range(2):
        for name in ("state", "misc"):
            arrive(first_messages[name, side])

    steps_told = len(reaches(n))
    for i in range(min(1, steps_told)):
        told(i)

    y_unpack(views[:4], lambda side, a: y_state[side, a] if a < 3 else y_misc[side, 0:E], lambda side: y_misc[side, E:2 * E], (0, 1, 2, 3))

    def by_region(values, t_kind):
        def row(i):
            return jnp.where(low_columns, values[i][0], jnp.where(own_columns, values[i][1], values[i][2]))
        middle = row(1)
        if t_kind == 0:
            return jnp.where(block == 0, row(0), middle)
        return jnp.where(block == 2, row(2), middle) if t_kind == 2 else middle

    walls = [[place_x + (me_s + i).astype(F32) / n + (me_g + j).astype(F32) / m - 1.0 for j in (-1, 0, 1)] for i in (-1, 0, 1)]
    wall_maps = [by_region(walls, i) for i in range(3)]
    row_index = lax.broadcasted_iota(jnp.int32, (E, 128), 0)
    x_open = jnp.where((row_index == 0) | (row_index == E - 1), 1.0, 0.0).astype(F32)

    def is_valid(rel):
        return (rel >= 0.0) & (rel <= 2.0)

    bricks = [jnp.where(is_valid(label[t, 0:8] - compare), 1.0, 0.0).astype(F32) for t in range(TILES)]
    for t in range(TILES):
        rel = label[t] - compare
        label[t] = rel
        good = is_valid(rel)
        for f in range(3):
            state[f, t, PAD:PAD + E] = jnp.where(good, state[f, t, PAD:PAD + E], 0.0)
        below = bricks[t - 1] if t > 0 else roll(bricks[TILES - 1], WIDE)
        above = bricks[t + 1] if t < TILES - 1 else roll(bricks[0], -WIDE)
        shut = 4.0 - (below + above + roll(bricks[t], 1) + roll(bricks[t], -1))
        missing = jnp.concatenate([shut] * 4, axis=0) + x_open
        solid = jnp.where(rel == 0.0, 0.05, jnp.where(rel == 1.0, 0.5, 1.5))
        source[2, t] = source[2, t] + solid * (wall_maps[kind(t)] * missing)

    for i in range(1, steps_told - 2):
        told(i)

    def tiles_of(ref):
        return [[ref[f, t, PAD:PAD + E] for t in range(TILES)] for f in range(3)]

    def around(ref, tiles, f, t):
        c = tiles[f][t]
        total = ref[f, t, PAD - 1:PAD - 1 + E] + ref[f, t, PAD + 1:PAD + 1 + E]
        total = total + (roll(c, 1) + roll(c, -1))
        total = total + (tiles[f][t - 1] if t > 0 else roll(tiles[f][TILES - 1], WIDE))
        total = total + (tiles[f][t + 1] if t < TILES - 1 else roll(tiles[f][0], -WIDE))
        return c, total

    def fold(x):
        return x[0:8] + x[8:16] + x[16:24] + x[24:32]

    def total_of(x):
        return jnp.sum(jnp.sum(x, axis=0, keepdims=True), axis=1, keepdims=True)

    def square_copy(k, d):
        return pltpu.make_async_remote_copy(
            src_ref=squares.at[k, 0], dst_ref=squares.at[k, d],
            send_sem=sq_send.at[k, d], recv_sem=sq_recv.at[k, d],
            device_id={"group": lax.rem(me_g + d, m)}, device_id_type=MESH)

    def coarse_copy(k, dg, d):
        return pltpu.make_async_remote_copy(
            src_ref=coarse.at[k, 1, me_s], dst_ref=coarse.at[k, 1 - dg, me_s],
            send_sem=c_send.at[k, 1 + dg, d], recv_sem=c_recv.at[k, 1 - dg, me_s],
            device_id={"space": lax.rem(me_s + d, n), "group": jnp.clip(me_g + dg, 0, m - 1)}, device_id_type=MESH)

    def coarse_arrival(k, dg, d):
        who = lax.rem(me_s + d, n)
        return pltpu.make_async_remote_copy(
            src_ref=coarse.at[k, 1 + dg, who], dst_ref=coarse.at[k, 1 + dg, who],
            send_sem=c_send.at[k, 1 + dg, d], recv_sem=c_recv.at[k, 1 + dg, who],
            device_id={"space": lax.rem(me_s + (1 if n > 1 else 0), n)}, device_id_type=MESH)

    def sweep(k, carry):
        square = jnp.zeros((E, 128), F32)
        tiles = tiles_of(state)
        for t in range(TILES):
            rel = label[t]
            pore = rel == 0.0
            active = rel == 1.0
            good = is_valid(rel)
            mine_here = good & own_columns & own_rows[kind(t)]
            conduct = (jnp.where(pore, 1.0, 0.2), jnp.where(pore, 1.0, 0.1),
                       jnp.where(pore, 0.05, jnp.where(active, 0.5, 1.5)))
            rates = jnp.where(pore, 0.0, jnp.where(active, 0.3, 0.02))
            pairs = [around(state, tiles, f, t) for f in range(3)]
            c, e, s = (p[0] for p in pairs)
            eta = s - e - 0.5 * c
            forward = jnp.exp(0.5 * eta)
            backward = jnp.exp(-0.5 * eta)
            current = rates * (forward - backward)
            slope = 0.5 * rates * (forward + backward)
            react = (-0.5 * current, -current, current)
            weight = jnp.where(good, OMEGA, 0.0)
            for f in range(3):
                v, total = pairs[f]
                misfit = 0.5 * v + conduct[f] * (6.0 * v - total) + react[f] - source[f, t]
                square = square + jnp.where(mine_here, misfit * misfit, 0.0)
                dg = 0.5 + 6.0 * conduct[f] + (0.25 * slope if f == 0 else slope)
                w = weight / dg
                if k == 0 and kind(t) != 1:
                    scale[f, t] = w
                upd[0, f, t, PAD:PAD + E] = -w * misfit
                gain[f, t] = w * conduct[f]
                mix[f, t] = w * slope * (0.5 if f == 0 else 1.0)
                diag[f, t] = jnp.where(mine_here, dg * (1.0 / OMEGA), 0.0)
        squares[k, 0] = fold(square)
        for d in range(1, m):
            square_copy(k, d).start()

        @pl.when(k == 0)
        def _():
            for i in range(max(1, steps_told - 2), steps_told - 1):
                told(i)
            for side in range(2):
                arrive(first_messages["source", side])
            for side in range(2):
                for q in range(4):
                    t, first = halo_tile(side, q)
                    here = (lane >= first + DEEP) & (lane < first + DEEP + E)
                    for f in range(3):
                        late = jnp.where(here, roll(y_source[side, f], first + DEEP - 32 * q), 0.0)
                        source[f, t] = source[f, t] + late
                        upd[0, f, t, PAD:PAD + E] = upd[0, f, t, PAD:PAD + E] + scale[f, t] * late

        def terms(u, tiles, t):
            pairs = [around(u, tiles, f, t) for f in range(3)]
            c, e, s = (p[0] for p in pairs)
            half = 0.5 * c
            cross = (s - e, s - half, e + half)
            return [(pairs[f][0], upd[0, f, t, PAD:PAD + E] + gain[f, t] * pairs[f][1] + mix[f, t] * cross[f]) for f in range(3)]

        def smooth_tiles(u, later, which):
            tiles = tiles_of(u)
            for t in which:
                for f, (v, term) in enumerate(terms(u, tiles, t)):
                    later[f, t, PAD:PAD + E] = (1.0 - OMEGA) * v + term

        for p in range(SMOOTH - 2):
            smooth_tiles(upd.at[0 if p == 0 else 1 + (p + 1) % 2], upd.at[1 + p % 2], range(TILES))
        u_last = upd.at[1 + (SMOOTH - 3) % 2]
        u = upd.at[1 + (SMOOTH - 2) % 2]
        u_views = [padded(u, f) for f in range(3)]
        sent_rows = range(DEEP - 1, TILES - DEEP + 1)
        smooth_tiles(u_last, u, sent_rows)

        @pl.when(k < NEWTON - 1)
        def _():
            for side in range(2):
                corner_tiles = []
                for f in range(3):
                    tile = None
                    for q in range(4):
                        t, first = spot(E - 4 + q if side == 0 else q)
                        part = roll(u_views[f].read(t), 32 * q - first)
                        tile = part if tile is None else jnp.where(quarter == q, part, tile)
                    corner_tiles.append(tile)
                    t, first = spot(E - 5 if side == 0 else 4)
                    q = (0, 3)[side]
                    deepest = roll(u_views[f].read(t), 32 * q - first)
                    yu_out[side, E * f:E * (f + 1)] = jnp.where(quarter == q, deepest, roll(tile, (32, -32)[side]))
                start(update_messages["y", side])
                for over in range(2):
                    du_out[2 * side + over, 0:E] = corner_pack(corner_tiles, over)
                    start(update_messages["d", 2 * side + over])

        smooth_tiles(u_last, u, [t for t in range(TILES) if t not in sent_rows])
        sums = [jnp.zeros((E, 128), F32) for _ in range(3)]
        tiles = tiles_of(u)
        for t in range(TILES):
            for f, (v, term) in enumerate(terms(u, tiles, t)):
                sums[f] = sums[f] + diag[f, t] * (term - OMEGA * v)
        totals = [total_of(x) for x in sums]
        for d in range(1, m):
            square_copy(k, d).wait_recv()
        part = squares[k, 0]
        for d in range(1, m):
            part = part + squares[k, d]
        packed = jnp.where(lane8 == 127, total_of(part), 0.0)
        for f in range(3):
            packed = jnp.where(lane8 == 3 * me_s + f, totals[f], packed)
        coarse[k, 1, me_s] = packed

        @pl.when(k == 0)
        def _():
            for i in range(max(1, steps_told - 1), steps_told):
                told(i)

        for d in range(1, n):
            coarse_copy(k, 0, d).start()

        def damping_of(group):
            whole = jnp.sum(jnp.where(lane8 == 127, group, 0.0), axis=1, keepdims=True)[0:1]
            cells = 3.0 * n * m * E * E * E
            return 1.0 / (1.0 + jnp.sqrt(whole / cells + 1e-6))

        def group_sum(i):
            acc = coarse[k, i, 0]
            for d in range(1, n):
                acc = acc + coarse[k, i, d]
            return acc

        @pl.when(k < NEWTON - 1)
        def _():
            for dg in (-1, 1):
                @pl.when(there(0, dg))
                def _():
                    for d in range(n):
                        coarse_copy(k, dg, d).start()
            for side in range(2):
                for i, tile in enumerate(z_pack(u_views, side)):
                    zu_out[side, E * i:E * (i + 1)] = tile
                start(update_messages["z", side])
            for side in range(2):
                arrive(update_messages["z", side])
            z_unpack(u_views, lambda side, i: zu_in[side, E * i:E * (i + 1)])
            for c in range(4):
                arrive(update_messages["d", c])
            corner_unpack(u_views, lambda c: du_in[c, 0:E])
            for side in range(2):
                arrive(update_messages["y", side])
            for side in range(2):
                for q in range(4):
                    t, first = (q, 0) if side == 0 else (TILES - 4 + q, 2 * WIDE)
                    here = (lane >= first + DEEP) & (lane < first + DEEP + E)
                    for f in range(3):
                        moved = roll(yu_in[side, E * f:E * (f + 1)], first + DEEP - 32 * q)
                        u[f, t, PAD:PAD + E] = jnp.where(here, moved, u[f, t, PAD:PAD + E])

            for d in range(1, n):
                coarse_arrival(k, 0, d).wait_recv()
            for dg in (-1, 1):
                @pl.when(there(0, dg))
                def _():
                    for d in range(n):
                        coarse_arrival(k, dg, d).wait_recv()
            groups = [group_sum(i) for i in range(3)]
            damping = damping_of(groups[1])
            around_me = [[None] * 3 for _ in range(3)]
            around_me[1][1] = near[...]
            for side in range(2):
                around_me[2 * side][1] = yu_in[side, 3 * E:]
                around_me[1][2 * side] = zu_in[side, 6 * E:]
                for over in range(2):
                    around_me[2 * side][2 * over] = du_in[2 * side + over, E:]
            lifts = [[jnp.sum(around_me[i][j] * groups[j], axis=1, keepdims=True) for j in range(3)] for i in range(3)]
            maps = [[by_region([[x[f:f + 1] for x in row] for row in lifts], i) for i in range(3)] for f in range(3)]
            for t in range(TILES):
                good = is_valid(label[t])
                for f in range(3):
                    value = state[f, t, PAD:PAD + E] + damping * (u[f, t, PAD:PAD + E] + maps[f][kind(t)])
                    state[f, t, PAD:PAD + E] = jnp.where(good, value, 0.0)

        @pl.when(k == NEWTON - 1)
        def _():
            for f in range(3):
                for i in range(RAW):
                    for view, where in ((padded(state, f), out), (u_views[f], last_u)):
                        tile = None
                        for q in range(4):
                            t, first = spot(4 * i + q)
                            part = roll(view.read(t), 32 * q - first)
                            tile = part if tile is None else jnp.where(quarter == q, part, tile)
                        where[f, :, i * 128:(i + 1) * 128] = tile
            for d in range(1, n):
                coarse_arrival(k, 0, d).wait_recv()
            group = group_sum(1)
            damping = damping_of(group)
            lift = mask * jnp.sum(near[...] * group, axis=1, keepdims=True)
            for f in range(3):
                out[f] = out[f] + damping * (last_u[f] + lift[f:f + 1])

        return carry

    for k in range(NEWTON):
        sweep(k, 0)

    for spec in list(first_messages.values()) + list(update_messages.values()):
        left(spec)
    for k in range(NEWTON):
        for d in range(1, m):
            square_copy(k, d).wait_send()
        for d in range(1, n):
            coarse_copy(k, 0, d).wait_send()
    for k in range(NEWTON - 1):
        for dg in (-1, 1):
            @pl.when(there(0, dg))
            def _():
                for d in range(n):
                    coarse_copy(k, dg, d).wait_send()


def shards(n, m, initial_state, phases, brick_coords, neighbours, source, coarse_inverse):
    anywhere = pl.BlockSpec(memory_space=pl.ANY)
    vmem = pl.BlockSpec(memory_space=pltpu.VMEM)
    padded = (3, TILES, E + 2 * PAD, 128)
    inner = (3, TILES, E, 128)
    dma = pltpu.SemaphoreType.DMA
    V = pltpu.VMEM
    result = pl.pallas_call(
        functools.partial(kernel, n, m),
        out_shape=V((3, E, E * E), F32),
        in_specs=[anywhere] * 5,
        out_specs=vmem,
        scratch_shapes=[
            pltpu.SMEM((1, 3), jnp.int32),
            V((3, 1, 3 * n), F32),
            V((3, E, E * E), F32),
            V((E, E * E), jnp.int32),
            V((3, E, E * E), F32),
            dma((5,)),
            V(padded, F32),
            V((SMOOTH - 1,) + padded, F32),
            V(inner, F32),
            V(inner, F32),
            V(inner, F32),
            V(inner, F32),
            V(inner, F32),
            V(inner[1:], F32),
            V((3, E, E * E), F32),
            V((8, 128), F32),
            V((2, 3, E, 128), F32), V((2, 3, E, 128), F32),
            V((2, 2 * E, 128), F32), V((2, 2 * E, 128), F32),
            V((4, E, 128), F32), V((4, E, 128), F32),
            V((2, 8 * E, 128), F32), V((2, 8 * E, 128), F32),
            V((2, 6 * E, 128), F32), V((2, 6 * E, 128), F32),
            dma((14,)), dma((14,)),
            V((2, 3 * E + 8, 128), F32), V((2, 3 * E + 8, 128), F32),
            V((4, E + 8, 128), F32), V((4, E + 8, 128), F32),
            V((2, 6 * E + 8, 128), F32), V((2, 6 * E + 8, 128), F32),
            dma((8,)), dma((8,)),
            V((NEWTON, m, 8, 128), F32),
            dma((NEWTON, m)), dma((NEWTON, m)),
            V((NEWTON, 3, n, 8, 128), F32),
            dma((NEWTON, 3, n)), dma((NEWTON, 3, n)),
            pltpu.SemaphoreType.REGULAR((max(1, len(reaches(n))), 2)),
        ],
        compiler_params=pltpu.CompilerParams(
            collective_id=0, has_side_effects=True, vmem_limit_bytes=56 * 1024 * 1024
        ),
    )(brick_coords, jnp.swapaxes(coarse_inverse, 0, 1), initial_state[0], phases[0], source[0])
    return result[None]


def solution(mesh):
    both = ("group", "space")
    return jax.shard_map(
        functools.partial(shards, mesh.shape["space"], mesh.shape["group"]),
        mesh=mesh,
        in_specs=(
            P(both, None, None, None),
            P(both, None, None),
            P(both, None),
            P(both, None),
            P(both, None, None, None),
            P("group", "space", None),
        ),
        out_specs=P(both, None, None, None),
        check_vma=False,
    )
```
